32 devices in a mesh: section: 2 (over x), seq: 4 (over y, core), dp: 4 (over z).
Axes of the slice: x: 2, y: 2, z: 4, core: 2. Of those that a mesh axis runs over, the one named last changes fastest.
Arguments:
- frozen_queries: bfloat16 [2, 4, 512, 4096], P('section', 'dp', 'seq'), may hold values from -128 to 128
- key_value_pairs: bfloat16 [2, 4, 512, 1024], P('section', 'dp', 'seq'), may hold values from -8 to 8
- adapter_input: bfloat16 [2, 4, 512, 64], P('section', 'dp', 'seq'), may hold values from -6 to 6
- adapter_up_matrix: bfloat16 [2, 64, 4096], P('section', None, 'seq'), may hold values from -0.75 to 0.75
- upstream: bfloat16 [2, 4, 512, 4096], P('section', 'dp', 'seq'), may hold values from -6 to 6
- document_index: int32 [2, 4, 512], P('section', 'dp'), may hold values from 0 to 15, as said below
Outputs:
- query_gradient: bfloat16 [2, 4, 512, 4096], P('section', 'dp', 'seq')
- key_value_gradient: bfloat16 [2, 4, 512, 1024], P('section', 'dp', 'seq')
- adapter_input_gradient: bfloat16 [2, 4, 512, 64], P('section', 'dp', 'seq')
- adapter_up_gradient: float32 [2, 64, 4096], P('section', 'dp', 'seq')
The draws below stay inside these ranges and needn't reach their ends.
Inputs may be any that keep to these rules, and one draw needn't show every extreme that they name: `document_index`: along each pack the numbers never fall; every number appears; every document spans at most 64 positions, and one document of each pack spans exactly that many.
All inputs are finite; a program needn't handle non-finite values.
Results may differ from the reference program's by a relative error of at most 0.014.
Values may be sent and summed in bfloat16 or wider, within the bound.
No kernel may reach another device: no remote copies, remote signals or barrier semaphores. Data moves between devices by JAX's collectives and lax.ppermute only.
A program may use at most 64 MiB of HBM per device.

```python
import math
import jax
import jax.numpy as jnp
from jax import lax

QUERY_HEADS = 32
HK = 4
HEAD_SIZE = 128
ADAPTER_RANK = 64
DOCS = 16
RELAY_SECTIONS = 2
ROLLOUT_PACKS = 4
PACK_LENGTH = 512
GROUP = 8
QH = 8


def aligned_keys(key, tie):
    first, second, third = jax.random.split(key, 3)
    shape = (RELAY_SECTIONS, ROLLOUT_PACKS, PACK_LENGTH, HK, 2, HEAD_SIZE)
    raw_values = jax.random.normal(first, shape, jnp.float32)
    spread = jnp.exp(jax.random.uniform(second, (RELAY_SECTIONS, ROLLOUT_PACKS, PACK_LENGTH, HK, 2, 1), jnp.float32, math.log(0.5), math.log(2.0)))
    chosen = jax.random.randint(third, (RELAY_SECTIONS, ROLLOUT_PACKS, PACK_LENGTH, 1, 1, 1), 0, 48) == 0
    spread = jnp.where(chosen, 1.0, spread)
    key_value_list = raw_values * spread
    positions = jnp.arange(PACK_LENGTH).reshape(1, 1, PACK_LENGTH, 1, 1, 1)
    following = jnp.roll(key_value_list, -1, axis=2)
    following_chosen = jnp.roll(chosen, -1, axis=2) & (positions < PACK_LENGTH - 1) & (tie > 0.5)
    key_half = jnp.where(following_chosen, 0.99 * following[..., 0:1, :], key_value_list[..., 0:1, :])
    key_value_list = jnp.clip(jnp.concatenate([key_half, key_value_list[..., 1:2, :]], axis=4), -8.0, 8.0)
    return key_value_list


def draw_key_value_pairs(key, part):
    key_value_list = aligned_keys(key, 0.0)
    return key_value_list.reshape(RELAY_SECTIONS, ROLLOUT_PACKS, PACK_LENGTH, HK * 2 * HEAD_SIZE).astype(jnp.bfloat16)


def draw_frozen_queries(key, part):
    key = jax.random.fold_in(key, 11)
    first, second = jax.random.split(key, 2)
    shape = (RELAY_SECTIONS, ROLLOUT_PACKS, PACK_LENGTH, QUERY_HEADS, HEAD_SIZE)
    spread = jnp.exp(jax.random.uniform(second, (RELAY_SECTIONS, ROLLOUT_PACKS, PACK_LENGTH, QUERY_HEADS, 1), jnp.float32, math.log(0.3), math.log(3.0)))
    raw_values = jax.random.normal(first, shape, jnp.float32)
    query_values = raw_values * spread
    query_values = jnp.clip(query_values, -128.0, 128.0)
    return query_values.reshape(RELAY_SECTIONS, ROLLOUT_PACKS, PACK_LENGTH, QUERY_HEADS * HEAD_SIZE).astype(jnp.bfloat16)


def pack_documents(key):
    first, second = jax.random.split(key, 2)
    most = PACK_LENGTH // 8
    others = DOCS - 1
    extra = PACK_LENGTH - most - others
    longest = jax.random.randint(first, (), 0, DOCS).astype(jnp.int32)
    order = jax.random.permutation(second, extra + others - 1).astype(jnp.int32)
    cuts = jnp.sort(order[:others - 1])
    edges = jnp.concatenate([jnp.full((1,), -1, jnp.int32), cuts, jnp.full((1,), extra + others - 1, jnp.int32)])
    extras = (edges[1:] - edges[:-1] - 1).astype(jnp.int32)

    def settle(step, current):
        over = jnp.maximum(current - (most - 1), 0).astype(jnp.int32)
        return (current - over + jnp.roll(over, 1)).astype(jnp.int32)
    extras = lax.fori_loop(0, 4 * others, settle, extras)
    short_lengths = (extras + 1).astype(jnp.int32)
    index_list = jnp.arange(DOCS, dtype=jnp.int32)
    before = short_lengths[jnp.clip(index_list, 0, DOCS - 2)]
    after = short_lengths[jnp.clip(index_list - 1, 0, DOCS - 2)]
    lengths = jnp.where(index_list < longest, before, jnp.where(index_list == longest, most, after)).astype(jnp.int32)
    bounds = jnp.cumsum(lengths)[:-1]
    positions = jnp.arange(PACK_LENGTH, dtype=jnp.int32)
    return jnp.sum((positions[:, None] >= bounds[None, :]).astype(jnp.int32), axis=1).astype(jnp.int32)


def draw_document_index(key, part):
    key = jax.random.fold_in(key, 29)
    keys = jax.random.split(key, RELAY_SECTIONS * ROLLOUT_PACKS)
    numbers = jax.vmap(pack_documents)(keys)
    return numbers.reshape(RELAY_SECTIONS, ROLLOUT_PACKS, PACK_LENGTH).astype(jnp.int32)


def levels(key, shape, cuts, least, high):
    loudness = 1.0
    for axis_at, shards_of in cuts:
        draws = jax.random.uniform(jax.random.fold_in(jax.random.fold_in(key, 6), axis_at), (shards_of,), jnp.float32, least / len(cuts), high / len(cuts))
        loudness = loudness * jnp.repeat(jnp.exp(draws), shape[axis_at] // shards_of).reshape((-1,) + (1,) * (len(shape) - 1 - axis_at))
    return loudness


def normal_values(own_key, shape, deviation, reach, shards=(), kind=jnp.bfloat16):
    array = jax.random.normal(own_key, shape, jnp.float32) * deviation
    if len(shards) > 0:
        array = levels(own_key, shape, shards, -0.22, 0.18) * array
    return jnp.clip(array, min=-reach, max=reach).astype(kind)


def setup_inputs(seed: int = 0) -> dict:
    seeds = jax.random.split(jax.random.key(seed), 7)
    return {
        "frozen_queries": draw_frozen_queries(jax.random.fold_in(seeds[6], 71), 0),
        "key_value_pairs": draw_key_value_pairs(jax.random.fold_in(seeds[6], 71), 0),
        "adapter_input": normal_values(seeds[2], (RELAY_SECTIONS, ROLLOUT_PACKS, PACK_LENGTH, ADAPTER_RANK), 1.0, 6.0, ((0, 2), (1, 4), (2, 4))),
        "adapter_up_matrix": normal_values(seeds[3], (RELAY_SECTIONS, ADAPTER_RANK, QUERY_HEADS * HEAD_SIZE), ADAPTER_RANK ** -0.5, 0.75, ((0, 2), (2, 4))),
        "upstream": normal_values(seeds[4], (RELAY_SECTIONS, ROLLOUT_PACKS, PACK_LENGTH, QUERY_HEADS * HEAD_SIZE), 1.0, 6.0, ((0, 2), (1, 4), (2, 4))),
        "document_index": draw_document_index(jax.random.fold_in(seeds[6], 71), 0),
    }


def head_grads(query_rows, key_rows, value_rows, cotangent_rows, visible):
    scale_factor = 1.0 / math.sqrt(HEAD_SIZE)
    scores = jnp.dot(query_rows, key_rows.T, preferred_element_type=jnp.float32) * scale_factor
    scores = jnp.where(visible, scores, -jnp.inf)
    shifted = jnp.exp(scores - lax.optimization_barrier(jnp.max(scores, axis=1, keepdims=True)))
    probs = shifted / lax.optimization_barrier(jnp.sum(shifted, axis=1, keepdims=True))
    probs_low = probs.astype(jnp.bfloat16)
    dprobs = jnp.dot(cotangent_rows, value_rows.T, preferred_element_type=jnp.float32)
    deltas = lax.optimization_barrier(jnp.sum(probs * dprobs, axis=1, keepdims=True))
    dscores = (probs * (dprobs - deltas)).astype(jnp.bfloat16)
    grad_query = (jnp.dot(dscores, key_rows, preferred_element_type=jnp.float32) * scale_factor).astype(jnp.bfloat16)
    grad_key = jnp.dot(dscores.T, query_rows, preferred_element_type=jnp.float32) * scale_factor
    grad_value = jnp.dot(probs_low.T, cotangent_rows, preferred_element_type=jnp.float32)
    return (grad_query, grad_key, grad_value)

def one_sequence(item_list):
    base_query_rows, key_value_rows, adapter_input_rows, cotangent_rows, document_numbers, adapter_weight = item_list
    length = base_query_rows.shape[0]
    query_values = (base_query_rows.astype(jnp.float32) + jnp.dot(adapter_input_rows, adapter_weight, preferred_element_type=jnp.float32)).astype(jnp.bfloat16)
    positions = jnp.arange(length, dtype=jnp.int32)
    visible = (document_numbers[:, None] == document_numbers[None, :]) & (positions[:, None] >= positions[None, :])
    query_heads = query_values.reshape(length, HK, GROUP, HEAD_SIZE).transpose(1, 2, 0, 3)
    cot_heads = cotangent_rows.reshape(length, HK, GROUP, HEAD_SIZE).transpose(1, 2, 0, 3)
    pair_heads = key_value_rows.reshape(length, HK, 2, HEAD_SIZE).transpose(1, 2, 0, 3)

    def per_pair(pair_items):
        group_queries, group_pairs, group_cots = pair_items

        def per_head(head_items):
            return head_grads(head_items[0], group_pairs[0], group_pairs[1], head_items[1], visible)
        query_gradient_part, grad_k, grad_v = lax.map(per_head, (group_queries, group_cots))
        partial_sums = jnp.stack([grad_k, grad_v], axis=1).reshape(GROUP // QH, QH, 2, length, HEAD_SIZE)
        partial_sums = lax.optimization_barrier(jnp.sum(partial_sums, axis=1)).astype(jnp.bfloat16)
        partial_sums = lax.optimization_barrier(partial_sums)
        return (query_gradient_part, lax.optimization_barrier(jnp.sum(partial_sums.astype(jnp.float32), axis=0)).astype(jnp.bfloat16))
    query_gradient_part, pair_gradient_list = lax.map(per_pair, (query_heads, pair_heads, cot_heads))
    query_gradient_rows = query_gradient_part.transpose(2, 0, 1, 3).reshape(length, QUERY_HEADS * HEAD_SIZE)
    pair_gradient_rows = pair_gradient_list.transpose(2, 0, 1, 3).reshape(length, HK * 2 * HEAD_SIZE)
    adapter_input_grad_rows = jnp.dot(query_gradient_rows, adapter_weight.T, preferred_element_type=jnp.float32).astype(jnp.bfloat16)
    weight_gradient = jnp.dot(adapter_input_rows.T, query_gradient_rows, preferred_element_type=jnp.float32)
    return (query_gradient_rows, pair_gradient_rows, adapter_input_grad_rows, weight_gradient)

def reference(frozen_queries, key_value_pairs, adapter_input, adapter_up_matrix, upstream, document_index):
    incoming_value = jnp.roll(upstream, -1, axis=0)

    def single_section(section_entries):
        base_query_part, key_value_list, adapter_input_rows, cotangent_list, document_numbers, weight_matrix = section_entries

        def pack_result(pack_items):
            return one_sequence(pack_items + (weight_matrix,))
        query_gradient_part, pair_gradient_list, gradient_row_list, weight_gradient = lax.map(pack_result, (base_query_part, key_value_list, adapter_input_rows, cotangent_list, document_numbers))
        return (query_gradient_part, pair_gradient_list, gradient_row_list, lax.optimization_barrier(jnp.sum(weight_gradient, axis=0)))
    query_gradient, key_value_gradient, adapter_input_gradient, adapter_up_gradient = lax.map(single_section, (frozen_queries, key_value_pairs, adapter_input, incoming_value, document_index, adapter_up_matrix))
    return (query_gradient, key_value_gradient, adapter_input_gradient, adapter_up_gradient)
```

```python
import functools
import math

import jax
import jax.numpy as jnp
from jax import lax
from jax.experimental import pallas as pl
from jax.experimental.pallas import tpu as pltpu
from jax.sharding import PartitionSpec as P

QUERY_HEADS = 32
HK = 4
HEAD_SIZE = 128
SCALE = 1.0 / math.sqrt(HEAD_SIZE)
SPAN_PARTS = 8


def passed_along(value, axis, steps):
    count = lax.axis_size(axis)
    pairs = [(source, (source + steps) % count) for source in range(count)]
    return lax.ppermute(value, axis, pairs)


def dot(left, right, left_dim, right_dim):
    return lax.dot_general(
        left, right, (((left_dim,), (right_dim,)), ((), ())), preferred_element_type=jnp.float32
    )


def chunk_kernel(first, last, received, picks, fq, at, up, cot, halo, own, bias, *rest):
    rest = list(rest)
    if not first:
        rest = rest[3:]
        input_sum = rest.pop(0)
    terms = [rest.pop(0) for _ in range(received)]
    dq_out, halo_out, own_out, input_out, weight_out = rest
    heads = fq.shape[1] // HEAD_SIZE
    halo_rows = halo.shape[0]
    keys = jnp.concatenate([halo[:, :HEAD_SIZE], own[:, :HEAD_SIZE]], axis=0)
    values = jnp.concatenate([halo[:, HEAD_SIZE:], own[:, HEAD_SIZE:]], axis=0)
    adapter = at[...]
    matrix = up[...]
    hidden = bias[...]
    queries = (fq[...].astype(jnp.float32) + dot(adapter, matrix, 0, 0)).astype(jnp.bfloat16)
    key_total = jnp.zeros((keys.shape[0], HEAD_SIZE), jnp.float32)
    value_total = key_total
    grads = []
    for head in range(heads):
        columns = slice(head * HEAD_SIZE, (head + 1) * HEAD_SIZE)
        query = queries[:, columns]
        cotangent = cot[:, columns]
        scores = dot(keys, query, 1, 1) * SCALE + hidden
        shifted = jnp.exp(scores - jnp.max(scores, axis=0, keepdims=True))
        probs = shifted * (1.0 / jnp.sum(shifted, axis=0, keepdims=True))
        dprobs = dot(values, cotangent, 1, 1)
        deltas = jnp.sum(probs * dprobs, axis=0, keepdims=True)
        dscores = (probs * (dprobs - deltas)).astype(jnp.bfloat16)
        grads.append((dot(dscores, keys, 0, 0) * SCALE).astype(jnp.bfloat16))
        key_total += dot(dscores, query, 1, 0)
        value_total += dot(probs.astype(jnp.bfloat16), cotangent, 1, 0)
    grad = jnp.concatenate(grads, axis=1)
    dq_out[...] = grad
    pair = jnp.concatenate([key_total * SCALE, value_total], axis=1)
    halo_out[...] = pair[:halo_rows].astype(halo_out.dtype)
    own_out[...] = pair[halo_rows:]
    input_term = dot(matrix, grad, 1, 1)
    if not first:
        input_term += input_sum[...]
    input_out[...] = input_term.astype(input_out.dtype)
    weight_term = dot(adapter, grad, 1, 0)
    for term in terms:
        weight_term += term[...].astype(jnp.float32)
    weight_out[...] = weight_term.astype(jnp.bfloat16)


def chunk_step(step, chunks, picks, fq, at, up, cot, halo, own, bias, carried, terms):
    rows, columns = fq.shape
    width = columns // chunks
    rank = at.shape[0]
    halo_rows = halo.shape[0]
    pair = 2 * HEAD_SIZE
    first, last = step == 0, step == chunks - 1
    halo_type = jnp.bfloat16 if chunks == HK else jnp.float32

    def whole(array):
        return pl.BlockSpec(array.shape, lambda i, picks: (0, 0))

    def chunk_of(height, across):
        return pl.BlockSpec((height, across), lambda i, picks: (0, picks[2 * step]))

    def head_of(height):
        return pl.BlockSpec((height, pair), lambda i, picks: (0, picks[2 * step + 1]))

    operands = [fq, at, up, cot, halo, own, bias]
    in_specs = [
        chunk_of(rows, width),
        whole(at),
        whole(up),
        whole(cot),
        head_of(halo_rows),
        head_of(rows),
        whole(bias),
    ]
    aliases = {}
    if not first:
        for place, array in enumerate(carried[:3]):
            aliases[1 + len(operands)] = place
            operands.append(array)
            in_specs.append(pl.BlockSpec(memory_space=pl.ANY))
        operands.append(carried[3])
        in_specs.append(whole(carried[3]))
    for term in terms:
        operands.append(term)
        in_specs.append(whole(term))
    out_shape = [
        jax.ShapeDtypeStruct((rows, columns), jnp.bfloat16),
        jax.ShapeDtypeStruct((halo_rows, chunks * pair), halo_type),
        jax.ShapeDtypeStruct((rows, chunks * pair), jnp.float32),
        jax.ShapeDtypeStruct((rank, rows), jnp.bfloat16 if last else jnp.float32),
        jax.ShapeDtypeStruct((rank, width), jnp.bfloat16),
    ]
    out_specs = [
        chunk_of(rows, width),
        chunk_of(halo_rows, pair),
        chunk_of(rows, pair),
        pl.BlockSpec((rank, rows), lambda i, picks: (0, 0)),
        pl.BlockSpec((rank, width), lambda i, picks: (0, 0)),
    ]
    heads = width // HEAD_SIZE
    return pl.pallas_call(
        functools.partial(chunk_kernel, first, last, len(terms)),
        grid_spec=pltpu.PrefetchScalarGridSpec(
            num_scalar_prefetch=1, grid=(1,), in_specs=in_specs, out_specs=out_specs
        ),
        out_shape=out_shape,
        input_output_aliases=aliases,
        compiler_params=pltpu.CompilerParams(vmem_limit_bytes=32 * 1024 * 1024),
        cost_estimate=pl.CostEstimate(
            flops=heads * 10 * rows * (rows + halo_rows) * HEAD_SIZE,
            bytes_accessed=8 * rows * width,
            transcendentals=heads * rows * (rows + halo_rows),
        ),
        name="chunk_step",
    )(picks, *operands)


def per_device(
    frozen_queries, key_value_pairs, adapter_input, adapter_up_matrix, upstream, document_index
):
    chunks = lax.axis_size("seq")
    place = lax.axis_index("seq")
    rows = frozen_queries.shape[2]
    length = document_index.shape[2]
    span = length // SPAN_PARTS
    width = QUERY_HEADS * HEAD_SIZE // chunks
    pair = 2 * HEAD_SIZE
    per_head = chunks // HK

    order = (place + 1 + jnp.arange(chunks, dtype=jnp.int32)) % chunks
    picks = jnp.stack([order, order // per_head], axis=1).reshape(2 * chunks)

    pieces = []
    left = span
    while left > 0:
        pieces.append((len(pieces) + 1, min(rows, left)))
        left -= rows

    own = key_value_pairs[0, 0]
    cots = []
    for step in range(chunks):
        part = lax.dynamic_slice_in_dim(upstream[0, 0], picks[2 * step] * width, width, 1)
        cots.append(passed_along(part, "section", -1))
        if step == 0:
            halo_parts = [
                passed_along(own[rows - count :], "seq", distance) for distance, count in pieces
            ]
            halo = jnp.concatenate(halo_parts[::-1], axis=0)
    own_matrix = adapter_up_matrix[0]
    matrices = [passed_along(own_matrix, "seq", -(step + 1)) for step in range(chunks - 1)]
    matrices.append(own_matrix)

    numbers = jnp.concatenate([jnp.full((span,), -1, jnp.int32), document_index[0, 0]])
    numbers = lax.dynamic_slice_in_dim(numbers, place * rows, span + rows, 0)
    reach = jnp.arange(span + rows, dtype=jnp.int32)[:, None] <= (
        jnp.arange(rows, dtype=jnp.int32)[None, :] + span
    )
    bias = jnp.where((numbers[:, None] == numbers[None, span:]) & reach, 0.0, -jnp.inf)
    bias = bias.astype(jnp.float32)

    adapter = adapter_input[0, 0].T
    carried, terms = None, []
    for step in range(chunks):
        *carried, term = chunk_step(
            step,
            chunks,
            picks,
            frozen_queries[0, 0],
            adapter,
            matrices[step],
            cots[step],
            halo,
            own,
            bias,
            carried,
            terms if step == chunks - 1 else [],
        )
        if step < chunks - 1:
            terms.append(passed_along(term, "seq", step + 1))
    query_gradient, halo_grads, own_grads, input_grad = carried

    packs = lax.axis_size("dp")
    slots = term.reshape(packs, term.shape[0] // packs, width)
    slots = lax.all_to_all(slots, "dp", split_axis=0, concat_axis=0)
    weight_share = jnp.sum(slots.astype(jnp.float32), axis=0)[None]

    if per_head > 1:
        halo_grads = jnp.sum(halo_grads.reshape(span, HK, per_head, pair), axis=2)
        halo_grads = halo_grads.astype(jnp.bfloat16).reshape(span, HK * pair)
        own_grads = jnp.sum(own_grads.reshape(rows, HK, per_head, pair), axis=2)
        own_grads = own_grads.reshape(rows, HK * pair)
    stop = span
    for distance, count in pieces:
        back = passed_along(halo_grads[stop - count : stop], "seq", -distance)
        stop -= count
        own_grads = own_grads.at[rows - count :].add(back.astype(jnp.float32))
    pair_grads = own_grads.astype(jnp.bfloat16)

    return (
        query_gradient[None, None],
        pair_grads[None, None],
        input_grad.T[None, None],
        weight_share,
    )


def solution(mesh):
    placed = (
        P("section", "dp", "seq", None),
        P("section", "dp", "seq", None),
        P("section", "dp", "seq", None),
        P("section", None, "seq"),
        P("section", "dp", "seq", None),
        P("section", "dp", None),
    )
    return jax.shard_map(
        per_device,
        mesh=mesh,
        in_specs=placed,
        out_specs=(
            P("section", "dp", "seq", None),
            P("section", "dp", "seq", None),
            P("section", "dp", "seq", None),
            P("section", "dp", "seq"),
        ),
        check_vma=False,
    )
```

```python
import functools
import math
from types import SimpleNamespace

import jax
import jax.numpy as jnp
from jax import lax
from jax.experimental import pallas as pl
from jax.experimental.pallas import tpu as pltpu
from jax.sharding import PartitionSpec as P

QUERY_HEADS = 32
HK = 4
HEAD_SIZE = 128
PAIR = 2 * HEAD_SIZE
SCALE = 1.0 / math.sqrt(HEAD_SIZE)
SPAN_PARTS = 8

WHOLE, FRONT, BACK, FINISH = range(4)
PHASE_NAMES = ("whole", "front", "back", "finish")
IN = "_in"
DQ = "dq_out"
DQ_IN = DQ + IN
SHARES = ["share" + str(index) for index in range(64)]
PENDING = ["pending" + str(index) for index in range(2)]
TERMS = ["term_in" + str(index) for index in range(64)]

VMEM = pl.BlockSpec(memory_space=pltpu.VMEM)
HBM = pl.BlockSpec(memory_space=pltpu.HBM)
LIMIT = 16 * 1024 * 1024
BLOCKS = 2


def passed_along(value, axis, steps):
    count = lax.axis_size(axis)
    pairs = [(source, (source + steps) % count) for source in range(count)]
    return lax.ppermute(value, axis, pairs)


def partner(place, away, count):
    if count & (count - 1) == 0:
        return place ^ away
    return (place + away) % count


def dot(left, right, left_dim, right_dim):
    return lax.dot_general(
        left, right, (((left_dim,), (right_dim,)), ((), ())), preferred_element_type=jnp.float32
    )


def chunk_at(step, chunks):
    return lax.rem(lax.axis_index("seq") + (2 * chunks - 1 - step), chunks)


def split_kernel(steps, chunks, bundled, upstream, own, matrix, *rest):
    rest = list(rest)
    sems = rest.pop()
    if steps[0] > 0:
        rest.pop(0)
    rows = upstream.shape[0]
    width = upstream.shape[1] // chunks
    copies = []

    def send(source, target):
        copies.append(pltpu.make_async_copy(source, target, sems.at[len(copies)]))
        copies[-1].start()

    for step in steps:
        start = pl.multiple_of(chunk_at(step, chunks) * width, HEAD_SIZE)
        columns = pl.ds(start, width)
        if step < chunks - 1:
            send(upstream.at[:, columns], rest.pop(0))
        else:
            send(upstream.at[pl.ds(0, rows // BLOCKS), columns], rest.pop(0))
            send(upstream.at[pl.ds(rows // BLOCKS, rows // BLOCKS), columns], rest.pop(0))
    if steps[0] > 0:
        send(matrix, rest.pop(0))
    if bundled > 0:
        bundle = rest.pop(0)
        send(own.at[pl.ds(rows - bundled, bundled)], bundle.at[pl.ds(0, bundled)])
        send(matrix, bundle.at[pl.ds(bundled, matrix.shape[0])])
    for copy in copies:
        copy.wait()


def split_columns(steps, chunks, bundled, upstream, own, matrix, after):
    rows, columns = upstream.shape
    shapes = []
    for step in steps:
        if step < chunks - 1:
            shapes.append(jax.ShapeDtypeStruct((rows, columns // chunks), upstream.dtype))
        else:
            half = jax.ShapeDtypeStruct((rows // BLOCKS, columns // chunks), upstream.dtype)
            shapes += [half] * BLOCKS
    if steps[0] > 0:
        shapes.append(jax.ShapeDtypeStruct(matrix.shape, matrix.dtype))
    if bundled > 0:
        shapes.append(jax.ShapeDtypeStruct((bundled + matrix.shape[0], own.shape[1]), own.dtype))
    operands = [
        pltpu.with_memory_space_constraint(array, pltpu.HBM) for array in (upstream, own, matrix)
    ] + after
    return list(
        pl.pallas_call(
            functools.partial(split_kernel, steps, chunks, bundled),
            in_specs=[HBM] * 3 + [VMEM] * len(after),
            out_specs=[VMEM] * len(shapes),
            out_shape=shapes,
            scratch_shapes=[pltpu.SemaphoreType.DMA((len(shapes) + 1,))],
            compiler_params=pltpu.CompilerParams(vmem_limit_bytes=LIMIT),
            cost_estimate=pl.CostEstimate(
                flops=0, bytes_accessed=4 * rows * columns, transcendentals=0
            ),
            name="split_columns",
        )(*operands)
    )


def stacked(array, rows):
    heads = array.shape[1] // HEAD_SIZE
    parts = [array[rows, head * HEAD_SIZE : (head + 1) * HEAD_SIZE] for head in range(heads)]
    return jnp.concatenate(parts, axis=0)


def softmax_block(query_stack, key_window, hidden):
    copies = query_stack.shape[0] // hidden.shape[1]
    scores = dot(key_window, query_stack, 1, 1) * SCALE
    scores += jnp.concatenate([hidden] * copies, axis=1)
    shifted = jnp.exp(scores - jnp.max(scores, axis=0, keepdims=True))
    return shifted * (1.0 / jnp.sum(shifted, axis=0, keepdims=True))


def block_grads(probs, key_window, value_window, cot_stack):
    dprobs = dot(value_window, cot_stack, 1, 1)
    deltas = jnp.sum(probs * dprobs, axis=0, keepdims=True)
    dscores = (probs * (dprobs - deltas)).astype(jnp.bfloat16)
    return dscores, (dot(dscores, key_window, 0, 0) * SCALE).astype(jnp.bfloat16)


def pair_terms(index, block, total, dscores, probs, query_stack, cot_stack):
    key_term = dot(dscores, query_stack, 1, 0) * SCALE
    value_term = dot(probs.astype(jnp.bfloat16), cot_stack, 1, 0)
    term = jnp.concatenate([key_term, value_term], axis=1)
    start = index * block
    rest = total - term.shape[0] - start
    if start > 0:
        term = jnp.concatenate([jnp.zeros((start, PAIR), jnp.float32), term], axis=0)
    if rest > 0:
        term = jnp.concatenate([term, jnp.zeros((rest, PAIR), jnp.float32)], axis=0)
    return term


def padded(grad, index, block):
    blank = jnp.zeros((block, grad.shape[1]), grad.dtype)
    return jnp.concatenate([grad if place == index else blank for place in range(BLOCKS)], axis=0)


def chunk_kernel(step, phase, chunks, up_row, pending, names, *refs):
    refs = SimpleNamespace(**dict(zip(names, refs)))
    first = step == 0
    fq, at, up, cot = refs.fq, refs.at, refs.up, refs.cot
    halo, own, bias = refs.halo, refs.own, refs.bias
    rows = fq.shape[0]
    block = rows // BLOCKS
    rank = at.shape[0]
    window = bias.shape[0] // BLOCKS
    span = window - block
    width = fq.shape[1] // chunks
    heads = width // HEAD_SIZE

    def columns_of(at_step):
        return pl.ds(pl.multiple_of(chunk_at(at_step, chunks) * width, HEAD_SIZE), width)

    copies = []
    for index, (at_step, start, count) in enumerate(pending):
        target = refs.dq_out.at[pl.ds(start, count), columns_of(at_step)]
        copies.append(pltpu.make_async_copy(getattr(refs, PENDING[index]), target, refs.sems.at[index]))
        copies[-1].start()

    chunk = chunk_at(step, chunks)
    place = lax.div(chunk, chunks // HK) if chunks > HK else chunk
    key_columns = pl.ds(pl.multiple_of(place * PAIR, HEAD_SIZE), HEAD_SIZE)
    value_columns = pl.ds(pl.multiple_of(place * PAIR + HEAD_SIZE, HEAD_SIZE), HEAD_SIZE)
    slot = pl.ds(pl.multiple_of(chunk * PAIR, HEAD_SIZE), PAIR)
    adapter = at[...]
    matrix = up[up_row : up_row + rank]

    if phase in (WHOLE, FRONT, BACK):
        keys = jnp.concatenate([halo[:span, key_columns], own[:, key_columns]], axis=0)
        values = jnp.concatenate([halo[:span, value_columns], own[:, value_columns]], axis=0)
    if phase in (WHOLE, FRONT):
        queries = fq[:, columns_of(step)].astype(jnp.float32) + dot(adapter, matrix, 0, 0)
        queries = queries.astype(jnp.bfloat16)
        query_stacks, probs = {}, {}
        for index in range(BLOCKS):
            query_stacks[index] = stacked(queries, slice(index * block, (index + 1) * block))
            probs[index] = softmax_block(
                query_stacks[index],
                keys[index * block : index * block + window],
                bias[index * window : (index + 1) * window],
            )
    else:
        query_stacks = {1: refs.query_stack[...]}
        probs = {1: refs.probs[...]}
    if phase == FRONT:
        refs.query_stack_out[...] = query_stacks[1]
        refs.probs_out[...] = probs[1]

    blocks = {WHOLE: (0, 1), FRONT: (0,), BACK: (1,), FINISH: (1,)}[phase]
    cot_stacks, dscores = {}, {}
    for index in blocks:
        start = index * block if phase == WHOLE else 0
        cot_stacks[index] = stacked(cot, slice(start, start + block))
        if phase == FINISH:
            dscores[index] = refs.dscores[...]
            continue
        low = index * block
        dscores[index], grad_stack = block_grads(
            probs[index], keys[low : low + window], values[low : low + window], cot_stacks[index]
        )
        for head in range(heads):
            columns = slice(head * HEAD_SIZE, (head + 1) * HEAD_SIZE)
            part = grad_stack[head * block : (head + 1) * block]
            refs.grad_out[start : start + block, columns] = part
    grad = (refs.pending1 if phase == FINISH else refs.grad_out)[...]
    if phase != WHOLE:
        grad = padded(grad, blocks[0], block)

    if phase != FINISH:
        weight_term = dot(adapter, grad, 1, 0)
        received_sum = jnp.zeros_like(weight_term) if first else refs.weight_sum[...]
        for name in names:
            if name in TERMS:
                received_sum += getattr(refs, name)[...].astype(jnp.float32)
    if phase == WHOLE:
        refs.weight_out[...] = received_sum
        refs.term_out[...] = weight_term.astype(jnp.bfloat16)
    elif phase == FRONT:
        refs.weight_out[...] = weight_term + received_sum
    elif phase == BACK:
        refs.dscores_out[...] = dscores[1]
        total = refs.total
        total[...] = (weight_term + received_sum).astype(jnp.bfloat16)
        shares = [name for name in names if name in SHARES]
        share_rows = rank // len(shares)
        for away, name in enumerate(shares):
            target = partner(lax.axis_index("dp"), away, len(shares))
            start = pl.multiple_of(target * share_rows, share_rows)
            getattr(refs, name)[...] = total[pl.ds(start, share_rows)]

    if phase != BACK:
        input_term = dot(matrix, grad, 1, 1)
        if not first:
            input_term += refs.input_sum[...]
        refs.input_out[...] = input_term.astype(refs.input_out.dtype)
        pair_total = refs.own_part[...] if phase == FINISH else 0.0
        for index in blocks:
            pair_total += pair_terms(
                index,
                block,
                span + rows,
                dscores[index],
                probs[index],
                query_stacks[index],
                cot_stacks[index],
            )
        if phase != FINISH:
            refs.halo_out[:, slot] = pair_total[:span].astype(refs.halo_out.dtype)
        if phase == FRONT:
            refs.own_part_out[...] = pair_total
        else:
            refs.own_out[:, slot] = pair_total[span:]
        if hasattr(refs, "pair_out"):
            low = rows - span
            refs.pair_out[:low] = refs.own_out[:low].astype(jnp.bfloat16)
            total = refs.own_out[low:] + refs.halo_back[...].astype(jnp.float32)
            refs.pair_out[low:] = total.astype(jnp.bfloat16)
    for copy in copies:
        copy.wait()


def chunk_step(step, phase, chunks, up_row, inputs, carried, pending, terms):
    fq, bias, at = inputs.fq, inputs.bias, inputs.at
    rows, columns = fq.shape
    width = columns // chunks
    heads = width // HEAD_SIZE
    rank = at.shape[0]
    block = rows // BLOCKS
    window = bias.shape[0] // BLOCKS
    span = window - block
    halo_type = jnp.bfloat16 if chunks == HK else jnp.float32

    outputs = {}
    if pending:
        outputs.update(dq_out=((rows, columns), jnp.bfloat16))
    if phase in (WHOLE, FRONT):
        outputs.update(halo_out=((span, chunks * PAIR), halo_type))
    if phase in (WHOLE, FINISH):
        outputs.update(own_out=((rows, chunks * PAIR), jnp.float32))
    handed = [name for name in outputs if hasattr(carried, name)]
    if phase != BACK:
        kind = jnp.bfloat16 if phase == FINISH else jnp.float32
        outputs.update(input_out=((rank, rows), kind))
    if phase != FINISH:
        grad_rows = rows if phase == WHOLE else block
        outputs.update(grad_out=((grad_rows, width), jnp.bfloat16))
    if phase == WHOLE:
        outputs.update(term_out=((rank, width), jnp.bfloat16))
    if phase in (WHOLE, FRONT):
        outputs.update(weight_out=((rank, width), jnp.float32))
    if phase == FRONT:
        outputs.update(query_stack_out=((heads * block, HEAD_SIZE), jnp.bfloat16))
        outputs.update(probs_out=((window, heads * block), jnp.float32))
        outputs.update(own_part_out=((span + rows, PAIR), jnp.float32))
    if phase == BACK:
        outputs.update(dscores_out=((window, heads * block), jnp.bfloat16))
        packs = lax.axis_size("dp")
        for away in range(packs):
            outputs[SHARES[away]] = ((rank // packs, width), jnp.bfloat16)

    operands = dict(vars(inputs))
    if hasattr(inputs, "halo_back"):
        outputs.update(pair_out=((rows, chunks * PAIR), jnp.bfloat16))
    aliases = {}
    for name in handed:
        aliases[len(operands)] = list(outputs).index(name)
        operands[name + IN] = getattr(carried, name)
    if step > 0 and phase != BACK:
        operands.update(input_sum=carried.input_out)
    if step > 0 and phase != FINISH:
        operands.update(weight_sum=carried.weight_out)
    if phase in (BACK, FINISH):
        operands.update(query_stack=carried.query_stack_out)
        operands.update(probs=carried.probs_out)
    if phase == FINISH:
        operands.update(own_part=carried.own_part_out)
        operands.update(dscores=carried.dscores_out)
    for index, (_, _, array) in enumerate(pending):
        operands[PENDING[index]] = array
    for index, term in enumerate(terms):
        operands[TERMS[index]] = term
    scratch = dict(
        total=pltpu.VMEM((rank, width), jnp.bfloat16),
        sems=pltpu.SemaphoreType.DMA((2,)),
    )
    names = list(operands) + list(outputs) + list(scratch)
    places = [(at_step, start, array.shape[0]) for at_step, start, array in pending]
    results = pl.pallas_call(
        functools.partial(chunk_kernel, step, phase, chunks, up_row, places, names),
        in_specs=[HBM if name == DQ_IN else VMEM for name in operands],
        out_specs=[HBM if name == DQ else VMEM for name in outputs],
        out_shape=[jax.ShapeDtypeStruct(*shape) for shape in outputs.values()],
        scratch_shapes=list(scratch.values()),
        input_output_aliases=aliases,
        compiler_params=pltpu.CompilerParams(vmem_limit_bytes=LIMIT),
        cost_estimate=pl.CostEstimate(
            flops=heads * 10 * rows * window * HEAD_SIZE,
            bytes_accessed=8 * rows * width,
            transcendentals=heads * rows * window,
        ),
        name="chunk_" + PHASE_NAMES[phase],
    )(*operands.values())
    vars(carried).update(zip(outputs, results))


def per_device(
    frozen_queries, key_value_pairs, adapter_input, adapter_up_matrix, upstream, document_index
):
    chunks = lax.axis_size("seq")
    place = lax.axis_index("seq")
    rows = frozen_queries.shape[2]
    block = rows // BLOCKS
    length = document_index.shape[2]
    span = length // SPAN_PARTS
    window = span + block
    per_head = chunks // HK
    steps = tuple(range(chunks))

    pieces = []
    left = span
    while left > 0:
        pieces.append((len(pieces) + 1, min(rows, left)))
        left -= rows

    own = key_value_pairs[0, 0]
    own_matrix = adapter_up_matrix[0]
    bundled = span if len(pieces) == 1 and own_matrix.shape[1] == own.shape[1] else 0

    parts = split_columns(steps[:1], chunks, 0, upstream[0, 0], own, own_matrix, [])
    parts += split_columns(steps[1:], chunks, bundled, upstream[0, 0], own, own_matrix, parts[:1])
    cots = [passed_along(part, "section", -1) for part in parts[: chunks + 1]]
    own_matrix = parts[chunks + 1]
    if bundled > 0:
        halo = passed_along(parts[-1], "seq", 1)
        matrices, up_rows = [halo], [span]
    else:
        halo_parts = [
            passed_along(own[rows - count :], "seq", distance) for distance, count in pieces
        ]
        halo = jnp.concatenate(halo_parts[::-1], axis=0)
        matrices, up_rows = [passed_along(own_matrix, "seq", 1)], [0]
    matrices += [passed_along(own_matrix, "seq", step + 1) for step in steps[1:-1]] + [own_matrix]
    up_rows += [0] * (chunks - 1)

    numbers = jnp.concatenate([jnp.full((span,), -1, jnp.int32), document_index[0, 0]])
    numbers = lax.dynamic_slice_in_dim(numbers, place * rows, span + rows, 0)
    reach = jnp.arange(window, dtype=jnp.int32)[:, None] <= (
        jnp.arange(block, dtype=jnp.int32)[None, :] + span
    )
    bias = []
    for start in range(0, rows, block):
        seen = numbers[start : start + window, None]
        same = seen == numbers[None, start + span : start + span + block]
        bias.append(jnp.where(same & reach, 0.0, -jnp.inf))
    bias = jnp.concatenate(bias, axis=0).astype(jnp.float32)
    bias = jnp.concatenate([bias, bias], axis=1)

    inputs = SimpleNamespace(
        fq=frozen_queries[0, 0], at=adapter_input[0, 0].T, halo=halo, own=own, bias=bias
    )
    carried, terms, pending = SimpleNamespace(), [], []
    for step in steps:
        phases = (WHOLE,) if step < chunks - 1 else (FRONT, BACK)
        for phase in phases:
            taken = 0 if step < 2 else len(terms) if phase == BACK else 1
            inputs.up = matrices[step]
            inputs.cot = cots[step + (phase == BACK)]
            written = [] if phase == BACK else pending
            chunk_step(
                step, phase, chunks, up_rows[step], inputs, carried, written, terms[:taken]
            )
            terms = terms[taken:]
            if phase == BACK:
                pending.append((step, block, carried.grad_out))
            else:
                pending = [(step, 0, carried.grad_out)]
            if phase == WHOLE:
                terms.append(passed_along(carried.term_out, "seq", -(step + 1)))

    packs = lax.axis_size("dp")
    weight_share = carried.share0.astype(jnp.float32)
    for away in range(1, packs):
        pairs = [(source, partner(source, away, packs)) for source in range(packs)]
        weight_share += lax.ppermute(getattr(carried, SHARES[away]), "dp", pairs).astype(jnp.float32)

    halo_grads = carried.halo_out
    if per_head > 1:
        halo_grads = jnp.sum(halo_grads.reshape(span, HK, per_head, PAIR), axis=2)
        halo_grads = halo_grads.astype(jnp.bfloat16).reshape(span, HK * PAIR)
    backs = []
    stop = span
    for distance, count in pieces:
        backs.append(passed_along(halo_grads[stop - count : stop], "seq", -distance))
        stop -= count
    if per_head == 1 and len(pieces) == 1:
        inputs.halo_back = backs[0]
    chunk_step(
        step, FINISH, chunks, up_rows[step], inputs, carried, pending, []
    )
    if hasattr(inputs, "halo_back"):
        pair_grads = carried.pair_out
    else:
        own_grads = jnp.sum(carried.own_out.reshape(rows, HK, per_head, PAIR), axis=2)
        own_grads = own_grads.reshape(rows, HK * PAIR)
        for back in backs:
            low = rows - back.shape[0]
            own_grads = own_grads.at[low:].add(back.astype(jnp.float32))
        pair_grads = own_grads.astype(jnp.bfloat16)

    return (
        carried.dq_out[None, None],
        pair_grads[None, None],
        carried.input_out.T[None, None],
        weight_share[None],
    )


def solution(mesh):
    placed = (
        P("section", "dp", "seq", None),
        P("section", "dp", "seq", None),
        P("section", "dp", "seq", None),
        P("section", None, "seq"),
        P("section", "dp", "seq", None),
        P("section", "dp", None),
    )
    return jax.shard_map(
        per_device,
        mesh=mesh,
        in_specs=placed,
        out_specs=(
            P("section", "dp", "seq", None),
            P("section", "dp", "seq", None),
            P("section", "dp", "seq", None),
            P("section", "dp", "seq"),
        ),
        check_vma=False,
    )
```

```python
import functools
import math
from types import SimpleNamespace

import jax
import jax.numpy as jnp
from jax import lax
from jax.experimental import pallas as pl
from jax.experimental.pallas import tpu as pltpu
from jax.sharding import PartitionSpec as P

QUERY_HEADS = 32
HK = 4
HEAD_SIZE = 128
PAIR = 2 * HEAD_SIZE
SCALE = 1.0 / math.sqrt(HEAD_SIZE)
SPAN_PARTS = 8

WHOLE, FRONT, BACK, FINISH = range(4)
PHASE_NAMES = ("whole", "front", "back", "finish")
IN = "_in"
DQ = "dq_out"
DQ_IN = DQ + IN
UPSTREAM = "upstream"
SHARES = ["share" + str(index) for index in range(64)]
PENDING = ["pending" + str(index) for index in range(2)]
TERMS = ["term_in" + str(index) for index in range(64)]

VMEM = pl.BlockSpec(memory_space=pltpu.VMEM)
HBM = pl.BlockSpec(memory_space=pltpu.HBM)
LIMIT = 16 * 1024 * 1024
BLOCKS = 2


def passed_along(value, axis, steps):
    count = lax.axis_size(axis)
    pairs = [(source, (source + steps) % count) for source in range(count)]
    return lax.ppermute(value, axis, pairs)


def dot(left, right, left_dim, right_dim):
    return lax.dot_general(
        left, right, (((left_dim,), (right_dim,)), ((), ())), preferred_element_type=jnp.float32
    )


def chunk_at(step, chunks):
    return lax.rem(lax.axis_index("seq") + (2 * chunks - 1 - step), chunks)


def piece_of(upstream, piece, chunks):
    rows = upstream.shape[0]
    width = upstream.shape[1] // chunks
    step = min(piece, chunks - 1)
    columns = pl.ds(pl.multiple_of(chunk_at(step, chunks) * width, HEAD_SIZE), width)
    if piece < chunks - 1:
        return upstream.at[:, columns]
    return upstream.at[pl.ds((piece - step) * (rows // BLOCKS), rows // BLOCKS), columns]


def piece_shape(upstream, piece, chunks):
    rows = upstream.shape[0] if piece < chunks - 1 else upstream.shape[0] // BLOCKS
    return jax.ShapeDtypeStruct((rows, upstream.shape[1] // chunks), upstream.dtype)


def split_kernel(piece, chunks, bundled, upstream, own, matrix, *rest):
    rest = list(rest)
    sems = rest.pop()
    if piece > 0:
        rest.pop(0)
    copies = []

    def send(source, target):
        copies.append(pltpu.make_async_copy(source, target, sems.at[len(copies)]))
        copies[-1].start()

    send(piece_of(upstream, piece, chunks), rest.pop(0))
    if piece == 2:
        send(matrix, rest.pop(0))
    if bundled > 0:
        bundle = rest.pop(0)
        send(own.at[pl.ds(own.shape[0] - bundled, bundled)], bundle.at[pl.ds(0, bundled)])
        send(matrix, bundle.at[pl.ds(bundled, matrix.shape[0])])
    for copy in copies:
        copy.wait()


def split_piece(piece, chunks, bundled, upstream, own, matrix, after):
    shapes = [piece_shape(upstream, piece, chunks)]
    if piece == 2:
        shapes.append(jax.ShapeDtypeStruct(matrix.shape, matrix.dtype))
    if bundled > 0:
        shapes.append(jax.ShapeDtypeStruct((bundled + matrix.shape[0], own.shape[1]), own.dtype))
    operands = [
        pltpu.with_memory_space_constraint(array, pltpu.HBM) for array in (upstream, own, matrix)
    ] + after
    return list(
        pl.pallas_call(
            functools.partial(split_kernel, piece, chunks, bundled),
            in_specs=[HBM] * 3 + [VMEM] * len(after),
            out_specs=[VMEM] * len(shapes),
            out_shape=shapes,
            scratch_shapes=[pltpu.SemaphoreType.DMA((len(shapes) + 1,))],
            compiler_params=pltpu.CompilerParams(vmem_limit_bytes=LIMIT),
            cost_estimate=pl.CostEstimate(
                flops=0, bytes_accessed=4 * upstream.size // chunks, transcendentals=0
            ),
            name="split_piece",
        )(*operands)
    )


def stacked(array, rows):
    heads = array.shape[1] // HEAD_SIZE
    parts = [array[rows, head * HEAD_SIZE : (head + 1) * HEAD_SIZE] for head in range(heads)]
    return jnp.concatenate(parts, axis=0)


def softmax_block(query_stack, key_window, hidden):
    copies = query_stack.shape[0] // hidden.shape[1]
    scores = dot(key_window, query_stack, 1, 1) * SCALE
    scores += jnp.concatenate([hidden] * copies, axis=1)
    shifted = jnp.exp(scores - jnp.max(scores, axis=0, keepdims=True))
    return shifted * (1.0 / jnp.sum(shifted, axis=0, keepdims=True))


def block_grads(probs, key_window, value_window, cot_stack):
    dprobs = dot(value_window, cot_stack, 1, 1)
    deltas = jnp.sum(probs * dprobs, axis=0, keepdims=True)
    dscores = (probs * (dprobs - deltas)).astype(jnp.bfloat16)
    return dscores, (dot(dscores, key_window, 0, 0) * SCALE).astype(jnp.bfloat16)


def pair_terms(index, block, total, dscores, probs, query_stack, cot_stack):
    key_term = dot(dscores, query_stack, 1, 0) * SCALE
    value_term = dot(probs.astype(jnp.bfloat16), cot_stack, 1, 0)
    term = jnp.concatenate([key_term, value_term], axis=1)
    start = index * block
    rest = total - term.shape[0] - start
    if start > 0:
        term = jnp.concatenate([jnp.zeros((start, PAIR), jnp.float32), term], axis=0)
    if rest > 0:
        term = jnp.concatenate([term, jnp.zeros((rest, PAIR), jnp.float32)], axis=0)
    return term


def padded(grad, index, block):
    blank = jnp.zeros((block, grad.shape[1]), grad.dtype)
    return jnp.concatenate([grad if place == index else blank for place in range(BLOCKS)], axis=0)


def chunk_kernel(step, phase, chunks, up_row, pending, names, *refs):
    refs = SimpleNamespace(**dict(zip(names, refs)))
    first = step == 0
    fq, at, up, cot = refs.fq, refs.at, refs.up, refs.cot
    halo, own, bias = refs.halo, refs.own, refs.bias
    rows = fq.shape[0]
    block = rows // BLOCKS
    rank = at.shape[0]
    window = bias.shape[0] // BLOCKS
    span = window - block
    width = fq.shape[1] // chunks
    heads = width // HEAD_SIZE

    def columns_of(at_step):
        return pl.ds(pl.multiple_of(chunk_at(at_step, chunks) * width, HEAD_SIZE), width)

    copies = []
    if hasattr(refs, "piece_out"):
        piece = piece_of(refs.upstream, step + 3, chunks)
        copies.append(pltpu.make_async_copy(piece, refs.piece_out, refs.sems.at[2]))
        copies[-1].start()
    for index, (at_step, start, count) in enumerate(pending):
        target = refs.dq_out.at[pl.ds(start, count), columns_of(at_step)]
        copies.append(pltpu.make_async_copy(getattr(refs, PENDING[index]), target, refs.sems.at[index]))
        copies[-1].start()

    chunk = chunk_at(step, chunks)
    place = lax.div(chunk, chunks // HK) if chunks > HK else chunk
    key_columns = pl.ds(pl.multiple_of(place * PAIR, HEAD_SIZE), HEAD_SIZE)
    value_columns = pl.ds(pl.multiple_of(place * PAIR + HEAD_SIZE, HEAD_SIZE), HEAD_SIZE)
    slot = pl.ds(pl.multiple_of(chunk * PAIR, HEAD_SIZE), PAIR)
    adapter = at[...]
    matrix = up[up_row : up_row + rank]

    if phase in (WHOLE, FRONT, BACK):
        keys = jnp.concatenate([halo[:span, key_columns], own[:, key_columns]], axis=0)
        values = jnp.concatenate([halo[:span, value_columns], own[:, value_columns]], axis=0)
    if phase in (WHOLE, FRONT):
        queries = fq[:, columns_of(step)].astype(jnp.float32) + dot(adapter, matrix, 0, 0)
        queries = queries.astype(jnp.bfloat16)
        query_stacks, probs = {}, {}
        for index in range(BLOCKS):
            query_stacks[index] = stacked(queries, slice(index * block, (index + 1) * block))
            probs[index] = softmax_block(
                query_stacks[index],
                keys[index * block : index * block + window],
                bias[index * window : (index + 1) * window],
            )
    else:
        query_stacks = {1: refs.query_stack[...]}
        probs = {1: refs.probs[...]}
    if phase == FRONT:
        refs.query_stack_out[...] = query_stacks[1]
        refs.probs_out[...] = probs[1]

    blocks = {WHOLE: (0, 1), FRONT: (0,), BACK: (1,), FINISH: (1,)}[phase]
    cot_stacks, dscores = {}, {}
    for index in blocks:
        start = index * block if phase == WHOLE else 0
        cot_stacks[index] = stacked(cot, slice(start, start + block))
        if phase == FINISH:
            dscores[index] = refs.dscores[...]
            continue
        low = index * block
        dscores[index], grad_stack = block_grads(
            probs[index], keys[low : low + window], values[low : low + window], cot_stacks[index]
        )
        for head in range(heads):
            columns = slice(head * HEAD_SIZE, (head + 1) * HEAD_SIZE)
            part = grad_stack[head * block : (head + 1) * block]
            refs.grad_out[start : start + block, columns] = part
    grad = (refs.pending1 if phase == FINISH else refs.grad_out)[...]
    if phase != WHOLE:
        grad = padded(grad, blocks[0], block)

    if phase != FINISH:
        weight_term = dot(adapter, grad, 1, 0)
        received_sum = jnp.zeros_like(weight_term) if first else refs.weight_sum[...]
        for name in names:
            if name in TERMS:
                received_sum += getattr(refs, name)[...].astype(jnp.float32)
    if phase == WHOLE:
        refs.weight_out[...] = received_sum
        refs.term_out[...] = weight_term.astype(jnp.bfloat16)
    elif phase == FRONT:
        refs.weight_out[...] = weight_term + received_sum
    elif phase == BACK:
        refs.dscores_out[...] = dscores[1]
        total = refs.total
        total[...] = (weight_term + received_sum).astype(jnp.bfloat16)
        shares = [name for name in names if name in SHARES]
        share_rows = rank // len(shares)
        for away, name in enumerate(shares):
            target = lax.rem(lax.axis_index("dp") + away, len(shares))
            start = pl.multiple_of(target * share_rows, share_rows)
            getattr(refs, name)[...] = total[pl.ds(start, share_rows)]

    if phase != BACK:
        input_term = dot(matrix, grad, 1, 1)
        if not first:
            input_term += refs.input_sum[...]
        refs.input_out[...] = input_term.astype(refs.input_out.dtype)
        pair_total = refs.own_part[...] if phase == FINISH else 0.0
        for index in blocks:
            pair_total += pair_terms(
                index,
                block,
                span + rows,
                dscores[index],
                probs[index],
                query_stacks[index],
                cot_stacks[index],
            )
        if phase != FINISH:
            refs.halo_out[:, slot] = pair_total[:span].astype(refs.halo_out.dtype)
        if phase == FRONT:
            refs.own_part_out[...] = pair_total
        else:
            refs.own_out[:, slot] = pair_total[span:]
        if hasattr(refs, "pair_out"):
            low = rows - span
            refs.pair_out[:low] = refs.own_out[:low].astype(jnp.bfloat16)
            total = refs.own_out[low:] + refs.halo_back[...].astype(jnp.float32)
            refs.pair_out[low:] = total.astype(jnp.bfloat16)
    for copy in copies:
        copy.wait()


def chunk_step(step, phase, chunks, up_row, inputs, carried, pending, terms):
    fq, bias, at = inputs.fq, inputs.bias, inputs.at
    rows, columns = fq.shape
    width = columns // chunks
    heads = width // HEAD_SIZE
    rank = at.shape[0]
    block = rows // BLOCKS
    window = bias.shape[0] // BLOCKS
    span = window - block
    halo_type = jnp.bfloat16 if chunks == HK else jnp.float32

    outputs = {}
    if pending:
        outputs.update(dq_out=((rows, columns), jnp.bfloat16))
    if phase in (WHOLE, FRONT):
        outputs.update(halo_out=((span, chunks * PAIR), halo_type))
    if phase in (WHOLE, FINISH):
        outputs.update(own_out=((rows, chunks * PAIR), jnp.float32))
    handed = [name for name in outputs if hasattr(carried, name)]
    if phase != BACK:
        kind = jnp.bfloat16 if phase == FINISH else jnp.float32
        outputs.update(input_out=((rank, rows), kind))
    if phase != FINISH:
        grad_rows = rows if phase == WHOLE else block
        outputs.update(grad_out=((grad_rows, width), jnp.bfloat16))
    if phase == WHOLE:
        outputs.update(term_out=((rank, width), jnp.bfloat16))
    if phase in (WHOLE, FRONT):
        outputs.update(weight_out=((rank, width), jnp.float32))
    if phase == FRONT:
        outputs.update(query_stack_out=((heads * block, HEAD_SIZE), jnp.bfloat16))
        outputs.update(probs_out=((window, heads * block), jnp.float32))
        outputs.update(own_part_out=((span + rows, PAIR), jnp.float32))
    if phase == BACK:
        outputs.update(dscores_out=((window, heads * block), jnp.bfloat16))
        packs = lax.axis_size("dp")
        for away in range(packs):
            outputs[SHARES[away]] = ((rank // packs, width), jnp.bfloat16)

    operands = dict(vars(inputs))
    if phase != WHOLE or step + 3 > chunks:
        del operands[UPSTREAM]
    else:
        outputs.update(piece_out=None)
    if hasattr(inputs, "halo_back"):
        outputs.update(pair_out=((rows, chunks * PAIR), jnp.bfloat16))
    aliases = {}
    for name in handed:
        aliases[len(operands)] = list(outputs).index(name)
        operands[name + IN] = getattr(carried, name)
    if step > 0 and phase != BACK:
        operands.update(input_sum=carried.input_out)
    if step > 0 and phase != FINISH:
        operands.update(weight_sum=carried.weight_out)
    if phase in (BACK, FINISH):
        operands.update(query_stack=carried.query_stack_out)
        operands.update(probs=carried.probs_out)
    if phase == FINISH:
        operands.update(own_part=carried.own_part_out)
        operands.update(dscores=carried.dscores_out)
    for index, (_, _, array) in enumerate(pending):
        operands[PENDING[index]] = array
    for index, term in enumerate(terms):
        operands[TERMS[index]] = term
    shapes = [shape and jax.ShapeDtypeStruct(*shape) for shape in outputs.values()]
    if hasattr(inputs, UPSTREAM) and None in shapes:
        shapes[shapes.index(None)] = piece_shape(inputs.upstream, step + 3, chunks)
    scratch = dict(
        total=pltpu.VMEM((rank, width), jnp.bfloat16),
        sems=pltpu.SemaphoreType.DMA((3,)),
    )
    names = list(operands) + list(outputs) + list(scratch)
    places = [(at_step, start, array.shape[0]) for at_step, start, array in pending]
    results = pl.pallas_call(
        functools.partial(chunk_kernel, step, phase, chunks, up_row, places, names),
        in_specs=[HBM if name in (DQ_IN, UPSTREAM) else VMEM for name in operands],
        out_specs=[HBM if name == DQ else VMEM for name in outputs],
        out_shape=shapes,
        scratch_shapes=list(scratch.values()),
        input_output_aliases=aliases,
        compiler_params=pltpu.CompilerParams(vmem_limit_bytes=LIMIT),
        cost_estimate=pl.CostEstimate(
            flops=heads * 10 * rows * window * HEAD_SIZE,
            bytes_accessed=8 * rows * width,
            transcendentals=heads * rows * window,
        ),
        name="chunk_" + PHASE_NAMES[phase],
    )(*operands.values())
    vars(carried).update(zip(outputs, results))


def per_device(
    frozen_queries, key_value_pairs, adapter_input, adapter_up_matrix, upstream, document_index
):
    chunks = lax.axis_size("seq")
    place = lax.axis_index("seq")
    rows = frozen_queries.shape[2]
    block = rows // BLOCKS
    length = document_index.shape[2]
    span = length // SPAN_PARTS
    window = span + block
    per_head = chunks // HK
    steps = tuple(range(chunks))

    pieces = []
    left = span
    while left > 0:
        pieces.append((len(pieces) + 1, min(rows, left)))
        left -= rows

    own = key_value_pairs[0, 0]
    own_matrix = adapter_up_matrix[0]
    bundled = span if len(pieces) == 1 and own_matrix.shape[1] == own.shape[1] else 0

    cotangents = upstream[0, 0]
    sources = (cotangents, own, own_matrix)
    first_piece = split_piece(0, chunks, 0, *sources, [])
    cots = [passed_along(first_piece[0], "section", -1)]
    parts = split_piece(1, chunks, bundled, *sources, first_piece)
    cots.append(passed_along(parts[0], "section", -1))
    later_part, own_matrix = split_piece(2, chunks, 0, *sources, cots[:1])
    cots.append(passed_along(later_part, "section", -1))
    if bundled > 0:
        halo = passed_along(parts[-1], "seq", 1)
        matrices, up_rows = [halo], [span]
    else:
        halo_parts = [
            passed_along(own[rows - count :], "seq", distance) for distance, count in pieces
        ]
        halo = jnp.concatenate(halo_parts[::-1], axis=0)
        matrices, up_rows = [passed_along(own_matrix, "seq", 1)], [0]
    matrices += [passed_along(own_matrix, "seq", step + 1) for step in steps[1:-1]] + [own_matrix]
    up_rows += [0] * (chunks - 1)

    numbers = jnp.concatenate([jnp.full((span,), -1, jnp.int32), document_index[0, 0]])
    numbers = lax.dynamic_slice_in_dim(numbers, place * rows, span + rows, 0)
    reach = jnp.arange(window, dtype=jnp.int32)[:, None] <= (
        jnp.arange(block, dtype=jnp.int32)[None, :] + span
    )
    bias = []
    for start in range(0, rows, block):
        seen = numbers[start : start + window, None]
        same = seen == numbers[None, start + span : start + span + block]
        bias.append(jnp.where(same & reach, 0.0, -jnp.inf))
    bias = jnp.concatenate(bias, axis=0).astype(jnp.float32)
    bias = jnp.concatenate([bias, bias], axis=1)

    inputs = SimpleNamespace(
        fq=frozen_queries[0, 0],
        at=adapter_input[0, 0].T,
        halo=halo,
        own=own,
        bias=bias,
        upstream=pltpu.with_memory_space_constraint(cotangents, pltpu.HBM),
    )
    carried, terms, pending = SimpleNamespace(), [], []
    for step in steps:
        phases = (WHOLE,) if step < chunks - 1 else (FRONT, BACK)
        for phase in phases:
            taken = 0 if step < 2 else len(terms) if phase == BACK else 1
            inputs.up = matrices[step]
            inputs.cot = cots[step + (phase == BACK)]
            written = [] if phase == BACK else pending
            chunk_step(
                step, phase, chunks, up_rows[step], inputs, carried, written, terms[:taken]
            )
            terms = terms[taken:]
            if phase == BACK:
                pending.append((step, block, carried.grad_out))
            else:
                pending = [(step, 0, carried.grad_out)]
            if phase == WHOLE and step + 3 <= chunks:
                cots.append(passed_along(carried.piece_out, "section", -1))
            if phase == WHOLE:
                terms.append(passed_along(carried.term_out, "seq", -(step + 1)))

    packs = lax.axis_size("dp")
    weight_share = carried.share0.astype(jnp.float32)
    for away in range(1, packs):
        share = passed_along(getattr(carried, SHARES[away]), "dp", away)
        weight_share += share.astype(jnp.float32)

    halo_grads = carried.halo_out
    if per_head > 1:
        halo_grads = jnp.sum(halo_grads.reshape(span, HK, per_head, PAIR), axis=2)
        halo_grads = halo_grads.astype(jnp.bfloat16).reshape(span, HK * PAIR)
    backs = []
    stop = span
    for distance, count in pieces:
        backs.append(passed_along(halo_grads[stop - count : stop], "seq", -distance))
        stop -= count
    if per_head == 1 and len(pieces) == 1:
        inputs.halo_back = backs[0]
    chunk_step(
        step, FINISH, chunks, up_rows[step], inputs, carried, pending, []
    )
    if hasattr(inputs, "halo_back"):
        pair_grads = carried.pair_out
    else:
        own_grads = jnp.sum(carried.own_out.reshape(rows, HK, per_head, PAIR), axis=2)
        own_grads = own_grads.reshape(rows, HK * PAIR)
        for back in backs:
            low = rows - back.shape[0]
            own_grads = own_grads.at[low:].add(back.astype(jnp.float32))
        pair_grads = own_grads.astype(jnp.bfloat16)

    return (
        carried.dq_out[None, None],
        pair_grads[None, None],
        carried.input_out.T[None, None],
        weight_share[None],
    )


def solution(mesh):
    placed = (
        P("section", "dp", "seq", None),
        P("section", "dp", "seq", None),
        P("section", "dp", "seq", None),
        P("section", None, "seq"),
        P("section", "dp", "seq", None),
        P("section", "dp", None),
    )
    return jax.shard_map(
        per_device,
        mesh=mesh,
        in_specs=placed,
        out_specs=(
            P("section", "dp", "seq", None),
            P("section", "dp", "seq", None),
            P("section", "dp", "seq", None),
            P("section", "dp", "seq"),
        ),
        check_vma=False,
    )
```

```python
import functools
import math
from types import SimpleNamespace

import jax
import jax.numpy as jnp
from jax import lax
from jax.experimental import pallas as pl
from jax.experimental.pallas import tpu as pltpu
from jax.sharding import PartitionSpec as P

QUERY_HEADS = 32
HK = 4
HEAD_SIZE = 128
PAIR = 2 * HEAD_SIZE
SCALE = 1.0 / math.sqrt(HEAD_SIZE)
SPAN_PARTS = 8
BLOCKS = 2
COPIES = 4
LIMIT = 16 * 1024 * 1024
IN = "_in"
IN_HBM = ("upstream", "pairs", "matrix", "dq", "dq" + IN)
VMEM = pl.BlockSpec(memory_space=pltpu.VMEM)
HBM = pl.BlockSpec(memory_space=pltpu.HBM)


def passed_along(value, axis, steps):
    count = lax.axis_size(axis)
    pairs = [(source, (source + steps) % count) for source in range(count)]
    return lax.ppermute(value, axis, pairs)


def dot(left, right, left_dim, right_dim):
    return lax.dot_general(
        left, right, (((left_dim,), (right_dim,)), ((), ())), preferred_element_type=jnp.float32
    )


def numbered(name, arrays):
    return {name + str(index): array for index, array in enumerate(arrays)}


def listed(refs, name):
    found = []
    while hasattr(refs, name + str(len(found))):
        found.append(getattr(refs, name + str(len(found))))
    return found


def run(body, sizes, inputs, outputs, scratch, flops=0):
    names = list(inputs) + list(outputs) + list(scratch)

    def kernel(*refs):
        body(sizes, SimpleNamespace(**dict(zip(names, refs))))

    operands = [
        pltpu.with_memory_space_constraint(array, pltpu.HBM) if name in IN_HBM[:3] else array
        for name, array in inputs.items()
    ]
    places = list(inputs)
    aliases = {
        places.index(name + IN): index
        for index, name in enumerate(outputs)
        if name + IN in inputs
    }
    results = pl.pallas_call(
        kernel,
        in_specs=[HBM if name in IN_HBM else VMEM for name in inputs],
        out_specs=[HBM if name in IN_HBM else VMEM for name in outputs],
        out_shape=[jax.ShapeDtypeStruct(shape, kind) for shape, kind in outputs.values()],
        scratch_shapes=list(scratch.values()),
        input_output_aliases=aliases,
        compiler_params=pltpu.CompilerParams(vmem_limit_bytes=LIMIT),
        cost_estimate=pl.CostEstimate(
            flops=flops, bytes_accessed=1024 * 1024, transcendentals=flops // 1024
        ),
        name=body.__name__,
    )(*operands)
    return SimpleNamespace(**dict(zip(outputs, results)))


def copy_rows(source, target, sems, copies):
    rows = source.shape[0] // COPIES
    for part in range(COPIES):
        piece = pl.ds(part * rows, rows)
        copies.append(
            pltpu.make_async_copy(source.at[piece], target.at[piece], sems.at[len(copies)])
        )
        copies[-1].start()


def chunk_at(step, chunks):
    return lax.rem(lax.axis_index("seq") + (2 * chunks - 1 - step), chunks)


def chunk_columns(z, step):
    return pl.ds(pl.multiple_of(chunk_at(step, z.chunks) * z.width, HEAD_SIZE), z.width)


def pair_columns(z, step):
    return pl.ds(pl.multiple_of(chunk_at(step, z.chunks) * PAIR, HEAD_SIZE), PAIR)


def split_first(z, refs):
    copies = []
    for step in (0, 1):
        target = refs.piece.at[:, pl.ds(step * z.width, z.width)]
        copy_rows(refs.upstream.at[:, chunk_columns(z, step)], target, refs.sems, copies)
    for copy in copies:
        copy.wait()


def split_rest(z, refs):
    copies = []
    pieces = listed(refs, "piece")
    for step, piece in zip(range(2, z.chunks - 1), pieces):
        copy_rows(refs.upstream.at[:, chunk_columns(z, step)], piece, refs.sems, copies)
    for index, piece in enumerate(pieces[-BLOCKS:]):
        rows = pl.ds(index * z.block, z.block)
        source = refs.upstream.at[rows, chunk_columns(z, z.chunks - 1)]
        copy_rows(source, piece, refs.sems, copies)
    copy_rows(refs.matrix, refs.matrix_copy, refs.sems, copies)
    if hasattr(refs, "bundle"):
        near = refs.pairs.at[pl.ds(z.rows - z.span, z.span)]
        copy_rows(near, refs.bundle.at[pl.ds(0, z.span)], refs.sems, copies)
        copy_rows(refs.matrix, refs.bundle.at[pl.ds(z.span, z.rank)], refs.sems, copies)
    for copy in copies:
        copy.wait()


def stacked(array, rows):
    heads = array.shape[1] // HEAD_SIZE
    parts = [array[rows, head * HEAD_SIZE : (head + 1) * HEAD_SIZE] for head in range(heads)]
    return jnp.concatenate(parts, axis=0)


def seen_rows(z, refs, step, second):
    per_head = z.chunks // HK
    chunk = chunk_at(step, z.chunks)
    place = lax.div(chunk, per_head) if per_head > 1 else chunk
    start = pl.multiple_of(place * PAIR + second * HEAD_SIZE, HEAD_SIZE)
    columns = pl.ds(start, HEAD_SIZE)
    return jnp.concatenate([refs.halo[: z.span, columns], refs.own[:, columns]], axis=0)


def windowed(z, array, index):
    return array[index * z.block : index * z.block + z.window]


def softmax_blocks(z, refs, step, matrix, keys):
    queries = refs.fq[:, chunk_columns(z, step)].astype(jnp.float32)
    queries = (queries + dot(refs.at[...], matrix, 0, 0)).astype(jnp.bfloat16)
    stacks, probs = [], []
    for index in range(BLOCKS):
        stack = stacked(queries, slice(index * z.block, (index + 1) * z.block))
        hidden = refs.bias[index * z.window : (index + 1) * z.window]
        scores = dot(windowed(z, keys, index), stack, 1, 1) * SCALE
        scores += jnp.concatenate([hidden] * (stack.shape[0] // hidden.shape[1]), axis=1)
        shifted = jnp.exp(scores - jnp.max(scores, axis=0, keepdims=True))
        stacks.append(stack)
        probs.append(shifted * (1.0 / jnp.sum(shifted, axis=0, keepdims=True)))
    return stacks, probs


def score_grads(z, index, probs, keys, values, cot_stack):
    dprobs = dot(windowed(z, values, index), cot_stack, 1, 1)
    deltas = jnp.sum(probs * dprobs, axis=0, keepdims=True)
    dscores = (probs * (dprobs - deltas)).astype(jnp.bfloat16)
    return dscores, (dot(dscores, windowed(z, keys, index), 0, 0) * SCALE).astype(jnp.bfloat16)


def unstack(z, grad_stack, target, start):
    for head in range(grad_stack.shape[0] // z.block):
        columns = slice(head * HEAD_SIZE, (head + 1) * HEAD_SIZE)
        target[start : start + z.block, columns] = grad_stack[head * z.block : (head + 1) * z.block]


def pair_terms(z, index, dscores, probs, query_stack, cot_stack):
    key_term = dot(dscores, query_stack, 1, 0) * SCALE
    value_term = dot(probs.astype(jnp.bfloat16), cot_stack, 1, 0)
    term = jnp.concatenate([key_term, value_term], axis=1)
    start = index * z.block
    rest = z.span + z.rows - z.window - start
    if start > 0:
        term = jnp.concatenate([jnp.zeros((start, PAIR), jnp.float32), term], axis=0)
    if rest > 0:
        term = jnp.concatenate([term, jnp.zeros((rest, PAIR), jnp.float32)], axis=0)
    return term


def padded(z, grad, index):
    blank = jnp.zeros((z.block, grad.shape[1]), grad.dtype)
    return jnp.concatenate([grad if place == index else blank for place in range(BLOCKS)], axis=0)


def forward(z, refs):
    step = z.chunks - 1
    keys = seen_rows(z, refs, step, 0)
    stacks, probs = softmax_blocks(z, refs, step, refs.up[...], keys)
    for index in range(BLOCKS):
        listed(refs, "stack")[index][...] = stacks[index]
        listed(refs, "probs")[index][...] = probs[index]


def whole(steps, z, refs):
    copies = []
    if hasattr(refs, "pending"):
        target = refs.dq.at[:, chunk_columns(z, steps[0] - 1)]
        copy_rows(refs.pending, target, refs.sems, copies)
    input_sum = refs.input_sum[...] if hasattr(refs, "input_sum") else 0.0
    for place, step in enumerate(steps):
        up = listed(refs, "up")[place]
        matrix = up[up.shape[0] - z.rank :]
        keys, values = seen_rows(z, refs, step, 0), seen_rows(z, refs, step, 1)
        stacks, probs = softmax_blocks(z, refs, step, matrix, keys)
        grad_ref = refs.grad if step == steps[-1] else refs.early
        cots = refs.cot[:, place * z.width : (place + 1) * z.width]
        pair_total = 0.0
        for index in range(BLOCKS):
            start = index * z.block
            cot_stack = stacked(cots, slice(start, start + z.block))
            dscores, grad_stack = score_grads(z, index, probs[index], keys, values, cot_stack)
            unstack(z, grad_stack, grad_ref, start)
            pair_total += pair_terms(z, index, dscores, probs[index], stacks[index], cot_stack)
        if step != steps[-1]:
            copy_rows(grad_ref, refs.dq.at[:, chunk_columns(z, step)], refs.sems, copies)
        grad = grad_ref[...]
        listed(refs, "term")[place][...] = dot(refs.at[...], grad, 1, 0).astype(jnp.bfloat16)
        refs.halo_grads[:, pair_columns(z, step)] = pair_total[: z.span].astype(
            refs.halo_grads.dtype
        )
        refs.own_grads[:, pair_columns(z, step)] = pair_total[z.span :]
        input_sum += dot(matrix, grad, 1, 1)
    refs.input_grad[...] = input_sum
    for copy in copies:
        copy.wait()


def front(z, refs):
    copies = []
    step = z.chunks - 1
    copy_rows(refs.pending, refs.dq.at[:, chunk_columns(z, step - 1)], refs.sems, copies)
    keys, values = seen_rows(z, refs, step, 0), seen_rows(z, refs, step, 1)
    probs = refs.probs[...]
    cot_stack = stacked(refs.cot, slice(0, z.block))
    dscores, grad_stack = score_grads(z, 0, probs, keys, values, cot_stack)
    unstack(z, grad_stack, refs.grad, 0)
    pair_total = pair_terms(z, 0, dscores, probs, refs.stack[...], cot_stack)
    refs.halo_grads[:, pair_columns(z, step)] = pair_total[: z.span].astype(refs.halo_grads.dtype)
    refs.own_part[...] = pair_total[z.span :]
    grad = padded(z, refs.grad[...], 0)
    weight = dot(refs.at[...], grad, 1, 0)
    for term in listed(refs, "term"):
        weight += term[...].astype(jnp.float32)
    refs.weight_part[...] = weight
    refs.input_grad[...] = refs.input_sum[...] + dot(refs.up[...], grad, 1, 1)
    for copy in copies:
        copy.wait()


def back(z, refs):
    step = z.chunks - 1
    keys, values = seen_rows(z, refs, step, 0), seen_rows(z, refs, step, 1)
    cot_stack = stacked(refs.cot, slice(0, z.block))
    dscores, grad_stack = score_grads(z, 1, refs.probs[...], keys, values, cot_stack)
    refs.dscores[...] = dscores
    unstack(z, grad_stack, refs.grad, 0)
    weight = refs.weight_part[...] + dot(refs.at[...], padded(z, refs.grad[...], 1), 1, 0)
    for term in listed(refs, "term"):
        weight += term[...].astype(jnp.float32)
    refs.total[...] = weight.astype(jnp.bfloat16)
    shares = listed(refs, "share")
    rows = z.rank // len(shares)
    for away, share in enumerate(shares):
        target = lax.rem(lax.axis_index("dp") + away, len(shares))
        share[...] = refs.total[pl.ds(pl.multiple_of(target * rows, rows), rows)]


def finish(z, refs):
    copies = []
    step = z.chunks - 1
    for index, grad in enumerate(listed(refs, "pending")):
        target = refs.dq.at[pl.ds(index * z.block, z.block), chunk_columns(z, step)]
        copy_rows(grad, target, refs.sems, copies)
    cot_stack = stacked(refs.cot, slice(0, z.block))
    pair_total = pair_terms(z, 1, refs.dscores[...], refs.probs[...], refs.stack[...], cot_stack)
    refs.own_grads[:, pair_columns(z, step)] = refs.own_part[...] + pair_total[z.span :]
    grad = padded(z, refs.pending1[...], 1)
    input_grad = refs.input_sum[...] + dot(refs.up[...], grad, 1, 1)
    refs.input_grad[...] = input_grad.astype(jnp.bfloat16)
    if hasattr(refs, "halo_back"):
        low = z.rows - z.span
        refs.pair_grads[:low] = refs.own_grads[:low].astype(jnp.bfloat16)
        total = refs.own_grads[low:] + refs.halo_back[...].astype(jnp.float32)
        refs.pair_grads[low:] = total.astype(jnp.bfloat16)
    for copy in copies:
        copy.wait()


def per_device(
    frozen_queries, key_value_pairs, adapter_input, adapter_up_matrix, upstream, document_index
):
    bf16, f32 = jnp.bfloat16, jnp.float32
    chunks = lax.axis_size("seq")
    packs = lax.axis_size("dp")
    place = lax.axis_index("seq")
    rows = frozen_queries.shape[2]
    columns = QUERY_HEADS * HEAD_SIZE
    block = rows // BLOCKS
    span = document_index.shape[2] // SPAN_PARTS
    window = span + block
    width = columns // chunks
    rank = adapter_input.shape[3]
    stack_rows = width // HEAD_SIZE * block
    per_head = chunks // HK
    last = chunks - 1
    z = SimpleNamespace(
        chunks=chunks, rows=rows, block=block, span=span, window=window, width=width, rank=rank
    )
    flops = 10 * stack_rows * window * HEAD_SIZE

    pieces = []
    left = span
    while left > 0:
        pieces.append((len(pieces) + 1, min(rows, left)))
        left -= rows

    own = key_value_pairs[0, 0]
    matrix = adapter_up_matrix[0]
    cotangents = upstream[0, 0]
    bundled = len(pieces) == 1 and matrix.shape[1] == own.shape[1]

    def sems(count):
        return dict(sems=pltpu.SemaphoreType.DMA((count * COPIES,)))

    first = run(
        split_first,
        z,
        dict(upstream=cotangents),
        dict(piece=((rows, 2 * width), bf16)),
        sems(2),
    ).piece
    cots = {0: passed_along(first, "section", -1)}
    held = [((rows, width), bf16)] * (last - 2) + [((block, width), bf16)] * BLOCKS
    outputs = numbered("piece", held) | dict(matrix_copy=((rank, width), bf16))
    if bundled:
        outputs.update(bundle=((span + rank, width), bf16))
    parts = run(
        split_rest,
        z,
        dict(upstream=cotangents, pairs=own, matrix=matrix, after=first),
        outputs,
        sems(len(outputs) + 1),
    )
    held = listed(parts, "piece")
    matrix_copy = parts.matrix_copy
    if bundled:
        halo = passed_along(parts.bundle, "seq", 1)
        ups = [halo]
    else:
        halo = [passed_along(own[rows - count :], "seq", distance) for distance, count in pieces]
        halo = jnp.concatenate(halo[::-1], axis=0)
        ups = [passed_along(matrix_copy, "seq", 1)]
    ups += [passed_along(matrix_copy, "seq", step + 1) for step in range(1, last)]

    numbers = jnp.concatenate([jnp.full((span,), -1, jnp.int32), document_index[0, 0]])
    numbers = lax.dynamic_slice_in_dim(numbers, place * rows, span + rows, 0)
    reach = jnp.arange(window, dtype=jnp.int32)[:, None] <= (
        jnp.arange(block, dtype=jnp.int32)[None, :] + span
    )
    bias = []
    for start in range(0, rows, block):
        seen = numbers[start : start + window, None]
        same = seen == numbers[None, start + span : start + span + block]
        bias.append(jnp.where(same & reach, 0.0, -jnp.inf))
    bias = jnp.concatenate(bias, axis=0).astype(f32)
    bias = jnp.concatenate([bias, bias], axis=1)
    fq = frozen_queries[0, 0]
    at = adapter_input[0, 0].T

    outputs = numbered("stack", [((stack_rows, HEAD_SIZE), bf16)] * BLOCKS)
    outputs |= numbered("probs", [((window, stack_rows), f32)] * BLOCKS)
    outputs.update(held=(held[0].shape, bf16))
    ahead = run(
        forward,
        z,
        dict(fq=fq, at=at, up=matrix_copy, halo=halo, own=own, bias=bias, held_in=held[0]),
        outputs,
        {},
        flops,
    )
    cots[2] = passed_along(ahead.held, "section", -1)

    halo_type = bf16 if per_head == 1 else f32
    halo_shape = ((span, chunks * PAIR), halo_type)
    own_shape = ((rows, chunks * PAIR), f32)
    dq_shape = ((rows, columns), bf16)
    input_shape = ((rank, rows), f32)
    terms = []
    state = None
    for steps in [(0, 1)] + [(step,) for step in range(2, last)]:
        inputs = dict(fq=fq, at=at, halo=halo, own=own, bias=bias, cot=cots[steps[0]])
        inputs |= numbered("up", [ups[step] for step in steps])
        outputs = dict(
            dq=dq_shape,
            halo_grads=halo_shape,
            own_grads=own_shape,
            input_grad=input_shape,
            grad=((rows, width), bf16),
        )
        outputs |= numbered("term", [((rank, width), bf16)] * len(steps))
        scratch = sems(len(steps))
        later = []
        if state is None:
            later = held[1:-1]
            scratch.update(early=pltpu.VMEM((rows, width), bf16))
        else:
            inputs.update(
                dq_in=state.dq,
                halo_grads_in=state.halo_grads,
                own_grads_in=state.own_grads,
                input_sum=state.input_grad,
                pending=state.grad,
            )
        if steps[0] == 2:
            later = held[-1:]
        named = numbered("later", later)
        inputs |= {name + IN: array for name, array in named.items()}
        outputs |= {name: (array.shape, bf16) for name, array in named.items()}
        body = functools.partial(whole, steps)
        body.__name__ = whole.__name__
        state = run(body, z, inputs, outputs, scratch, 2 * len(steps) * flops)
        for array in listed(state, "later"):
            cots[len(cots) + 1] = passed_along(array, "section", -1)
        for step, term in zip(steps, listed(state, "term")):
            terms.append(passed_along(term, "seq", -(step + 1)))

    common = dict(at=at, up=matrix, halo=halo, own=own)
    outputs = dict(
        dq=dq_shape,
        halo_grads=halo_shape,
        own_part=((rows, PAIR), f32),
        weight_part=((rank, width), f32),
        input_grad=input_shape,
        grad=((block, width), bf16),
    )
    early = run(
        front,
        z,
        common
        | dict(
            cot=cots[last],
            stack=ahead.stack0,
            probs=ahead.probs0,
            dq_in=state.dq,
            halo_grads_in=state.halo_grads,
            input_sum=state.input_grad,
            pending=state.grad,
        )
        | numbered("term", terms[:-1]),
        outputs,
        sems(1),
        flops,
    )
    halo_grads = early.halo_grads
    if per_head > 1:
        halo_grads = jnp.sum(halo_grads.reshape(span, HK, per_head, PAIR), axis=2)
        halo_grads = halo_grads.astype(bf16).reshape(span, HK * PAIR)
    backs = []
    stop = span
    for distance, count in pieces:
        backs.append(passed_along(halo_grads[stop - count : stop], "seq", -distance))
        stop -= count

    outputs = dict(grad=((block, width), bf16), dscores=((window, stack_rows), bf16))
    outputs |= numbered("share", [((rank // packs, width), bf16)] * packs)
    late = run(
        back,
        z,
        common
        | dict(cot=cots[last + 1], probs=ahead.probs1, weight_part=early.weight_part)
        | numbered("term", terms[-1:]),
        outputs,
        dict(total=pltpu.VMEM((rank, width), bf16)),
        flops,
    )
    shares = listed(late, "share")
    shares[1:] = [passed_along(shares[away], "dp", away) for away in range(1, packs)]

    merged = per_head == 1 and len(pieces) == 1
    outputs = dict(dq=dq_shape, own_grads=own_shape, input_grad=((rank, rows), bf16))
    inputs = dict(
        at=at,
        up=matrix,
        cot=cots[last + 1],
        stack=ahead.stack1,
        probs=ahead.probs1,
        dscores=late.dscores,
        own_part=early.own_part,
        input_sum=early.input_grad,
        dq_in=early.dq,
        own_grads_in=state.own_grads,
        share_in=shares[0],
    )
    outputs.update(share=(shares[0].shape, bf16))
    if merged:
        inputs.update(halo_back=backs[0])
        outputs.update(pair_grads=((rows, HK * PAIR), bf16))
    final = run(
        finish,
        z,
        inputs | numbered("pending", [early.grad, late.grad]),
        outputs,
        sems(BLOCKS),
        flops,
    )
    weight_share = final.share.astype(f32)
    for share in shares[1:]:
        weight_share += share.astype(f32)
    if merged:
        pair_grads = final.pair_grads
    else:
        own_grads = jnp.sum(final.own_grads.reshape(rows, HK, per_head, PAIR), axis=2)
        own_grads = own_grads.reshape(rows, HK * PAIR)
        for rows_back in backs:
            low = rows - rows_back.shape[0]
            own_grads = own_grads.at[low:].add(rows_back.astype(f32))
        pair_grads = own_grads.astype(bf16)

    return (
        final.dq[None, None],
        pair_grads[None, None],
        final.input_grad.T[None, None],
        weight_share[None],
    )


def solution(mesh):
    placed = (
        P("section", "dp", "seq", None),
        P("section", "dp", "seq", None),
        P("section", "dp", "seq", None),
        P("section", None, "seq"),
        P("section", "dp", "seq", None),
        P("section", "dp", None),
    )
    return jax.shard_map(
        per_device,
        mesh=mesh,
        in_specs=placed,
        out_specs=(
            P("section", "dp", "seq", None),
            P("section", "dp", "seq", None),
            P("section", "dp", "seq", None),
            P("section", "dp", "seq"),
        ),
        check_vma=False,
    )
```

```python
import functools
import math
from types import SimpleNamespace

import jax
import jax.numpy as jnp
from jax import lax
from jax.experimental import pallas as pl
from jax.experimental.pallas import tpu as pltpu
from jax.sharding import PartitionSpec as P

QUERY_HEADS = 32
HK = 4
HEAD_SIZE = 128
PAIR = 2 * HEAD_SIZE
SCALE = 1.0 / math.sqrt(HEAD_SIZE)
SPAN_PARTS = 8
BLOCKS = 2
COPIES = 4
LIMIT = 16 * 1024 * 1024
IN = "_in"
IN_HBM = ("upstream", "pairs", "matrix", "dq", "dq" + IN)
VMEM = pl.BlockSpec(memory_space=pltpu.VMEM)
HBM = pl.BlockSpec(memory_space=pltpu.HBM)


def passed_along(value, axis, steps):
    count = lax.axis_size(axis)
    pairs = [(source, (source + steps) % count) for source in range(count)]
    return lax.ppermute(value, axis, pairs)


def swapped(value, axis, bit):
    pairs = [(source, source ^ bit) for source in range(lax.axis_size(axis))]
    return lax.ppermute(value, axis, pairs)


def dot(left, right, left_dim, right_dim):
    return lax.dot_general(
        left, right, (((left_dim,), (right_dim,)), ((), ())), preferred_element_type=jnp.float32
    )


def low_bit(number):
    return number & -number


def numbered(name, arrays):
    return {name + str(index): array for index, array in enumerate(arrays)}


def listed(refs, name):
    found = []
    while hasattr(refs, name + str(len(found))):
        found.append(getattr(refs, name + str(len(found))))
    return found


def run(body, sizes, inputs, outputs, scratch, flops=0):
    names = list(inputs) + list(outputs) + list(scratch)

    def kernel(*refs):
        body(sizes, SimpleNamespace(**dict(zip(names, refs))))

    operands = [
        pltpu.with_memory_space_constraint(array, pltpu.HBM) if name in IN_HBM[:3] else array
        for name, array in inputs.items()
    ]
    places = list(inputs)
    aliases = {
        places.index(name + IN): index
        for index, name in enumerate(outputs)
        if name + IN in inputs
    }
    results = pl.pallas_call(
        kernel,
        in_specs=[HBM if name in IN_HBM else VMEM for name in inputs],
        out_specs=[HBM if name in IN_HBM else VMEM for name in outputs],
        out_shape=[jax.ShapeDtypeStruct(shape, kind) for shape, kind in outputs.values()],
        scratch_shapes=list(scratch.values()),
        input_output_aliases=aliases,
        compiler_params=pltpu.CompilerParams(vmem_limit_bytes=LIMIT),
        cost_estimate=pl.CostEstimate(
            flops=flops, bytes_accessed=1024 * 1024, transcendentals=flops // 1024
        ),
        name=body.__name__,
    )(*operands)
    return SimpleNamespace(**dict(zip(outputs, results)))


def copy_rows(source, target, sems, copies, parts=1):
    rows = source.shape[0] // parts
    for part in range(parts):
        piece = pl.ds(part * rows, rows)
        copies.append(
            pltpu.make_async_copy(source.at[piece], target.at[piece], sems.at[len(copies)])
        )
        copies[-1].start()


def chunk_at(step, chunks):
    return lax.axis_index("seq") ^ (chunks - 1 - step)


def chunk_columns(z, step):
    return pl.ds(pl.multiple_of(chunk_at(step, z.chunks) * z.width, HEAD_SIZE), z.width)


def pair_columns(z, step):
    return pl.ds(pl.multiple_of(chunk_at(step, z.chunks) * PAIR, HEAD_SIZE), PAIR)


def split_first(z, refs):
    copies = []
    source = refs.upstream.at[:, chunk_columns(z, 0)]
    copy_rows(source, refs.piece, refs.sems, copies, COPIES)
    for copy in copies:
        copy.wait()


def split_rest(z, refs):
    copies = []
    pieces = listed(refs, "piece")
    for step, piece in zip(range(1, z.chunks - 1), pieces):
        copy_rows(refs.upstream.at[:, chunk_columns(z, step)], piece, refs.sems, copies, COPIES)
    for index, piece in enumerate(pieces[-BLOCKS:]):
        rows = pl.ds(index * z.block, z.block)
        source = refs.upstream.at[rows, chunk_columns(z, z.chunks - 1)]
        copy_rows(source, piece, refs.sems, copies, COPIES)
    copy_rows(refs.matrix, refs.matrix_copy, refs.sems, copies, COPIES)
    copy_rows(refs.pairs, refs.pairs_copy, refs.sems, copies, COPIES)
    for copy in copies:
        copy.wait()


def stacked(array, rows):
    heads = array.shape[1] // HEAD_SIZE
    parts = [array[rows, head * HEAD_SIZE : (head + 1) * HEAD_SIZE] for head in range(heads)]
    return jnp.concatenate(parts, axis=0)


def seen_rows(z, refs, step, second):
    per_head = z.chunks // HK
    chunk = chunk_at(step, z.chunks)
    place = lax.div(chunk, per_head) if per_head > 1 else chunk
    start = pl.multiple_of(place * PAIR + second * HEAD_SIZE, HEAD_SIZE)
    columns = pl.ds(start, HEAD_SIZE)
    return jnp.concatenate([refs.halo[: z.span, columns], refs.own[:, columns]], axis=0)


def windowed(z, array, index):
    return array[index * z.block : index * z.block + z.window]


def softmax_blocks(z, refs, step, matrix, keys):
    queries = refs.fq[:, chunk_columns(z, step)].astype(jnp.float32)
    queries = (queries + dot(refs.at[...], matrix, 0, 0)).astype(jnp.bfloat16)
    stacks, probs = [], []
    for index in range(BLOCKS):
        stack = stacked(queries, slice(index * z.block, (index + 1) * z.block))
        hidden = refs.bias[index * z.window : (index + 1) * z.window]
        scores = dot(windowed(z, keys, index), stack, 1, 1) * SCALE
        scores += jnp.concatenate([hidden] * (stack.shape[0] // hidden.shape[1]), axis=1)
        shifted = jnp.exp(scores - jnp.max(scores, axis=0, keepdims=True))
        stacks.append(stack)
        probs.append(shifted * (1.0 / jnp.sum(shifted, axis=0, keepdims=True)))
    return stacks, probs


def score_grads(z, index, probs, keys, values, cot_stack):
    dprobs = dot(windowed(z, values, index), cot_stack, 1, 1)
    deltas = jnp.sum(probs * dprobs, axis=0, keepdims=True)
    dscores = (probs * (dprobs - deltas)).astype(jnp.bfloat16)
    return dscores, (dot(dscores, windowed(z, keys, index), 0, 0) * SCALE).astype(jnp.bfloat16)


def unstack(z, grad_stack, target, start):
    for head in range(grad_stack.shape[0] // z.block):
        columns = slice(head * HEAD_SIZE, (head + 1) * HEAD_SIZE)
        target[start : start + z.block, columns] = grad_stack[head * z.block : (head + 1) * z.block]


def pair_terms(z, index, dscores, probs, query_stack, cot_stack):
    key_term = dot(dscores, query_stack, 1, 0) * SCALE
    value_term = dot(probs.astype(jnp.bfloat16), cot_stack, 1, 0)
    term = jnp.concatenate([key_term, value_term], axis=1)
    start = index * z.block
    rest = z.span + z.rows - z.window - start
    if start > 0:
        term = jnp.concatenate([jnp.zeros((start, PAIR), jnp.float32), term], axis=0)
    if rest > 0:
        term = jnp.concatenate([term, jnp.zeros((rest, PAIR), jnp.float32)], axis=0)
    return term


def padded(z, grad, index):
    blank = jnp.zeros((z.block, grad.shape[1]), grad.dtype)
    return jnp.concatenate([grad if place == index else blank for place in range(BLOCKS)], axis=0)


def forward(z, refs):
    step = z.chunks - 1
    keys = seen_rows(z, refs, step, 0)
    stacks, probs = softmax_blocks(z, refs, step, refs.up[...], keys)
    for index in range(BLOCKS):
        listed(refs, "stack")[index][...] = stacks[index]
        listed(refs, "probs")[index][...] = probs[index]


def whole(step, z, refs):
    copies = []
    if hasattr(refs, "pending"):
        copy_rows(refs.pending, refs.dq.at[:, chunk_columns(z, step - 1)], refs.sems, copies)
    matrix = refs.up[...]
    keys, values = seen_rows(z, refs, step, 0), seen_rows(z, refs, step, 1)
    stacks, probs = softmax_blocks(z, refs, step, matrix, keys)
    pair_total = 0.0
    for index in range(BLOCKS):
        start = index * z.block
        cot_stack = stacked(refs.cot, slice(start, start + z.block))
        dscores, grad_stack = score_grads(z, index, probs[index], keys, values, cot_stack)
        unstack(z, grad_stack, refs.grad, start)
        pair_total += pair_terms(z, index, dscores, probs[index], stacks[index], cot_stack)
    grad = refs.grad[...]
    weight = dot(refs.at[...], grad, 1, 0)
    for term in listed(refs, "term"):
        weight += term[...].astype(jnp.float32)
    refs.weight[...] = weight.astype(jnp.bfloat16)
    kind = refs.halo_grads.dtype
    refs.halo_grads[:, pair_columns(z, step)] = pair_total[: z.span].astype(kind)
    refs.own_grads[:, pair_columns(z, step)] = pair_total[z.span :]
    input_grad = dot(matrix, grad, 1, 1)
    if step > 0:
        input_grad += refs.input_sum[...]
    refs.input_grad[...] = input_grad
    for copy in copies:
        copy.wait()


def front(z, refs):
    copies = []
    step = z.chunks - 1
    for place, grad in enumerate(listed(refs, "pending")):
        target = refs.dq.at[:, chunk_columns(z, step - BLOCKS + place)]
        copy_rows(grad, target, refs.sems, copies)
    keys, values = seen_rows(z, refs, step, 0), seen_rows(z, refs, step, 1)
    probs = refs.probs[...]
    cot_stack = stacked(refs.cot, slice(0, z.block))
    dscores, grad_stack = score_grads(z, 0, probs, keys, values, cot_stack)
    unstack(z, grad_stack, refs.grad, 0)
    pair_total = pair_terms(z, 0, dscores, probs, refs.stack[...], cot_stack)
    refs.halo_grads[:, pair_columns(z, step)] = pair_total[: z.span].astype(refs.halo_grads.dtype)
    refs.own_part[...] = pair_total[z.span :]
    grad = padded(z, refs.grad[...], 0)
    weight = dot(refs.at[...], grad, 1, 0)
    for term in listed(refs, "term"):
        weight += term[...].astype(jnp.float32)
    refs.weight_part[...] = weight
    refs.input_grad[...] = refs.input_sum[...] + dot(refs.up[...], grad, 1, 1)
    for copy in copies:
        copy.wait()


def back(z, refs):
    step = z.chunks - 1
    keys, values = seen_rows(z, refs, step, 0), seen_rows(z, refs, step, 1)
    cot_stack = stacked(refs.cot, slice(0, z.block))
    dscores, grad_stack = score_grads(z, 1, refs.probs[...], keys, values, cot_stack)
    refs.dscores[...] = dscores
    unstack(z, grad_stack, refs.grad, 0)
    weight = refs.weight_part[...] + dot(refs.at[...], padded(z, refs.grad[...], 1), 1, 0)
    for term in listed(refs, "term"):
        weight += term[...].astype(jnp.float32)
    refs.total[...] = weight.astype(jnp.bfloat16)
    shares = listed(refs, "share")
    rows = z.rank // len(shares)
    for away, share in enumerate(shares):
        target = lax.rem(lax.axis_index("dp") + away, len(shares))
        share[...] = refs.total[pl.ds(pl.multiple_of(target * rows, rows), rows)]


def finish(z, refs):
    copies = []
    step = z.chunks - 1
    for index, grad in enumerate(listed(refs, "pending")):
        target = refs.dq.at[pl.ds(index * z.block, z.block), chunk_columns(z, step)]
        copy_rows(grad, target, refs.sems, copies)
    cot_stack = stacked(refs.cot, slice(0, z.block))
    pair_total = pair_terms(z, 1, refs.dscores[...], refs.probs[...], refs.stack[...], cot_stack)
    refs.own_grads[:, pair_columns(z, step)] = refs.own_part[...] + pair_total[z.span :]
    grad = padded(z, refs.pending1[...], 1)
    input_grad = refs.input_sum[...] + dot(refs.up[...], grad, 1, 1)
    refs.input_grad[...] = input_grad.astype(jnp.bfloat16)
    if hasattr(refs, "halo_back"):
        low = z.rows - z.span
        refs.pair_grads[:low] = refs.own_grads[:low].astype(jnp.bfloat16)
        total = refs.own_grads[low:] + refs.halo_back[...].astype(jnp.float32)
        refs.pair_grads[low:] = total.astype(jnp.bfloat16)
    for copy in copies:
        copy.wait()


def per_device(
    frozen_queries, key_value_pairs, adapter_input, adapter_up_matrix, upstream, document_index
):
    bf16, f32 = jnp.bfloat16, jnp.float32
    chunks = lax.axis_size("seq")
    packs = lax.axis_size("dp")
    place = lax.axis_index("seq")
    rows = frozen_queries.shape[2]
    columns = QUERY_HEADS * HEAD_SIZE
    block = rows // BLOCKS
    span = document_index.shape[2] // SPAN_PARTS
    window = span + block
    width = columns // chunks
    rank = adapter_input.shape[3]
    stack_rows = width // HEAD_SIZE * block
    per_head = chunks // HK
    last = chunks - 1
    z = SimpleNamespace(
        chunks=chunks, rows=rows, block=block, span=span, window=window, width=width, rank=rank
    )
    flops = 10 * stack_rows * window * HEAD_SIZE

    pieces = []
    left = span
    while left > 0:
        pieces.append((len(pieces) + 1, min(rows, left)))
        left -= rows

    own = key_value_pairs[0, 0]
    matrix = adapter_up_matrix[0]
    cotangents = upstream[0, 0]

    def sems(count):
        return dict(sems=pltpu.SemaphoreType.DMA((count,)))

    piece = ((rows, width), bf16)
    first = run(split_first, z, dict(upstream=cotangents), dict(piece=piece), sems(COPIES)).piece
    cots = [passed_along(first, "section", -1)]
    outputs = numbered("piece", [piece] * (last - 1) + [((block, width), bf16)] * BLOCKS)
    outputs.update(matrix_copy=((rank, width), bf16), pairs_copy=(own.shape, bf16))
    parts = run(
        split_rest,
        z,
        dict(upstream=cotangents, pairs=own, matrix=matrix, after=first),
        outputs,
        sems(COPIES * len(outputs)),
    )
    held = listed(parts, "piece")
    cots.append(passed_along(held[0], "section", -1))
    own, matrix = parts.pairs_copy, parts.matrix_copy
    halo = [passed_along(own[rows - count :], "seq", distance) for distance, count in pieces]
    halo = jnp.concatenate(halo[::-1], axis=0)
    ups = {0: matrix}
    for away in sorted(range(1, chunks), key=low_bit, reverse=True):
        bit = low_bit(away)
        ups[away] = swapped(ups[away - bit], "seq", bit)

    numbers = jnp.concatenate([jnp.full((span,), -1, jnp.int32), document_index[0, 0]])
    numbers = lax.dynamic_slice_in_dim(numbers, place * rows, span + rows, 0)
    reach = jnp.arange(window, dtype=jnp.int32)[:, None] <= (
        jnp.arange(block, dtype=jnp.int32)[None, :] + span
    )
    bias = []
    for start in range(0, rows, block):
        seen = numbers[start : start + window, None]
        same = seen == numbers[None, start + span : start + span + block]
        bias.append(jnp.where(same & reach, 0.0, -jnp.inf))
    bias = jnp.concatenate(bias, axis=0).astype(f32)
    bias = jnp.concatenate([bias, bias], axis=1)
    fq = frozen_queries[0, 0]
    at = adapter_input[0, 0].T

    outputs = numbered("stack", [((stack_rows, HEAD_SIZE), bf16)] * BLOCKS)
    outputs |= numbered("probs", [((window, stack_rows), f32)] * BLOCKS)
    outputs.update(held=(held[1].shape, bf16))
    ahead = run(
        forward,
        z,
        dict(fq=fq, at=at, up=matrix, halo=halo, own=own, bias=bias, held_in=held[1]),
        outputs,
        {},
        flops,
    )
    cots.append(passed_along(ahead.held, "section", -1))

    halo_shape = ((span, chunks * PAIR), bf16 if per_head == 1 else f32)
    own_shape = ((rows, chunks * PAIR), f32)
    dq_shape = ((rows, columns), bf16)
    input_shape = ((rank, rows), f32)
    terms = {away: [] for away in range(chunks)}
    grads = []
    state = None
    for step in range(last):
        away = last - step
        inputs = dict(fq=fq, at=at, halo=halo, own=own, bias=bias, cot=cots[step], up=ups[away])
        inputs |= numbered("term", terms[away])
        outputs = dict(
            halo_grads=halo_shape,
            own_grads=own_shape,
            input_grad=input_shape,
            grad=piece,
            weight=((rank, width), bf16),
        )
        if step > 0:
            inputs.update(
                halo_grads_in=state.halo_grads,
                own_grads_in=state.own_grads,
                input_sum=state.input_grad,
            )
        if 0 < step < last - 1:
            inputs.update(pending=grads[-1])
            outputs.update(dq=dq_shape)
            if step > 1:
                inputs.update(dq_in=dq)
        if step + 2 < len(held):
            inputs.update(held_in=held[step + 2])
            outputs.update(held=(held[step + 2].shape, bf16))
        body = functools.partial(whole, step)
        body.__name__ = whole.__name__
        state = run(body, z, inputs, outputs, sems(1), 2 * flops)
        grads.append(state.grad)
        dq = getattr(state, "dq", None) if step < last - 1 else dq
        if step + 2 < len(held):
            cots.append(passed_along(state.held, "section", -1))
        bit = low_bit(away)
        terms[away - bit].append(swapped(state.weight, "seq", bit))

    common = dict(at=at, up=matrix, halo=halo, own=own)
    outputs = dict(
        dq=dq_shape,
        halo_grads=halo_shape,
        own_part=((rows, PAIR), f32),
        weight_part=((rank, width), f32),
        input_grad=input_shape,
        grad=((block, width), bf16),
    )
    early = run(
        front,
        z,
        common
        | dict(
            cot=cots[last],
            stack=ahead.stack0,
            probs=ahead.probs0,
            dq_in=dq,
            halo_grads_in=state.halo_grads,
            input_sum=state.input_grad,
        )
        | numbered("pending", grads[-BLOCKS:])
        | numbered("term", terms[0][:-1]),
        outputs,
        sems(BLOCKS),
        flops,
    )
    halo_grads = early.halo_grads
    if per_head > 1:
        halo_grads = jnp.sum(halo_grads.reshape(span, HK, per_head, PAIR), axis=2)
        halo_grads = halo_grads.astype(bf16).reshape(span, HK * PAIR)
    backs = []
    stop = span
    for distance, count in pieces:
        backs.append(passed_along(halo_grads[stop - count : stop], "seq", -distance))
        stop -= count

    outputs = dict(grad=((block, width), bf16), dscores=((window, stack_rows), bf16))
    outputs |= numbered("share", [((rank // packs, width), bf16)] * packs)
    late = run(
        back,
        z,
        common
        | dict(cot=cots[last + 1], probs=ahead.probs1, weight_part=early.weight_part)
        | numbered("term", terms[0][-1:]),
        outputs,
        dict(total=pltpu.VMEM((rank, width), bf16)),
        flops,
    )
    shares = listed(late, "share")
    shares[1:] = [passed_along(shares[away], "dp", away) for away in range(1, packs)]

    merged = per_head == 1 and len(pieces) == 1
    outputs = dict(dq=dq_shape, own_grads=own_shape, input_grad=((rank, rows), bf16))
    inputs = dict(
        at=at,
        up=matrix,
        cot=cots[last + 1],
        stack=ahead.stack1,
        probs=ahead.probs1,
        dscores=late.dscores,
        own_part=early.own_part,
        input_sum=early.input_grad,
        dq_in=early.dq,
        own_grads_in=state.own_grads,
        share_in=shares[0],
    )
    outputs.update(share=(shares[0].shape, bf16))
    if merged:
        inputs.update(halo_back=backs[0])
        outputs.update(pair_grads=((rows, HK * PAIR), bf16))
    final = run(
        finish,
        z,
        inputs | numbered("pending", [early.grad, late.grad]),
        outputs,
        sems(BLOCKS),
        flops,
    )
    weight_share = final.share.astype(f32)
    for share in shares[1:]:
        weight_share += share.astype(f32)
    if merged:
        pair_grads = final.pair_grads
    else:
        own_grads = jnp.sum(final.own_grads.reshape(rows, HK, per_head, PAIR), axis=2)
        own_grads = own_grads.reshape(rows, HK * PAIR)
        for rows_back in backs:
            low = rows - rows_back.shape[0]
            own_grads = own_grads.at[low:].add(rows_back.astype(f32))
        pair_grads = own_grads.astype(bf16)

    return (
        final.dq[None, None],
        pair_grads[None, None],
        final.input_grad.T[None, None],
        weight_share[None],
    )


def solution(mesh):
    placed = (
        P("section", "dp", "seq", None),
        P("section", "dp", "seq", None),
        P("section", "dp", "seq", None),
        P("section", None, "seq"),
        P("section", "dp", "seq", None),
        P("section", "dp", None),
    )
    return jax.shard_map(
        per_device,
        mesh=mesh,
        in_specs=placed,
        out_specs=(
            P("section", "dp", "seq", None),
            P("section", "dp", "seq", None),
            P("section", "dp", "seq", None),
            P("section", "dp", "seq"),
        ),
        check_vma=False,
    )
```

```python
import functools
import math
from types import SimpleNamespace

import jax
import jax.numpy as jnp
from jax import lax
from jax.experimental import pallas as pl
from jax.experimental.pallas import tpu as pltpu
from jax.sharding import PartitionSpec as P

QUERY_HEADS = 32
HK = 4
HEAD_SIZE = 128
PAIR = 2 * HEAD_SIZE
SCALE = 1.0 / math.sqrt(HEAD_SIZE)
SPAN_PARTS = 8
BLOCKS = 2
COPIES = 4
LIMIT = 16 * 1024 * 1024
IN = "_in"
IN_HBM = ("upstream", "pairs", "matrix", "dq", "dq" + IN)
ANYWHERE = ("held", "held" + IN, "after")
VMEM = pl.BlockSpec(memory_space=pltpu.VMEM)
HBM = pl.BlockSpec(memory_space=pltpu.HBM)
ANY = pl.BlockSpec(memory_space=pl.ANY)


def passed_along(value, axis, steps):
    count = lax.axis_size(axis)
    pairs = [(source, (source + steps) % count) for source in range(count)]
    return lax.ppermute(value, axis, pairs)


def swapped(value, axis, bit):
    pairs = [(source, source ^ bit) for source in range(lax.axis_size(axis))]
    return lax.ppermute(value, axis, pairs)


def dot(left, right, left_dim, right_dim):
    return lax.dot_general(
        left, right, (((left_dim,), (right_dim,)), ((), ())), preferred_element_type=jnp.float32
    )


def low_bit(number):
    return number & -number


def numbered(name, arrays):
    return {name + str(index): array for index, array in enumerate(arrays)}


def listed(refs, name):
    found = []
    while hasattr(refs, name + str(len(found))):
        found.append(getattr(refs, name + str(len(found))))
    return found


def spec_of(name):
    return HBM if name in IN_HBM else ANY if name in ANYWHERE else VMEM


def run(body, sizes, inputs, outputs, scratch, flops=0):
    names = list(inputs) + list(outputs) + list(scratch)

    def kernel(*refs):
        body(sizes, SimpleNamespace(**dict(zip(names, refs))))

    operands = [
        pltpu.with_memory_space_constraint(array, pltpu.HBM) if name in IN_HBM[:3] else array
        for name, array in inputs.items()
    ]
    places = list(inputs)
    aliases = {
        places.index(name + IN): index
        for index, name in enumerate(outputs)
        if name + IN in inputs
    }
    results = pl.pallas_call(
        kernel,
        in_specs=[spec_of(name) for name in inputs],
        out_specs=[spec_of(name) for name in outputs],
        out_shape=[jax.ShapeDtypeStruct(shape, kind) for shape, kind in outputs.values()],
        scratch_shapes=list(scratch.values()),
        input_output_aliases=aliases,
        compiler_params=pltpu.CompilerParams(vmem_limit_bytes=LIMIT),
        cost_estimate=pl.CostEstimate(
            flops=flops // 1024, bytes_accessed=1024, transcendentals=flops // 1024
        ),
        name=body.__name__,
    )(*operands)
    return SimpleNamespace(**dict(zip(outputs, results)))


def copy_rows(source, target, sems, copies, parts=1):
    rows = source.shape[0] // parts
    for part in range(parts):
        piece = pl.ds(part * rows, rows)
        copies.append(
            pltpu.make_async_copy(source.at[piece], target.at[piece], sems.at[len(copies)])
        )
        copies[-1].start()


def chunk_at(step, chunks):
    return lax.axis_index("seq") ^ (chunks - 1 - step)


def chunk_columns(z, step):
    return pl.ds(pl.multiple_of(chunk_at(step, z.chunks) * z.width, HEAD_SIZE), z.width)


def pair_columns(z, step):
    return pl.ds(pl.multiple_of(chunk_at(step, z.chunks) * PAIR, HEAD_SIZE), PAIR)


def split_first(z, refs):
    copies = []
    source = refs.upstream.at[:, chunk_columns(z, 0)]
    copy_rows(source, refs.piece, refs.sems, copies, COPIES)
    for copy in copies:
        copy.wait()


def split_second(z, refs):
    copies = []
    source = refs.upstream.at[:, chunk_columns(z, 1)]
    copy_rows(source, refs.piece, refs.sems, copies, COPIES)
    copy_rows(refs.matrix, refs.matrix_copy, refs.sems, copies, COPIES)
    copy_rows(refs.pairs, refs.pairs_copy, refs.sems, copies, COPIES)
    for copy in copies:
        copy.wait()


def split_rest(z, refs):
    copies = []
    pieces = listed(refs, "piece")
    for step, piece in zip(range(2, z.chunks - 1), pieces):
        copy_rows(refs.upstream.at[:, chunk_columns(z, step)], piece, refs.sems, copies, COPIES)
    for index, piece in enumerate(pieces[-BLOCKS:]):
        rows = pl.ds(index * z.block, z.block)
        source = refs.upstream.at[rows, chunk_columns(z, z.chunks - 1)]
        copy_rows(source, piece, refs.sems, copies, COPIES)
    for copy in copies:
        copy.wait()


def stacked(array, rows):
    heads = array.shape[1] // HEAD_SIZE
    parts = [array[rows, head * HEAD_SIZE : (head + 1) * HEAD_SIZE] for head in range(heads)]
    return jnp.concatenate(parts, axis=0)


def seen_rows(z, refs, step, second):
    per_head = z.chunks // HK
    chunk = chunk_at(step, z.chunks)
    place = lax.div(chunk, per_head) if per_head > 1 else chunk
    start = pl.multiple_of(place * PAIR + second * HEAD_SIZE, HEAD_SIZE)
    columns = pl.ds(start, HEAD_SIZE)
    return jnp.concatenate([refs.halo[: z.span, columns], refs.own[:, columns]], axis=0)


def windowed(z, array, index):
    return array[index * z.block : index * z.block + z.window]


def softmax_blocks(z, refs, step, matrix, keys):
    queries = refs.fq[:, chunk_columns(z, step)].astype(jnp.float32)
    queries = (queries + dot(refs.at[...], matrix, 0, 0)).astype(jnp.bfloat16)
    stacks, probs = [], []
    for index in range(BLOCKS):
        stack = stacked(queries, slice(index * z.block, (index + 1) * z.block))
        hidden = refs.bias[index * z.window : (index + 1) * z.window]
        scores = dot(windowed(z, keys, index), stack, 1, 1) * SCALE
        scores += jnp.concatenate([hidden] * (stack.shape[0] // hidden.shape[1]), axis=1)
        shifted = jnp.exp(scores - jnp.max(scores, axis=0, keepdims=True))
        stacks.append(stack)
        probs.append(shifted * (1.0 / jnp.sum(shifted, axis=0, keepdims=True)))
    return stacks, probs


def score_grads(z, index, probs, keys, values, cot_stack):
    dprobs = dot(windowed(z, values, index), cot_stack, 1, 1)
    deltas = jnp.sum(probs * dprobs, axis=0, keepdims=True)
    dscores = (probs * (dprobs - deltas)).astype(jnp.bfloat16)
    return dscores, (dot(dscores, windowed(z, keys, index), 0, 0) * SCALE).astype(jnp.bfloat16)


def unstack(z, grad_stack, target, start):
    for head in range(grad_stack.shape[0] // z.block):
        columns = slice(head * HEAD_SIZE, (head + 1) * HEAD_SIZE)
        target[start : start + z.block, columns] = grad_stack[head * z.block : (head + 1) * z.block]


def pair_terms(z, index, dscores, probs, query_stack, cot_stack):
    key_term = dot(dscores, query_stack, 1, 0) * SCALE
    value_term = dot(probs.astype(jnp.bfloat16), cot_stack, 1, 0)
    term = jnp.concatenate([key_term, value_term], axis=1)
    start = index * z.block
    rest = z.span + z.rows - z.window - start
    if start > 0:
        term = jnp.concatenate([jnp.zeros((start, PAIR), jnp.float32), term], axis=0)
    if rest > 0:
        term = jnp.concatenate([term, jnp.zeros((rest, PAIR), jnp.float32)], axis=0)
    return term


def padded(z, grad, index):
    blank = jnp.zeros((z.block, grad.shape[1]), grad.dtype)
    return jnp.concatenate([grad if place == index else blank for place in range(BLOCKS)], axis=0)


def forward(z, refs):
    step = z.chunks - 1
    keys = seen_rows(z, refs, step, 0)
    stacks, probs = softmax_blocks(z, refs, step, refs.up[...], keys)
    for index in range(BLOCKS):
        listed(refs, "stack")[index][...] = stacks[index]
        listed(refs, "probs")[index][...] = probs[index]


def whole(step, z, refs):
    copies = []
    if hasattr(refs, "pending"):
        copy_rows(refs.pending, refs.dq.at[:, chunk_columns(z, step - 1)], refs.sems, copies)
    matrix = refs.up[...]
    keys, values = seen_rows(z, refs, step, 0), seen_rows(z, refs, step, 1)
    stacks, probs = softmax_blocks(z, refs, step, matrix, keys)
    pair_total = 0.0
    for index in range(BLOCKS):
        start = index * z.block
        cot_stack = stacked(refs.cot, slice(start, start + z.block))
        dscores, grad_stack = score_grads(z, index, probs[index], keys, values, cot_stack)
        unstack(z, grad_stack, refs.grad, start)
        pair_total += pair_terms(z, index, dscores, probs[index], stacks[index], cot_stack)
    grad = refs.grad[...]
    weight = dot(refs.at[...], grad, 1, 0)
    for term in listed(refs, "term"):
        weight += term[...].astype(jnp.float32)
    refs.weight[...] = weight.astype(jnp.bfloat16)
    refs.halo_part[...] = pair_total[: z.span].astype(refs.halo_part.dtype)
    refs.own_part[...] = pair_total[z.span :]
    input_grad = dot(matrix, grad, 1, 1)
    if step > 0:
        input_grad += refs.input_sum[...]
    refs.input_grad[...] = input_grad
    for copy in copies:
        copy.wait()


def front(z, refs):
    copies = []
    step = z.chunks - 1
    for place, grad in enumerate(listed(refs, "pending")):
        target = refs.dq.at[:, chunk_columns(z, step - BLOCKS + place)]
        copy_rows(grad, target, refs.sems, copies)
    keys, values = seen_rows(z, refs, step, 0), seen_rows(z, refs, step, 1)
    probs = refs.probs[...]
    cot_stack = stacked(refs.cot, slice(0, z.block))
    dscores, grad_stack = score_grads(z, 0, probs, keys, values, cot_stack)
    unstack(z, grad_stack, refs.grad, 0)
    pair_total = pair_terms(z, 0, dscores, probs, refs.stack[...], cot_stack)
    kind = refs.halo_grads.dtype
    for place, part in enumerate(listed(refs, "halo_part")):
        refs.halo_grads[:, pair_columns(z, place)] = part[...]
    refs.halo_grads[:, pair_columns(z, step)] = pair_total[: z.span].astype(kind)
    refs.own_part[...] = pair_total[z.span :]
    grad = padded(z, refs.grad[...], 0)
    weight = dot(refs.at[...], grad, 1, 0)
    for term in listed(refs, "term"):
        weight += term[...].astype(jnp.float32)
    refs.weight_part[...] = weight
    refs.input_grad[...] = refs.input_sum[...] + dot(refs.up[...], grad, 1, 1)
    for copy in copies:
        copy.wait()


def back(z, refs):
    step = z.chunks - 1
    keys, values = seen_rows(z, refs, step, 0), seen_rows(z, refs, step, 1)
    cot_stack = stacked(refs.cot, slice(0, z.block))
    dscores, grad_stack = score_grads(z, 1, refs.probs[...], keys, values, cot_stack)
    refs.dscores[...] = dscores
    unstack(z, grad_stack, refs.grad, 0)
    weight = refs.weight_part[...] + dot(refs.at[...], padded(z, refs.grad[...], 1), 1, 0)
    for term in listed(refs, "term"):
        weight += term[...].astype(jnp.float32)
    refs.total[...] = weight.astype(jnp.bfloat16)
    shares = listed(refs, "share")
    rows = z.rank // len(shares)
    for away, share in enumerate(shares):
        target = lax.rem(lax.axis_index("dp") + away, len(shares))
        share[...] = refs.total[pl.ds(pl.multiple_of(target * rows, rows), rows)]


def finish(z, refs):
    copies = []
    step = z.chunks - 1
    for index, grad in enumerate(listed(refs, "pending")):
        target = refs.dq.at[pl.ds(index * z.block, z.block), chunk_columns(z, step)]
        copy_rows(grad, target, refs.sems, copies)
    cot_stack = stacked(refs.cot, slice(0, z.block))
    pair_total = pair_terms(z, 1, refs.dscores[...], refs.probs[...], refs.stack[...], cot_stack)
    parts = [part[...] for part in listed(refs, "own_part")]
    parts[step] += pair_total[z.span :]
    low = z.rows - z.span
    for place, part in enumerate(parts):
        columns = pair_columns(z, place)
        if hasattr(refs, "halo_back"):
            refs.pair_grads[:low, columns] = part[:low].astype(jnp.bfloat16)
            part = part[low:] + refs.halo_back[:, columns].astype(jnp.float32)
            refs.pair_grads[low:, columns] = part.astype(jnp.bfloat16)
        else:
            refs.own_grads[:, columns] = part
    refs.share_out[...] = refs.share[...]
    grad = padded(z, refs.pending1[...], 1)
    input_grad = refs.input_sum[...] + dot(refs.up[...], grad, 1, 1)
    refs.input_grad[...] = input_grad.astype(jnp.bfloat16)
    for copy in copies:
        copy.wait()


def per_device(
    frozen_queries, key_value_pairs, adapter_input, adapter_up_matrix, upstream, document_index
):
    bf16, f32 = jnp.bfloat16, jnp.float32
    chunks = lax.axis_size("seq")
    packs = lax.axis_size("dp")
    place = lax.axis_index("seq")
    rows = frozen_queries.shape[2]
    columns = QUERY_HEADS * HEAD_SIZE
    block = rows // BLOCKS
    span = document_index.shape[2] // SPAN_PARTS
    window = span + block
    width = columns // chunks
    rank = adapter_input.shape[3]
    stack_rows = width // HEAD_SIZE * block
    per_head = chunks // HK
    last = chunks - 1
    z = SimpleNamespace(
        chunks=chunks, rows=rows, block=block, span=span, window=window, width=width, rank=rank
    )
    flops = 10 * stack_rows * window * HEAD_SIZE

    pieces = []
    left = span
    while left > 0:
        pieces.append((len(pieces) + 1, min(rows, left)))
        left -= rows

    own = key_value_pairs[0, 0]
    matrix = adapter_up_matrix[0]
    cotangents = upstream[0, 0]

    def sems(count):
        return dict(sems=pltpu.SemaphoreType.DMA((count,)))

    piece = ((rows, width), bf16)
    first = run(split_first, z, dict(upstream=cotangents), dict(piece=piece), sems(COPIES)).piece
    cots = [passed_along(first, "section", -1)]
    outputs = dict(
        piece=piece, matrix_copy=((rank, width), bf16), pairs_copy=(own.shape, bf16)
    )
    second = run(
        split_second,
        z,
        dict(upstream=cotangents, pairs=own, matrix=matrix, after=first),
        outputs,
        sems(COPIES * len(outputs)),
    )
    cots.append(passed_along(second.piece, "section", -1))
    own, matrix = second.pairs_copy, second.matrix_copy
    outputs = numbered("piece", [piece] * (last - 2) + [((block, width), bf16)] * BLOCKS)
    rest = run(
        split_rest,
        z,
        dict(upstream=cotangents, after=second.piece),
        outputs,
        sems(COPIES * len(outputs)),
    )
    held = listed(rest, "piece")
    cots.append(passed_along(held[0], "section", -1))
    halo = [passed_along(own[rows - count :], "seq", distance) for distance, count in pieces]
    halo = jnp.concatenate(halo[::-1], axis=0)
    ups = {0: matrix}
    for away in sorted(range(1, chunks), key=low_bit, reverse=True):
        bit = low_bit(away)
        ups[away] = swapped(ups[away - bit], "seq", bit)

    numbers = jnp.concatenate([jnp.full((span,), -1, jnp.int32), document_index[0, 0]])
    numbers = lax.dynamic_slice_in_dim(numbers, place * rows, span + rows, 0)
    reach = jnp.arange(window, dtype=jnp.int32)[:, None] <= (
        jnp.arange(block, dtype=jnp.int32)[None, :] + span
    )
    bias = []
    for start in range(0, rows, block):
        seen = numbers[start : start + window, None]
        same = seen == numbers[None, start + span : start + span + block]
        bias.append(jnp.where(same & reach, 0.0, -jnp.inf))
    bias = jnp.concatenate(bias, axis=0).astype(f32)
    bias = jnp.concatenate([bias, bias], axis=1)
    fq = frozen_queries[0, 0]
    at = adapter_input[0, 0].T

    outputs = numbered("stack", [((stack_rows, HEAD_SIZE), bf16)] * BLOCKS)
    outputs |= numbered("probs", [((window, stack_rows), f32)] * BLOCKS)
    outputs.update(held=(held[1].shape, bf16))
    inputs = dict(fq=fq, at=at, up=matrix, halo=halo, own=own, bias=bias, held_in=held[1])
    ahead = run(forward, z, inputs, outputs, {}, flops)
    cots.append(passed_along(ahead.held, "section", -1))

    halo_type = bf16 if per_head == 1 else f32
    halo_part, own_part = ((span, PAIR), halo_type), ((rows, PAIR), f32)
    dq_shape = ((rows, columns), bf16)
    input_shape = ((rank, rows), f32)
    terms = {away: [] for away in range(chunks)}
    grads, halo_parts, own_parts = [], [], []
    state = None
    for step in range(last):
        away = last - step
        inputs = dict(fq=fq, at=at, halo=halo, own=own, bias=bias, cot=cots[step], up=ups[away])
        inputs |= numbered("term", terms[away])
        outputs = dict(
            halo_part=halo_part,
            own_part=own_part,
            input_grad=input_shape,
            grad=piece,
            weight=((rank, width), bf16),
        )
        if step > 0:
            inputs.update(input_sum=state.input_grad)
        else:
            inputs.update(after=ahead.stack0)
        if 0 < step < last - 1:
            inputs.update(pending=grads[-1])
            outputs.update(dq=dq_shape)
            if step > 1:
                inputs.update(dq_in=dq)
        if step + 2 < len(held):
            inputs.update(held_in=held[step + 2])
            outputs.update(held=(held[step + 2].shape, bf16))
        body = functools.partial(whole, step)
        body.__name__ = whole.__name__
        state = run(body, z, inputs, outputs, sems(1), 2 * flops)
        grads.append(state.grad)
        halo_parts.append(state.halo_part)
        own_parts.append(state.own_part)
        dq = getattr(state, "dq", None) if step < last - 1 else dq
        if step + 2 < len(held):
            cots.append(passed_along(state.held, "section", -1))
        bit = low_bit(away)
        terms[away - bit].append(swapped(state.weight, "seq", bit))

    common = dict(at=at, up=matrix, halo=halo, own=own)
    outputs = dict(
        dq=dq_shape,
        halo_grads=((span, chunks * PAIR), halo_type),
        own_part=own_part,
        weight_part=((rank, width), f32),
        input_grad=input_shape,
        grad=((block, width), bf16),
    )
    early = run(
        front,
        z,
        common
        | dict(
            cot=cots[last],
            stack=ahead.stack0,
            probs=ahead.probs0,
            dq_in=dq,
            input_sum=state.input_grad,
        )
        | numbered("halo_part", halo_parts)
        | numbered("pending", grads[-BLOCKS:])
        | numbered("term", terms[0][:-1]),
        outputs,
        sems(BLOCKS),
        flops,
    )
    halo_grads = early.halo_grads
    if per_head > 1:
        halo_grads = jnp.sum(halo_grads.reshape(span, HK, per_head, PAIR), axis=2)
        halo_grads = halo_grads.astype(bf16).reshape(span, HK * PAIR)
    backs = []
    stop = span
    for distance, count in pieces:
        backs.append(passed_along(halo_grads[stop - count : stop], "seq", -distance))
        stop -= count

    outputs = dict(grad=((block, width), bf16), dscores=((window, stack_rows), bf16))
    outputs |= numbered("share", [((rank // packs, width), bf16)] * packs)
    late = run(
        back,
        z,
        common
        | dict(cot=cots[last + 1], probs=ahead.probs1, weight_part=early.weight_part)
        | numbered("term", terms[0][-1:]),
        outputs,
        dict(total=pltpu.VMEM((rank, width), bf16)),
        flops,
    )
    shares = listed(late, "share")
    shares[1:] = [passed_along(shares[away], "dp", away) for away in range(1, packs)]

    merged = per_head == 1 and len(pieces) == 1
    outputs = dict(dq=dq_shape, input_grad=((rank, rows), bf16))
    outputs.update(share_out=((rank // packs, width), bf16))
    inputs = dict(
        at=at,
        up=matrix,
        cot=cots[last + 1],
        stack=ahead.stack1,
        probs=ahead.probs1,
        dscores=late.dscores,
        input_sum=early.input_grad,
        dq_in=early.dq,
        share=shares[0],
    )
    inputs |= numbered("own_part", own_parts + [early.own_part])
    if merged:
        inputs.update(halo_back=backs[0])
        outputs.update(pair_grads=((rows, HK * PAIR), bf16))
    else:
        outputs.update(own_grads=((rows, chunks * PAIR), f32))
    final = run(
        finish,
        z,
        inputs | numbered("pending", [early.grad, late.grad]),
        outputs,
        sems(BLOCKS),
        flops,
    )
    weight_share = final.share_out.astype(f32)
    for share in shares[1:]:
        weight_share += share.astype(f32)
    if merged:
        pair_grads = final.pair_grads
    else:
        own_grads = jnp.sum(final.own_grads.reshape(rows, HK, per_head, PAIR), axis=2)
        own_grads = own_grads.reshape(rows, HK * PAIR)
        for rows_back in backs:
            low = rows - rows_back.shape[0]
            own_grads = own_grads.at[low:].add(rows_back.astype(f32))
        pair_grads = own_grads.astype(bf16)

    return (
        final.dq[None, None],
        pair_grads[None, None],
        final.input_grad.T[None, None],
        weight_share[None],
    )


def solution(mesh):
    placed = (
        P("section", "dp", "seq", None),
        P("section", "dp", "seq", None),
        P("section", "dp", "seq", None),
        P("section", None, "seq"),
        P("section", "dp", "seq", None),
        P("section", "dp", None),
    )
    return jax.shard_map(
        per_device,
        mesh=mesh,
        in_specs=placed,
        out_specs=(
            P("section", "dp", "seq", None),
            P("section", "dp", "seq", None),
            P("section", "dp", "seq", None),
            P("section", "dp", "seq"),
        ),
        check_vma=False,
    )
```

```python
import functools
import math
from types import SimpleNamespace

import jax
import jax.numpy as jnp
from jax import lax
from jax.experimental import pallas as pl
from jax.experimental.pallas import tpu as pltpu
from jax.sharding import PartitionSpec as P

QUERY_HEADS = 32
HK = 4
HEAD_SIZE = 128
PAIR = 2 * HEAD_SIZE
SCALE = 1.0 / math.sqrt(HEAD_SIZE)
SPAN_PARTS = 8
BLOCKS = 2
COPIES = 4
LIMIT = 16 * 1024 * 1024
IN = "_in"
IN_HBM = ("upstream", "pairs", "matrix", "dq", "dq" + IN)
ANYWHERE = ("held", "held" + IN, "after")
VMEM = pl.BlockSpec(memory_space=pltpu.VMEM)
HBM = pl.BlockSpec(memory_space=pltpu.HBM)
ANY = pl.BlockSpec(memory_space=pl.ANY)


def passed_along(value, axis, steps):
    count = lax.axis_size(axis)
    pairs = [(source, (source + steps) % count) for source in range(count)]
    return lax.ppermute(value, axis, pairs)


def swapped(value, axis, bit):
    pairs = [(source, source ^ bit) for source in range(lax.axis_size(axis))]
    return lax.ppermute(value, axis, pairs)


def dot(left, right, left_dim, right_dim):
    return lax.dot_general(
        left, right, (((left_dim,), (right_dim,)), ((), ())), preferred_element_type=jnp.float32
    )


def low_bit(number):
    return number & -number


def numbered(name, arrays):
    return {name + str(index): array for index, array in enumerate(arrays)}


def listed(refs, name):
    found = []
    while hasattr(refs, name + str(len(found))):
        found.append(getattr(refs, name + str(len(found))))
    return found


def spec_of(name):
    return HBM if name in IN_HBM else ANY if name in ANYWHERE else VMEM


def run(body, sizes, inputs, outputs, scratch, flops=0):
    names = list(inputs) + list(outputs) + list(scratch)

    def kernel(*refs):
        body(sizes, SimpleNamespace(**dict(zip(names, refs))))

    operands = [
        pltpu.with_memory_space_constraint(array, pltpu.HBM) if name in IN_HBM[:3] else array
        for name, array in inputs.items()
    ]
    places = list(inputs)
    aliases = {
        places.index(name + IN): index
        for index, name in enumerate(outputs)
        if name + IN in inputs
    }
    results = pl.pallas_call(
        kernel,
        in_specs=[spec_of(name) for name in inputs],
        out_specs=[spec_of(name) for name in outputs],
        out_shape=[jax.ShapeDtypeStruct(shape, kind) for shape, kind in outputs.values()],
        scratch_shapes=list(scratch.values()),
        input_output_aliases=aliases,
        compiler_params=pltpu.CompilerParams(vmem_limit_bytes=LIMIT),
        cost_estimate=pl.CostEstimate(
            flops=flops // 1024, bytes_accessed=1024, transcendentals=flops // 1024
        ),
        name=body.__name__,
    )(*operands)
    return SimpleNamespace(**dict(zip(outputs, results)))


def copy_rows(source, target, sems, copies, parts=1):
    rows = source.shape[0] // parts
    for part in range(parts):
        piece = pl.ds(part * rows, rows)
        copies.append(
            pltpu.make_async_copy(source.at[piece], target.at[piece], sems.at[len(copies)])
        )
        copies[-1].start()


def chunk_at(step, chunks):
    return lax.axis_index("seq") ^ (chunks - 1 - step)


def chunk_columns(z, step):
    return pl.ds(pl.multiple_of(chunk_at(step, z.chunks) * z.width, HEAD_SIZE), z.width)


def pair_columns(z, step):
    return pl.ds(pl.multiple_of(chunk_at(step, z.chunks) * PAIR, HEAD_SIZE), PAIR)


def split_first(z, refs):
    copies = []
    source = refs.upstream.at[:, chunk_columns(z, 0)]
    copy_rows(source, refs.piece, refs.sems, copies, COPIES)
    for copy in copies:
        copy.wait()


def split_second(z, refs):
    copies = []
    source = refs.upstream.at[:, chunk_columns(z, 1)]
    copy_rows(source, refs.piece, refs.sems, copies, COPIES)
    copy_rows(refs.matrix, refs.matrix_copy, refs.sems, copies, COPIES)
    copy_rows(refs.pairs, refs.pairs_copy, refs.sems, copies, COPIES)
    for copy in copies:
        copy.wait()


def split_rest(z, refs):
    copies = []
    pieces = listed(refs, "piece")
    for step, piece in zip(range(2, z.chunks - 1), pieces):
        copy_rows(refs.upstream.at[:, chunk_columns(z, step)], piece, refs.sems, copies, COPIES)
    for index, piece in enumerate(pieces[-BLOCKS:]):
        rows = pl.ds(index * z.block, z.block)
        source = refs.upstream.at[rows, chunk_columns(z, z.chunks - 1)]
        copy_rows(source, piece, refs.sems, copies, COPIES)
    for copy in copies:
        copy.wait()


def stacked(array, rows):
    heads = array.shape[1] // HEAD_SIZE
    parts = [array[rows, head * HEAD_SIZE : (head + 1) * HEAD_SIZE] for head in range(heads)]
    return jnp.concatenate(parts, axis=0)


def seen_rows(z, refs, step, second):
    per_head = z.chunks // HK
    chunk = chunk_at(step, z.chunks)
    place = lax.div(chunk, per_head) if per_head > 1 else chunk
    start = pl.multiple_of(place * PAIR + second * HEAD_SIZE, HEAD_SIZE)
    columns = pl.ds(start, HEAD_SIZE)
    return jnp.concatenate([refs.halo[: z.span, columns], refs.own[:, columns]], axis=0)


def windowed(z, array, index):
    return array[index * z.block : index * z.block + z.window]


def softmax_blocks(z, refs, step, matrix, keys):
    queries = refs.fq[:, chunk_columns(z, step)].astype(jnp.float32)
    queries = (queries + dot(refs.at[...], matrix, 0, 0)).astype(jnp.bfloat16)
    stacks, probs = [], []
    for index in range(BLOCKS):
        stack = stacked(queries, slice(index * z.block, (index + 1) * z.block))
        hidden = refs.bias[index * z.window : (index + 1) * z.window]
        scores = dot(windowed(z, keys, index), stack, 1, 1) * SCALE
        scores += jnp.concatenate([hidden] * (stack.shape[0] // hidden.shape[1]), axis=1)
        shifted = jnp.exp(scores - jnp.max(scores, axis=0, keepdims=True))
        stacks.append(stack)
        probs.append(shifted * (1.0 / jnp.sum(shifted, axis=0, keepdims=True)))
    return stacks, probs


def score_grads(z, index, probs, keys, values, cot_stack):
    dprobs = dot(windowed(z, values, index), cot_stack, 1, 1)
    deltas = jnp.sum(probs * dprobs, axis=0, keepdims=True)
    dscores = (probs * (dprobs - deltas)).astype(jnp.bfloat16)
    return dscores, (dot(dscores, windowed(z, keys, index), 0, 0) * SCALE).astype(jnp.bfloat16)


def unstack(z, grad_stack, target, start):
    for head in range(grad_stack.shape[0] // z.block):
        columns = slice(head * HEAD_SIZE, (head + 1) * HEAD_SIZE)
        target[start : start + z.block, columns] = grad_stack[head * z.block : (head + 1) * z.block]


def pair_terms(z, index, dscores, probs, query_stack, cot_stack):
    key_term = dot(dscores, query_stack, 1, 0) * SCALE
    value_term = dot(probs.astype(jnp.bfloat16), cot_stack, 1, 0)
    term = jnp.concatenate([key_term, value_term], axis=1)
    start = index * z.block
    rest = z.span + z.rows - z.window - start
    if start > 0:
        term = jnp.concatenate([jnp.zeros((start, PAIR), jnp.float32), term], axis=0)
    if rest > 0:
        term = jnp.concatenate([term, jnp.zeros((rest, PAIR), jnp.float32)], axis=0)
    return term


def padded(z, grad, index):
    blank = jnp.zeros((z.block, grad.shape[1]), grad.dtype)
    return jnp.concatenate([grad if place == index else blank for place in range(BLOCKS)], axis=0)


def forward(z, refs):
    step = z.chunks - 1
    keys = seen_rows(z, refs, step, 0)
    stacks, probs = softmax_blocks(z, refs, step, refs.up[...], keys)
    for index in range(BLOCKS):
        listed(refs, "stack")[index][...] = stacks[index]
        listed(refs, "probs")[index][...] = probs[index]


def whole(step, z, refs):
    copies = []
    if hasattr(refs, "pending"):
        copy_rows(refs.pending, refs.dq.at[:, chunk_columns(z, step - 1)], refs.sems, copies)
    matrix = refs.up[...]
    keys, values = seen_rows(z, refs, step, 0), seen_rows(z, refs, step, 1)
    stacks, probs = softmax_blocks(z, refs, step, matrix, keys)
    pair_total = 0.0
    for index in range(BLOCKS):
        start = index * z.block
        cot_stack = stacked(refs.cot, slice(start, start + z.block))
        dscores, grad_stack = score_grads(z, index, probs[index], keys, values, cot_stack)
        unstack(z, grad_stack, refs.grad, start)
        pair_total += pair_terms(z, index, dscores, probs[index], stacks[index], cot_stack)
    grad = refs.grad[...]
    weight = dot(refs.at[...], grad, 1, 0)
    for term in listed(refs, "term"):
        weight += term[...].astype(jnp.float32)
    refs.weight[...] = weight.astype(jnp.bfloat16)
    refs.halo_part[...] = pair_total[: z.span].astype(refs.halo_part.dtype)
    refs.own_part[...] = pair_total[z.span :]
    input_grad = dot(matrix, grad, 1, 1)
    if step > 0:
        input_grad += refs.input_sum[...]
    refs.input_grad[...] = input_grad
    for copy in copies:
        copy.wait()


def front(z, refs):
    copies = []
    step = z.chunks - 1
    for place, grad in enumerate(listed(refs, "pending")):
        target = refs.dq.at[:, chunk_columns(z, step - BLOCKS + place)]
        copy_rows(grad, target, refs.sems, copies)
    keys, values = seen_rows(z, refs, step, 0), seen_rows(z, refs, step, 1)
    probs = refs.probs[...]
    cot_stack = stacked(refs.cot, slice(0, z.block))
    dscores, grad_stack = score_grads(z, 0, probs, keys, values, cot_stack)
    unstack(z, grad_stack, refs.grad, 0)
    pair_total = pair_terms(z, 0, dscores, probs, refs.stack[...], cot_stack)
    kind = refs.halo_grads.dtype
    for place, part in enumerate(listed(refs, "halo_part")):
        refs.halo_grads[:, pair_columns(z, place)] = part[...]
    refs.halo_grads[:, pair_columns(z, step)] = pair_total[: z.span].astype(kind)
    refs.own_part[...] = pair_total[z.span :]
    grad = padded(z, refs.grad[...], 0)
    weight = dot(refs.at[...], grad, 1, 0)
    for term in listed(refs, "term"):
        weight += term[...].astype(jnp.float32)
    refs.weight_part[...] = weight
    refs.input_grad[...] = refs.input_sum[...] + dot(refs.up[...], grad, 1, 1)
    for copy in copies:
        copy.wait()


def back(z, refs):
    step = z.chunks - 1
    keys, values = seen_rows(z, refs, step, 0), seen_rows(z, refs, step, 1)
    cot_stack = stacked(refs.cot, slice(0, z.block))
    dscores, grad_stack = score_grads(z, 1, refs.probs[...], keys, values, cot_stack)
    refs.dscores[...] = dscores
    unstack(z, grad_stack, refs.grad, 0)
    weight = refs.weight_part[...] + dot(refs.at[...], padded(z, refs.grad[...], 1), 1, 0)
    for term in listed(refs, "term"):
        weight += term[...].astype(jnp.float32)
    refs.total[...] = weight.astype(jnp.bfloat16)
    shares = listed(refs, "share")
    rows = z.rank // len(shares)
    for away, share in enumerate(shares):
        target = lax.axis_index("dp") ^ away
        share[...] = refs.total[pl.ds(pl.multiple_of(target * rows, rows), rows)]


def finish(z, refs):
    copies = []
    step = z.chunks - 1
    for index, grad in enumerate(listed(refs, "pending")):
        target = refs.dq.at[pl.ds(index * z.block, z.block), chunk_columns(z, step)]
        copy_rows(grad, target, refs.sems, copies)
    cot_stack = stacked(refs.cot, slice(0, z.block))
    pair_total = pair_terms(z, 1, refs.dscores[...], refs.probs[...], refs.stack[...], cot_stack)
    parts = [part[...] for part in listed(refs, "own_part")]
    parts[step] += pair_total[z.span :]
    low = z.rows - z.span
    for place, part in enumerate(parts):
        columns = pair_columns(z, place)
        if hasattr(refs, "halo_back"):
            refs.pair_grads[:low, columns] = part[:low].astype(jnp.bfloat16)
            part = part[low:] + refs.halo_back[:, columns].astype(jnp.float32)
            refs.pair_grads[low:, columns] = part.astype(jnp.bfloat16)
        else:
            refs.own_grads[:, columns] = part
    refs.share_out[...] = refs.share[...]
    grad = padded(z, refs.pending1[...], 1)
    input_grad = refs.input_sum[...] + dot(refs.up[...], grad, 1, 1)
    refs.input_grad[...] = input_grad.astype(jnp.bfloat16)
    for copy in copies:
        copy.wait()


def per_device(
    frozen_queries, key_value_pairs, adapter_input, adapter_up_matrix, upstream, document_index
):
    bf16, f32 = jnp.bfloat16, jnp.float32
    chunks = lax.axis_size("seq")
    packs = lax.axis_size("dp")
    place = lax.axis_index("seq")
    rows = frozen_queries.shape[2]
    columns = QUERY_HEADS * HEAD_SIZE
    block = rows // BLOCKS
    span = document_index.shape[2] // SPAN_PARTS
    window = span + block
    width = columns // chunks
    rank = adapter_input.shape[3]
    stack_rows = width // HEAD_SIZE * block
    per_head = chunks // HK
    last = chunks - 1
    z = SimpleNamespace(
        chunks=chunks, rows=rows, block=block, span=span, window=window, width=width, rank=rank
    )
    flops = 10 * stack_rows * window * HEAD_SIZE

    pieces = []
    left = span
    while left > 0:
        pieces.append((len(pieces) + 1, min(rows, left)))
        left -= rows

    own = key_value_pairs[0, 0]
    matrix = adapter_up_matrix[0]
    cotangents = upstream[0, 0]

    def sems(count):
        return dict(sems=pltpu.SemaphoreType.DMA((count,)))

    piece = ((rows, width), bf16)
    first = run(split_first, z, dict(upstream=cotangents), dict(piece=piece), sems(COPIES)).piece
    cots = [passed_along(first, "section", -1)]
    outputs = dict(
        piece=piece, matrix_copy=((rank, width), bf16), pairs_copy=(own.shape, bf16)
    )
    second = run(
        split_second,
        z,
        dict(upstream=cotangents, pairs=own, matrix=matrix, after=first),
        outputs,
        sems(COPIES * len(outputs)),
    )
    cots.append(passed_along(second.piece, "section", -1))
    own, matrix = second.pairs_copy, second.matrix_copy
    outputs = numbered("piece", [piece] * (last - 2) + [((block, width), bf16)] * BLOCKS)
    rest = run(
        split_rest,
        z,
        dict(upstream=cotangents, after=second.piece),
        outputs,
        sems(COPIES * len(outputs)),
    )
    held = listed(rest, "piece")
    cots.append(passed_along(held[0], "section", -1))
    halo = [passed_along(own[rows - count :], "seq", distance) for distance, count in pieces]
    halo = jnp.concatenate(halo[::-1], axis=0)
    ups = {0: matrix}
    for away in sorted(range(1, chunks), key=low_bit, reverse=True):
        bit = low_bit(away)
        ups[away] = swapped(ups[away - bit], "seq", bit)

    numbers = jnp.concatenate([jnp.full((span,), -1, jnp.int32), document_index[0, 0]])
    numbers = lax.dynamic_slice_in_dim(numbers, place * rows, span + rows, 0)
    reach = jnp.arange(window, dtype=jnp.int32)[:, None] <= (
        jnp.arange(block, dtype=jnp.int32)[None, :] + span
    )
    bias = []
    for start in range(0, rows, block):
        seen = numbers[start : start + window, None]
        same = seen == numbers[None, start + span : start + span + block]
        bias.append(jnp.where(same & reach, 0.0, -jnp.inf))
    bias = jnp.concatenate(bias, axis=0).astype(f32)
    bias = jnp.concatenate([bias, bias], axis=1)
    fq = frozen_queries[0, 0]
    at = adapter_input[0, 0].T

    outputs = numbered("stack", [((stack_rows, HEAD_SIZE), bf16)] * BLOCKS)
    outputs |= numbered("probs", [((window, stack_rows), f32)] * BLOCKS)
    outputs.update(held=(held[1].shape, bf16))
    inputs = dict(fq=fq, at=at, up=matrix, halo=halo, own=own, bias=bias, held_in=held[1])
    ahead = run(forward, z, inputs, outputs, {}, flops)
    cots.append(passed_along(ahead.held, "section", -1))

    halo_type = bf16 if per_head == 1 else f32
    halo_part, own_part = ((span, PAIR), halo_type), ((rows, PAIR), f32)
    dq_shape = ((rows, columns), bf16)
    input_shape = ((rank, rows), f32)
    terms = {away: [] for away in range(chunks)}
    grads, halo_parts, own_parts = [], [], []
    state = None
    for step in range(last):
        away = last - step
        inputs = dict(fq=fq, at=at, halo=halo, own=own, bias=bias, cot=cots[step], up=ups[away])
        inputs |= numbered("term", terms[away])
        outputs = dict(
            halo_part=halo_part,
            own_part=own_part,
            input_grad=input_shape,
            grad=piece,
            weight=((rank, width), bf16),
        )
        if step > 0:
            inputs.update(input_sum=state.input_grad)
        else:
            inputs.update(after=ahead.stack0)
        if 0 < step < last - 1:
            inputs.update(pending=grads[-1])
            outputs.update(dq=dq_shape)
            if step > 1:
                inputs.update(dq_in=dq)
        if step + 2 < len(held):
            inputs.update(held_in=held[step + 2])
            outputs.update(held=(held[step + 2].shape, bf16))
        body = functools.partial(whole, step)
        body.__name__ = whole.__name__
        state = run(body, z, inputs, outputs, sems(1), 2 * flops)
        grads.append(state.grad)
        halo_parts.append(state.halo_part)
        own_parts.append(state.own_part)
        dq = getattr(state, "dq", None) if step < last - 1 else dq
        if step + 2 < len(held):
            cots.append(passed_along(state.held, "section", -1))
        bit = low_bit(away)
        terms[away - bit].append(swapped(state.weight, "seq", bit))

    common = dict(at=at, up=matrix, halo=halo, own=own)
    outputs = dict(
        dq=dq_shape,
        halo_grads=((span, chunks * PAIR), halo_type),
        own_part=own_part,
        weight_part=((rank, width), f32),
        input_grad=input_shape,
        grad=((block, width), bf16),
    )
    early = run(
        front,
        z,
        common
        | dict(
            cot=cots[last],
            stack=ahead.stack0,
            probs=ahead.probs0,
            dq_in=dq,
            input_sum=state.input_grad,
        )
        | numbered("halo_part", halo_parts)
        | numbered("pending", grads[-BLOCKS:])
        | numbered("term", terms[0][:-1]),
        outputs,
        sems(BLOCKS),
        flops,
    )
    halo_grads = early.halo_grads
    if per_head > 1:
        halo_grads = jnp.sum(halo_grads.reshape(span, HK, per_head, PAIR), axis=2)
        halo_grads = halo_grads.astype(bf16).reshape(span, HK * PAIR)
    backs = []
    stop = span
    for distance, count in pieces:
        backs.append(passed_along(halo_grads[stop - count : stop], "seq", -distance))
        stop -= count

    outputs = dict(grad=((block, width), bf16), dscores=((window, stack_rows), bf16))
    assert packs == 4
    outputs |= numbered("share", [((rank // packs, width), bf16)] * packs)
    late = run(
        back,
        z,
        common
        | dict(cot=cots[last + 1], probs=ahead.probs1, weight_part=early.weight_part)
        | numbered("term", terms[0][-1:]),
        outputs,
        dict(total=pltpu.VMEM((rank, width), bf16)),
        flops,
    )
    shares = listed(late, "share")
    for away in (2, 3, 1):
        shares[away] = swapped(shares[away], "dp", away)

    merged = per_head == 1 and len(pieces) == 1
    outputs = dict(dq=dq_shape, input_grad=((rank, rows), bf16))
    outputs.update(share_out=((rank // packs, width), bf16))
    inputs = dict(
        at=at,
        up=matrix,
        cot=cots[last + 1],
        stack=ahead.stack1,
        probs=ahead.probs1,
        dscores=late.dscores,
        input_sum=early.input_grad,
        dq_in=early.dq,
        share=shares[0],
    )
    inputs |= numbered("own_part", own_parts + [early.own_part])
    if merged:
        inputs.update(halo_back=backs[0])
        outputs.update(pair_grads=((rows, HK * PAIR), bf16))
    else:
        outputs.update(own_grads=((rows, chunks * PAIR), f32))
    final = run(
        finish,
        z,
        inputs | numbered("pending", [early.grad, late.grad]),
        outputs,
        sems(BLOCKS),
        flops,
    )
    weight_share = final.share_out.astype(f32)
    for share in shares[1:]:
        weight_share += share.astype(f32)
    if merged:
        pair_grads = final.pair_grads
    else:
        own_grads = jnp.sum(final.own_grads.reshape(rows, HK, per_head, PAIR), axis=2)
        own_grads = own_grads.reshape(rows, HK * PAIR)
        for rows_back in backs:
            low = rows - rows_back.shape[0]
            own_grads = own_grads.at[low:].add(rows_back.astype(f32))
        pair_grads = own_grads.astype(bf16)

    return (
        final.dq[None, None],
        pair_grads[None, None],
        final.input_grad.T[None, None],
        weight_share[None],
    )


def solution(mesh):
    placed = (
        P("section", "dp", "seq", None),
        P("section", "dp", "seq", None),
        P("section", "dp", "seq", None),
        P("section", None, "seq"),
        P("section", "dp", "seq", None),
        P("section", "dp", None),
    )
    return jax.shard_map(
        per_device,
        mesh=mesh,
        in_specs=placed,
        out_specs=(
            P("section", "dp", "seq", None),
            P("section", "dp", "seq", None),
            P("section", "dp", "seq", None),
            P("section", "dp", "seq"),
        ),
        check_vma=False,
    )
```

```python
import functools
import math
from types import SimpleNamespace

import jax
import jax.numpy as jnp
from jax import lax
from jax.experimental import pallas as pl
from jax.experimental.pallas import tpu as pltpu
from jax.sharding import PartitionSpec as P

QUERY_HEADS = 32
HK = 4
HEAD_SIZE = 128
PAIR = 2 * HEAD_SIZE
SCALE = 1.0 / math.sqrt(HEAD_SIZE)
SPAN_PARTS = 8
BLOCKS = 2
COPIES = 4
LIMIT = 16 * 1024 * 1024
IN = "_in"
IN_HBM = ("upstream", "pairs", "matrix", "dq", "dq" + IN)
ANYWHERE = ("held", "held" + IN, "after")
VMEM = pl.BlockSpec(memory_space=pltpu.VMEM)
HBM = pl.BlockSpec(memory_space=pltpu.HBM)
ANY = pl.BlockSpec(memory_space=pl.ANY)


def passed_along(value, axis, steps):
    count = lax.axis_size(axis)
    pairs = [(source, (source + steps) % count) for source in range(count)]
    return lax.ppermute(value, axis, pairs)


def shifted(value, axis, steps):
    count = lax.axis_size(axis)
    pairs = [(source, source + steps) for source in range(count) if 0 <= source + steps < count]
    return lax.ppermute(value, axis, pairs)


def swapped(value, axis, bit):
    pairs = [(source, source ^ bit) for source in range(lax.axis_size(axis))]
    return lax.ppermute(value, axis, pairs)


def dot(left, right, left_dim, right_dim):
    return lax.dot_general(
        left, right, (((left_dim,), (right_dim,)), ((), ())), preferred_element_type=jnp.float32
    )


def low_bit(number):
    return number & -number


def numbered(name, arrays):
    return {name + str(index): array for index, array in enumerate(arrays)}


def listed(refs, name):
    found = []
    while hasattr(refs, name + str(len(found))):
        found.append(getattr(refs, name + str(len(found))))
    return found


def spec_of(name):
    return HBM if name in IN_HBM else ANY if name in ANYWHERE else VMEM


def run(body, sizes, inputs, outputs, scratch, flops=0):
    names = list(inputs) + list(outputs) + list(scratch)

    def kernel(*refs):
        body(sizes, SimpleNamespace(**dict(zip(names, refs))))

    operands = [
        pltpu.with_memory_space_constraint(array, pltpu.HBM) if name in IN_HBM[:3] else array
        for name, array in inputs.items()
    ]
    places = list(inputs)
    aliases = {
        places.index(name + IN): index
        for index, name in enumerate(outputs)
        if name + IN in inputs
    }
    results = pl.pallas_call(
        kernel,
        in_specs=[spec_of(name) for name in inputs],
        out_specs=[spec_of(name) for name in outputs],
        out_shape=[jax.ShapeDtypeStruct(shape, kind) for shape, kind in outputs.values()],
        scratch_shapes=list(scratch.values()),
        input_output_aliases=aliases,
        compiler_params=pltpu.CompilerParams(vmem_limit_bytes=LIMIT),
        cost_estimate=pl.CostEstimate(
            flops=flops // 1024, bytes_accessed=1024, transcendentals=flops // 1024
        ),
        name=body.__name__,
    )(*operands)
    return SimpleNamespace(**dict(zip(outputs, results)))


def copy_rows(source, target, sems, copies, parts=1):
    rows = source.shape[0] // parts
    for part in range(parts):
        piece = pl.ds(part * rows, rows)
        copies.append(
            pltpu.make_async_copy(source.at[piece], target.at[piece], sems.at[len(copies)])
        )
        copies[-1].start()


def chunk_at(step, chunks):
    return lax.axis_index("seq") ^ (chunks - 1 - step)


def chunk_columns(z, step):
    return pl.ds(pl.multiple_of(chunk_at(step, z.chunks) * z.width, HEAD_SIZE), z.width)


def pair_columns(z, step):
    return pl.ds(pl.multiple_of(chunk_at(step, z.chunks) * PAIR, HEAD_SIZE), PAIR)


def split_first(z, refs):
    copies = []
    source = refs.upstream.at[:, chunk_columns(z, 0)]
    copy_rows(source, refs.piece, refs.sems, copies, COPIES)
    for copy in copies:
        copy.wait()


def split_second(z, refs):
    copies = []
    source = refs.upstream.at[:, chunk_columns(z, 1)]
    copy_rows(source, refs.piece, refs.sems, copies, COPIES)
    copy_rows(refs.matrix, refs.matrix_copy, refs.sems, copies, COPIES)
    copy_rows(refs.pairs, refs.pairs_copy, refs.sems, copies, COPIES)
    for copy in copies:
        copy.wait()


def split_rest(z, refs):
    copies = []
    pieces = listed(refs, "piece")
    for step, piece in zip(range(2, z.chunks - 1), pieces):
        copy_rows(refs.upstream.at[:, chunk_columns(z, step)], piece, refs.sems, copies, COPIES)
    for index, piece in enumerate(pieces[-BLOCKS:]):
        rows = pl.ds(index * z.block, z.block)
        source = refs.upstream.at[rows, chunk_columns(z, z.chunks - 1)]
        copy_rows(source, piece, refs.sems, copies, COPIES)
    for copy in copies:
        copy.wait()


def stacked(array, rows):
    heads = array.shape[1] // HEAD_SIZE
    parts = [array[rows, head * HEAD_SIZE : (head + 1) * HEAD_SIZE] for head in range(heads)]
    return jnp.concatenate(parts, axis=0)


def seen_rows(z, refs, step, second):
    per_head = z.chunks // HK
    chunk = chunk_at(step, z.chunks)
    place = lax.div(chunk, per_head) if per_head > 1 else chunk
    start = pl.multiple_of(place * PAIR + second * HEAD_SIZE, HEAD_SIZE)
    columns = pl.ds(start, HEAD_SIZE)
    return jnp.concatenate([refs.halo[: z.span, columns], refs.own[:, columns]], axis=0)


def windowed(z, array, index):
    return array[index * z.block : index * z.block + z.window]


def softmax_blocks(z, refs, step, matrix, keys):
    queries = refs.fq[:, chunk_columns(z, step)].astype(jnp.float32)
    queries = (queries + dot(refs.at[...], matrix, 0, 0)).astype(jnp.bfloat16)
    stacks, probs = [], []
    for index in range(BLOCKS):
        stack = stacked(queries, slice(index * z.block, (index + 1) * z.block))
        hidden = refs.bias[index * z.window : (index + 1) * z.window]
        scores = dot(windowed(z, keys, index), stack, 1, 1) * SCALE
        scores += jnp.concatenate([hidden] * (stack.shape[0] // hidden.shape[1]), axis=1)
        shifted = jnp.exp(scores - jnp.max(scores, axis=0, keepdims=True))
        stacks.append(stack)
        probs.append(shifted * (1.0 / jnp.sum(shifted, axis=0, keepdims=True)))
    return stacks, probs


def score_grads(z, index, probs, keys, values, cot_stack):
    dprobs = dot(windowed(z, values, index), cot_stack, 1, 1)
    deltas = jnp.sum(probs * dprobs, axis=0, keepdims=True)
    dscores = (probs * (dprobs - deltas)).astype(jnp.bfloat16)
    return dscores, (dot(dscores, windowed(z, keys, index), 0, 0) * SCALE).astype(jnp.bfloat16)


def unstack(z, grad_stack, target, start):
    for head in range(grad_stack.shape[0] // z.block):
        columns = slice(head * HEAD_SIZE, (head + 1) * HEAD_SIZE)
        target[start : start + z.block, columns] = grad_stack[head * z.block : (head + 1) * z.block]


def pair_terms(z, index, dscores, probs, query_stack, cot_stack):
    key_term = dot(dscores, query_stack, 1, 0) * SCALE
    value_term = dot(probs.astype(jnp.bfloat16), cot_stack, 1, 0)
    term = jnp.concatenate([key_term, value_term], axis=1)
    start = index * z.block
    rest = z.span + z.rows - z.window - start
    if start > 0:
        term = jnp.concatenate([jnp.zeros((start, PAIR), jnp.float32), term], axis=0)
    if rest > 0:
        term = jnp.concatenate([term, jnp.zeros((rest, PAIR), jnp.float32)], axis=0)
    return term


def padded(z, grad, index):
    blank = jnp.zeros((z.block, grad.shape[1]), grad.dtype)
    return jnp.concatenate([grad if place == index else blank for place in range(BLOCKS)], axis=0)


def forward(z, refs):
    step = z.chunks - 1
    keys = seen_rows(z, refs, step, 0)
    stacks, probs = softmax_blocks(z, refs, step, refs.up[...], keys)
    for index in range(BLOCKS):
        listed(refs, "stack")[index][...] = stacks[index]
        listed(refs, "probs")[index][...] = probs[index]


def whole(step, z, refs):
    copies = []
    if hasattr(refs, "pending"):
        copy_rows(refs.pending, refs.dq.at[:, chunk_columns(z, step - 1)], refs.sems, copies)
    matrix = refs.up[...]
    keys, values = seen_rows(z, refs, step, 0), seen_rows(z, refs, step, 1)
    stacks, probs = softmax_blocks(z, refs, step, matrix, keys)
    pair_total = 0.0
    for index in range(BLOCKS):
        start = index * z.block
        cot_stack = stacked(refs.cot, slice(start, start + z.block))
        dscores, grad_stack = score_grads(z, index, probs[index], keys, values, cot_stack)
        unstack(z, grad_stack, refs.grad, start)
        pair_total += pair_terms(z, index, dscores, probs[index], stacks[index], cot_stack)
    grad = refs.grad[...]
    weight = dot(refs.at[...], grad, 1, 0)
    for term in listed(refs, "term"):
        weight += term[...].astype(jnp.float32)
    refs.weight[...] = weight.astype(jnp.bfloat16)
    refs.halo_part[...] = pair_total[: z.span].astype(refs.halo_part.dtype)
    refs.own_part[...] = pair_total[z.span :]
    input_grad = dot(matrix, grad, 1, 1)
    if step > 0:
        input_grad += refs.input_sum[...]
    refs.input_grad[...] = input_grad
    for copy in copies:
        copy.wait()


def front(z, refs):
    copies = []
    step = z.chunks - 1
    for place, grad in enumerate(listed(refs, "pending")):
        target = refs.dq.at[:, chunk_columns(z, step - BLOCKS + place)]
        copy_rows(grad, target, refs.sems, copies)
    keys, values = seen_rows(z, refs, step, 0), seen_rows(z, refs, step, 1)
    probs = refs.probs[...]
    cot_stack = stacked(refs.cot, slice(0, z.block))
    dscores, grad_stack = score_grads(z, 0, probs, keys, values, cot_stack)
    unstack(z, grad_stack, refs.grad, 0)
    pair_total = pair_terms(z, 0, dscores, probs, refs.stack[...], cot_stack)
    kind = refs.halo_grads.dtype
    for place, part in enumerate(listed(refs, "halo_part")):
        refs.halo_grads[:, pair_columns(z, place)] = part[...]
    refs.halo_grads[:, pair_columns(z, step)] = pair_total[: z.span].astype(kind)
    refs.own_part[...] = pair_total[z.span :]
    grad = padded(z, refs.grad[...], 0)
    weight = dot(refs.at[...], grad, 1, 0)
    for term in listed(refs, "term"):
        weight += term[...].astype(jnp.float32)
    refs.weight_part[...] = weight
    refs.input_grad[...] = refs.input_sum[...] + dot(refs.up[...], grad, 1, 1)
    for copy in copies:
        copy.wait()


def back(z, refs):
    step = z.chunks - 1
    keys, values = seen_rows(z, refs, step, 0), seen_rows(z, refs, step, 1)
    cot_stack = stacked(refs.cot, slice(0, z.block))
    dscores, grad_stack = score_grads(z, 1, refs.probs[...], keys, values, cot_stack)
    refs.dscores[...] = dscores
    unstack(z, grad_stack, refs.grad, 0)
    weight = refs.weight_part[...] + dot(refs.at[...], padded(z, refs.grad[...], 1), 1, 0)
    for term in listed(refs, "term"):
        weight += term[...].astype(jnp.float32)
    refs.total[...] = weight.astype(jnp.bfloat16)
    shares = listed(refs, "share")
    rows = z.rank // len(shares)
    for away, share in enumerate(shares):
        target = lax.rem(lax.axis_index("dp") + away, len(shares))
        share[...] = refs.total[pl.ds(pl.multiple_of(target * rows, rows), rows)]


def finish(z, refs):
    copies = []
    step = z.chunks - 1
    for index, grad in enumerate(listed(refs, "pending")):
        target = refs.dq.at[pl.ds(index * z.block, z.block), chunk_columns(z, step)]
        copy_rows(grad, target, refs.sems, copies)
    cot_stack = stacked(refs.cot, slice(0, z.block))
    pair_total = pair_terms(z, 1, refs.dscores[...], refs.probs[...], refs.stack[...], cot_stack)
    parts = [part[...] for part in listed(refs, "own_part")]
    parts[step] += pair_total[z.span :]
    low = z.rows - z.span
    for place, part in enumerate(parts):
        columns = pair_columns(z, place)
        if hasattr(refs, "halo_back"):
            refs.pair_grads[:low, columns] = part[:low].astype(jnp.bfloat16)
            part = part[low:] + refs.halo_back[:, columns].astype(jnp.float32)
            refs.pair_grads[low:, columns] = part.astype(jnp.bfloat16)
        else:
            refs.own_grads[:, columns] = part
    refs.share_out[...] = refs.share[...]
    grad = padded(z, refs.pending1[...], 1)
    input_grad = refs.input_sum[...] + dot(refs.up[...], grad, 1, 1)
    refs.input_grad[...] = input_grad.astype(jnp.bfloat16)
    for copy in copies:
        copy.wait()


def per_device(
    frozen_queries, key_value_pairs, adapter_input, adapter_up_matrix, upstream, document_index
):
    bf16, f32 = jnp.bfloat16, jnp.float32
    chunks = lax.axis_size("seq")
    packs = lax.axis_size("dp")
    place = lax.axis_index("seq")
    rows = frozen_queries.shape[2]
    columns = QUERY_HEADS * HEAD_SIZE
    block = rows // BLOCKS
    span = document_index.shape[2] // SPAN_PARTS
    window = span + block
    width = columns // chunks
    rank = adapter_input.shape[3]
    stack_rows = width // HEAD_SIZE * block
    per_head = chunks // HK
    last = chunks - 1
    z = SimpleNamespace(
        chunks=chunks, rows=rows, block=block, span=span, window=window, width=width, rank=rank
    )
    flops = 10 * stack_rows * window * HEAD_SIZE

    pieces = []
    left = span
    while left > 0:
        pieces.append((len(pieces) + 1, min(rows, left)))
        left -= rows

    own = key_value_pairs[0, 0]
    matrix = adapter_up_matrix[0]
    cotangents = upstream[0, 0]

    def sems(count):
        return dict(sems=pltpu.SemaphoreType.DMA((count,)))

    piece = ((rows, width), bf16)
    first = run(split_first, z, dict(upstream=cotangents), dict(piece=piece), sems(COPIES)).piece
    cots = [passed_along(first, "section", -1)]
    outputs = dict(
        piece=piece, matrix_copy=((rank, width), bf16), pairs_copy=(own.shape, bf16)
    )
    second = run(
        split_second,
        z,
        dict(upstream=cotangents, pairs=own, matrix=matrix, after=first),
        outputs,
        sems(COPIES * len(outputs)),
    )
    cots.append(passed_along(second.piece, "section", -1))
    own, matrix = second.pairs_copy, second.matrix_copy
    outputs = numbered("piece", [piece] * (last - 2) + [((block, width), bf16)] * BLOCKS)
    rest = run(
        split_rest,
        z,
        dict(upstream=cotangents, after=second.piece),
        outputs,
        sems(COPIES * len(outputs)),
    )
    held = listed(rest, "piece")
    cots.append(passed_along(held[0], "section", -1))
    halo = [shifted(own[rows - count :], "seq", distance) for distance, count in pieces]
    halo = jnp.concatenate(halo[::-1], axis=0)
    ups = {0: matrix}
    for away in sorted(range(1, chunks), key=low_bit, reverse=True):
        bit = low_bit(away)
        ups[away] = swapped(ups[away - bit], "seq", bit)

    numbers = jnp.concatenate([jnp.full((span,), -1, jnp.int32), document_index[0, 0]])
    numbers = lax.dynamic_slice_in_dim(numbers, place * rows, span + rows, 0)
    reach = jnp.arange(window, dtype=jnp.int32)[:, None] <= (
        jnp.arange(block, dtype=jnp.int32)[None, :] + span
    )
    bias = []
    for start in range(0, rows, block):
        seen = numbers[start : start + window, None]
        same = seen == numbers[None, start + span : start + span + block]
        bias.append(jnp.where(same & reach, 0.0, -jnp.inf))
    bias = jnp.concatenate(bias, axis=0).astype(f32)
    bias = jnp.concatenate([bias, bias], axis=1)
    fq = frozen_queries[0, 0]
    at = adapter_input[0, 0].T

    outputs = numbered("stack", [((stack_rows, HEAD_SIZE), bf16)] * BLOCKS)
    outputs |= numbered("probs", [((window, stack_rows), f32)] * BLOCKS)
    outputs.update(held=(held[1].shape, bf16))
    inputs = dict(fq=fq, at=at, up=matrix, halo=halo, own=own, bias=bias, held_in=held[1])
    ahead = run(forward, z, inputs, outputs, {}, flops)
    cots.append(passed_along(ahead.held, "section", -1))

    halo_type = bf16 if per_head == 1 else f32
    halo_part, own_part = ((span, PAIR), halo_type), ((rows, PAIR), f32)
    dq_shape = ((rows, columns), bf16)
    input_shape = ((rank, rows), f32)
    terms = {away: [] for away in range(chunks)}
    grads, halo_parts, own_parts = [], [], []
    state = None
    for step in range(last):
        away = last - step
        inputs = dict(fq=fq, at=at, halo=halo, own=own, bias=bias, cot=cots[step], up=ups[away])
        inputs |= numbered("term", terms[away])
        outputs = dict(
            halo_part=halo_part,
            own_part=own_part,
            input_grad=input_shape,
            grad=piece,
            weight=((rank, width), bf16),
        )
        if step > 0:
            inputs.update(input_sum=state.input_grad)
        else:
            inputs.update(after=ahead.stack0)
        if 0 < step < last - 1:
            inputs.update(pending=grads[-1])
            outputs.update(dq=dq_shape)
            if step > 1:
                inputs.update(dq_in=dq)
        if step + 2 < len(held):
            inputs.update(held_in=held[step + 2])
            outputs.update(held=(held[step + 2].shape, bf16))
        body = functools.partial(whole, step)
        body.__name__ = whole.__name__
        state = run(body, z, inputs, outputs, sems(1), 2 * flops)
        grads.append(state.grad)
        halo_parts.append(state.halo_part)
        own_parts.append(state.own_part)
        dq = getattr(state, "dq", None) if step < last - 1 else dq
        if step + 2 < len(held):
            cots.append(passed_along(state.held, "section", -1))
        bit = low_bit(away)
        terms[away - bit].append(swapped(state.weight, "seq", bit))

    common = dict(at=at, up=matrix, halo=halo, own=own)
    outputs = dict(
        dq=dq_shape,
        halo_grads=((span, chunks * PAIR), halo_type),
        own_part=own_part,
        weight_part=((rank, width), f32),
        input_grad=input_shape,
        grad=((block, width), bf16),
    )
    early = run(
        front,
        z,
        common
        | dict(
            cot=cots[last],
            stack=ahead.stack0,
            probs=ahead.probs0,
            dq_in=dq,
            input_sum=state.input_grad,
        )
        | numbered("halo_part", halo_parts)
        | numbered("pending", grads[-BLOCKS:])
        | numbered("term", terms[0][:-1]),
        outputs,
        sems(BLOCKS),
        flops,
    )
    halo_grads = early.halo_grads
    if per_head > 1:
        halo_grads = jnp.sum(halo_grads.reshape(span, HK, per_head, PAIR), axis=2)
        halo_grads = halo_grads.astype(bf16).reshape(span, HK * PAIR)
    backs = []
    stop = span
    for distance, count in pieces:
        backs.append(shifted(halo_grads[stop - count : stop], "seq", -distance))
        stop -= count

    outputs = dict(grad=((block, width), bf16), dscores=((window, stack_rows), bf16))
    outputs |= numbered("share", [((rank // packs, width), bf16)] * packs)
    late = run(
        back,
        z,
        common
        | dict(cot=cots[last + 1], probs=ahead.probs1, weight_part=early.weight_part)
        | numbered("term", terms[0][-1:]),
        outputs,
        dict(total=pltpu.VMEM((rank, width), bf16)),
        flops,
    )
    shares = listed(late, "share")
    shares[1:] = [passed_along(shares[away], "dp", away) for away in range(1, packs)]

    merged = per_head == 1 and len(pieces) == 1
    outputs = dict(dq=dq_shape, input_grad=((rank, rows), bf16))
    outputs.update(share_out=((rank // packs, width), bf16))
    inputs = dict(
        at=at,
        up=matrix,
        cot=cots[last + 1],
        stack=ahead.stack1,
        probs=ahead.probs1,
        dscores=late.dscores,
        input_sum=early.input_grad,
        dq_in=early.dq,
        share=shares[0],
    )
    inputs |= numbered("own_part", own_parts + [early.own_part])
    if merged:
        inputs.update(halo_back=backs[0])
        outputs.update(pair_grads=((rows, HK * PAIR), bf16))
    else:
        outputs.update(own_grads=((rows, chunks * PAIR), f32))
    final = run(
        finish,
        z,
        inputs | numbered("pending", [early.grad, late.grad]),
        outputs,
        sems(BLOCKS),
        flops,
    )
    weight_share = final.share_out.astype(f32)
    for share in shares[1:]:
        weight_share += share.astype(f32)
    if merged:
        pair_grads = final.pair_grads
    else:
        own_grads = jnp.sum(final.own_grads.reshape(rows, HK, per_head, PAIR), axis=2)
        own_grads = own_grads.reshape(rows, HK * PAIR)
        for rows_back in backs:
            low = rows - rows_back.shape[0]
            own_grads = own_grads.at[low:].add(rows_back.astype(f32))
        pair_grads = own_grads.astype(bf16)

    return (
        final.dq[None, None],
        pair_grads[None, None],
        final.input_grad.T[None, None],
        weight_share[None],
    )


def solution(mesh):
    placed = (
        P("section", "dp", "seq", None),
        P("section", "dp", "seq", None),
        P("section", "dp", "seq", None),
        P("section", None, "seq"),
        P("section", "dp", "seq", None),
        P("section", "dp", None),
    )
    return jax.shard_map(
        per_device,
        mesh=mesh,
        in_specs=placed,
        out_specs=(
            P("section", "dp", "seq", None),
            P("section", "dp", "seq", None),
            P("section", "dp", "seq", None),
            P("section", "dp", "seq"),
        ),
        check_vma=False,
    )
```

```python
import functools
import math
from types import SimpleNamespace

import jax
import jax.numpy as jnp
from jax import lax
from jax.experimental import pallas as pl
from jax.experimental.pallas import tpu as pltpu
from jax.sharding import PartitionSpec as P

QUERY_HEADS = 32
HK = 4
HEAD_SIZE = 128
PAIR = 2 * HEAD_SIZE
SCALE = 1.0 / math.sqrt(HEAD_SIZE)
SPAN_PARTS = 8
BLOCKS = 2
COPIES = 4
LIMIT = 16 * 1024 * 1024
IN = "_in"
IN_HBM = ("upstream", "pairs", "matrix", "dq", "dq" + IN)
ANYWHERE = ("held", "held" + IN, "after")
VMEM = pl.BlockSpec(memory_space=pltpu.VMEM)
HBM = pl.BlockSpec(memory_space=pltpu.HBM)
ANY = pl.BlockSpec(memory_space=pl.ANY)


def passed_along(value, axis, steps):
    count = lax.axis_size(axis)
    pairs = [(source, (source + steps) % count) for source in range(count)]
    return lax.ppermute(value, axis, pairs)


def swapped(value, axis, bit):
    pairs = [(source, source ^ bit) for source in range(lax.axis_size(axis))]
    return lax.ppermute(value, axis, pairs)


def dot(left, right, left_dim, right_dim):
    return lax.dot_general(
        left, right, (((left_dim,), (right_dim,)), ((), ())), preferred_element_type=jnp.float32
    )


def low_bit(number):
    return number & -number


def numbered(name, arrays):
    return {name + str(index): array for index, array in enumerate(arrays)}


def listed(refs, name):
    found = []
    while hasattr(refs, name + str(len(found))):
        found.append(getattr(refs, name + str(len(found))))
    return found


def spec_of(name):
    return HBM if name in IN_HBM else ANY if name in ANYWHERE else VMEM


def run(body, sizes, inputs, outputs, scratch, flops=0):
    names = list(inputs) + list(outputs) + list(scratch)

    def kernel(*refs):
        body(sizes, SimpleNamespace(**dict(zip(names, refs))))

    operands = [
        pltpu.with_memory_space_constraint(array, pltpu.HBM) if name in IN_HBM[:3] else array
        for name, array in inputs.items()
    ]
    places = list(inputs)
    aliases = {
        places.index(name + IN): index
        for index, name in enumerate(outputs)
        if name + IN in inputs
    }
    results = pl.pallas_call(
        kernel,
        in_specs=[spec_of(name) for name in inputs],
        out_specs=[spec_of(name) for name in outputs],
        out_shape=[jax.ShapeDtypeStruct(shape, kind) for shape, kind in outputs.values()],
        scratch_shapes=list(scratch.values()),
        input_output_aliases=aliases,
        compiler_params=pltpu.CompilerParams(vmem_limit_bytes=LIMIT),
        cost_estimate=pl.CostEstimate(
            flops=flops // 1024, bytes_accessed=1024, transcendentals=flops // 1024
        ),
        name=body.__name__,
    )(*operands)
    return SimpleNamespace(**dict(zip(outputs, results)))


def copy_rows(source, target, sems, copies, parts=1):
    rows = source.shape[0] // parts
    for part in range(parts):
        piece = pl.ds(part * rows, rows)
        copies.append(
            pltpu.make_async_copy(source.at[piece], target.at[piece], sems.at[len(copies)])
        )
        copies[-1].start()


def chunk_at(step, chunks):
    return lax.axis_index("seq") ^ (chunks - 1 - step)


def chunk_columns(z, step):
    return pl.ds(pl.multiple_of(chunk_at(step, z.chunks) * z.width, HEAD_SIZE), z.width)


def pair_columns(z, step):
    return pl.ds(pl.multiple_of(chunk_at(step, z.chunks) * PAIR, HEAD_SIZE), PAIR)


def split_first(z, refs):
    copies = []
    source = refs.upstream.at[:, chunk_columns(z, 0)]
    copy_rows(source, refs.piece, refs.sems, copies, COPIES)
    for copy in copies:
        copy.wait()


def split_second(z, refs):
    copies = []
    source = refs.upstream.at[:, chunk_columns(z, 1)]
    copy_rows(source, refs.piece, refs.sems, copies, COPIES)
    copy_rows(refs.matrix, refs.matrix_copy, refs.sems, copies, COPIES)
    copy_rows(refs.pairs, refs.pairs_copy, refs.sems, copies, COPIES)
    for copy in copies:
        copy.wait()


def split_rest(z, refs):
    copies = []
    pieces = listed(refs, "piece")
    for step, piece in zip(range(2, z.chunks - 1), pieces):
        copy_rows(refs.upstream.at[:, chunk_columns(z, step)], piece, refs.sems, copies, COPIES)
    for index, piece in enumerate(pieces[-BLOCKS:]):
        rows = pl.ds(index * z.block, z.block)
        source = refs.upstream.at[rows, chunk_columns(z, z.chunks - 1)]
        copy_rows(source, piece, refs.sems, copies, COPIES)
    for copy in copies:
        copy.wait()


def stacked(array, rows):
    heads = array.shape[1] // HEAD_SIZE
    parts = [array[rows, head * HEAD_SIZE : (head + 1) * HEAD_SIZE] for head in range(heads)]
    return jnp.concatenate(parts, axis=0)


def seen_rows(z, refs, step, second):
    per_head = z.chunks // HK
    chunk = chunk_at(step, z.chunks)
    place = lax.div(chunk, per_head) if per_head > 1 else chunk
    start = pl.multiple_of(place * PAIR + second * HEAD_SIZE, HEAD_SIZE)
    columns = pl.ds(start, HEAD_SIZE)
    return jnp.concatenate([refs.halo[: z.span, columns], refs.own[:, columns]], axis=0)


def windowed(z, array, index):
    return array[index * z.block : index * z.block + z.window]


def softmax_blocks(z, refs, step, matrix, keys):
    queries = refs.fq[:, chunk_columns(z, step)].astype(jnp.float32)
    queries = (queries + dot(refs.at[...], matrix, 0, 0)).astype(jnp.bfloat16)
    stacks, probs = [], []
    for index in range(BLOCKS):
        stack = stacked(queries, slice(index * z.block, (index + 1) * z.block))
        hidden = refs.bias[index * z.window : (index + 1) * z.window]
        scores = dot(windowed(z, keys, index), stack, 1, 1) * SCALE
        scores += jnp.concatenate([hidden] * (stack.shape[0] // hidden.shape[1]), axis=1)
        shifted = jnp.exp(scores - jnp.max(scores, axis=0, keepdims=True))
        stacks.append(stack)
        probs.append(shifted * (1.0 / jnp.sum(shifted, axis=0, keepdims=True)))
    return stacks, probs


def score_grads(z, index, probs, keys, values, cot_stack):
    dprobs = dot(windowed(z, values, index), cot_stack, 1, 1)
    deltas = jnp.sum(probs * dprobs, axis=0, keepdims=True)
    dscores = (probs * (dprobs - deltas)).astype(jnp.bfloat16)
    return dscores, (dot(dscores, windowed(z, keys, index), 0, 0) * SCALE).astype(jnp.bfloat16)


def unstack(z, grad_stack, target, start):
    for head in range(grad_stack.shape[0] // z.block):
        columns = slice(head * HEAD_SIZE, (head + 1) * HEAD_SIZE)
        target[start : start + z.block, columns] = grad_stack[head * z.block : (head + 1) * z.block]


def pair_terms(z, index, dscores, probs, query_stack, cot_stack):
    key_term = dot(dscores, query_stack, 1, 0) * SCALE
    value_term = dot(probs.astype(jnp.bfloat16), cot_stack, 1, 0)
    term = jnp.concatenate([key_term, value_term], axis=1)
    start = index * z.block
    rest = z.span + z.rows - z.window - start
    if start > 0:
        term = jnp.concatenate([jnp.zeros((start, PAIR), jnp.float32), term], axis=0)
    if rest > 0:
        term = jnp.concatenate([term, jnp.zeros((rest, PAIR), jnp.float32)], axis=0)
    return term


def padded(z, grad, index):
    blank = jnp.zeros((z.block, grad.shape[1]), grad.dtype)
    return jnp.concatenate([grad if place == index else blank for place in range(BLOCKS)], axis=0)


def forward(z, refs):
    step = z.chunks - 1
    keys = seen_rows(z, refs, step, 0)
    stacks, probs = softmax_blocks(z, refs, step, refs.up[...], keys)
    for index in range(BLOCKS):
        listed(refs, "stack")[index][...] = stacks[index]
        listed(refs, "probs")[index][...] = probs[index]


def whole(step, z, refs):
    copies = []
    if hasattr(refs, "pending"):
        copy_rows(refs.pending, refs.dq.at[:, chunk_columns(z, step - 1)], refs.sems, copies)
    matrix = refs.up[...]
    keys, values = seen_rows(z, refs, step, 0), seen_rows(z, refs, step, 1)
    stacks, probs = softmax_blocks(z, refs, step, matrix, keys)
    pair_total = 0.0
    for index in range(BLOCKS):
        start = index * z.block
        cot_stack = stacked(refs.cot, slice(start, start + z.block))
        dscores, grad_stack = score_grads(z, index, probs[index], keys, values, cot_stack)
        unstack(z, grad_stack, refs.grad, start)
        pair_total += pair_terms(z, index, dscores, probs[index], stacks[index], cot_stack)
    grad = refs.grad[...]
    weight = dot(refs.at[...], grad, 1, 0)
    for term in listed(refs, "term"):
        weight += term[...].astype(jnp.float32)
    refs.weight[...] = weight.astype(jnp.bfloat16)
    refs.halo_part[...] = pair_total[: z.span].astype(refs.halo_part.dtype)
    refs.own_part[...] = pair_total[z.span :]
    input_grad = dot(matrix, grad, 1, 1)
    if step > 0:
        input_grad += refs.input_sum[...]
    refs.input_grad[...] = input_grad
    for copy in copies:
        copy.wait()


def front(z, refs):
    copies = []
    step = z.chunks - 1
    for place, grad in enumerate(listed(refs, "pending")):
        target = refs.dq.at[:, chunk_columns(z, step - BLOCKS + place)]
        copy_rows(grad, target, refs.sems, copies)
    keys, values = seen_rows(z, refs, step, 0), seen_rows(z, refs, step, 1)
    probs = refs.probs[...]
    cot_stack = stacked(refs.cot, slice(0, z.block))
    dscores, grad_stack = score_grads(z, 0, probs, keys, values, cot_stack)
    unstack(z, grad_stack, refs.grad, 0)
    pair_total = pair_terms(z, 0, dscores, probs, refs.stack[...], cot_stack)
    kind = refs.halo_grads.dtype
    for place, part in enumerate(listed(refs, "halo_part")):
        refs.halo_grads[:, pair_columns(z, place)] = part[...]
    refs.halo_grads[:, pair_columns(z, step)] = pair_total[: z.span].astype(kind)
    refs.own_part[...] = pair_total[z.span :]
    grad = padded(z, refs.grad[...], 0)
    weight = dot(refs.at[...], grad, 1, 0)
    for term in listed(refs, "term"):
        weight += term[...].astype(jnp.float32)
    refs.weight_part[...] = weight
    refs.input_grad[...] = refs.input_sum[...] + dot(refs.up[...], grad, 1, 1)
    for copy in copies:
        copy.wait()


def back(z, refs):
    step = z.chunks - 1
    keys, values = seen_rows(z, refs, step, 0), seen_rows(z, refs, step, 1)
    cot_stack = stacked(refs.cot, slice(0, z.block))
    dscores, grad_stack = score_grads(z, 1, refs.probs[...], keys, values, cot_stack)
    refs.dscores[...] = dscores
    unstack(z, grad_stack, refs.grad, 0)
    weight = refs.weight_part[...] + dot(refs.at[...], padded(z, refs.grad[...], 1), 1, 0)
    for term in listed(refs, "term"):
        weight += term[...].astype(jnp.float32)
    refs.total[...] = weight.astype(jnp.bfloat16)
    shares = listed(refs, "share")
    rows = z.rank // len(shares)
    for away, share in enumerate(shares):
        target = lax.rem(lax.axis_index("dp") + away, len(shares))
        share[...] = refs.total[pl.ds(pl.multiple_of(target * rows, rows), rows)]


def finish(z, refs):
    copies = []
    step = z.chunks - 1
    for index, grad in enumerate(listed(refs, "pending")):
        target = refs.dq.at[pl.ds(index * z.block, z.block), chunk_columns(z, step)]
        copy_rows(grad, target, refs.sems, copies)
    cot_stack = stacked(refs.cot, slice(0, z.block))
    pair_total = pair_terms(z, 1, refs.dscores[...], refs.probs[...], refs.stack[...], cot_stack)
    parts = [part[...] for part in listed(refs, "own_part")]
    parts[step] += pair_total[z.span :]
    low = z.rows - z.span
    for place, part in enumerate(parts):
        columns = pair_columns(z, place)
        if hasattr(refs, "halo_back"):
            refs.pair_grads[:low, columns] = part[:low].astype(jnp.bfloat16)
            part = part[low:] + refs.halo_back[:, columns].astype(jnp.float32)
            refs.pair_grads[low:, columns] = part.astype(jnp.bfloat16)
        else:
            refs.own_grads[:, columns] = part
    refs.share_out[...] = refs.share[...]
    grad = padded(z, refs.pending1[...], 1)
    input_grad = refs.input_sum[...] + dot(refs.up[...], grad, 1, 1)
    refs.input_grad[...] = input_grad.astype(jnp.bfloat16)
    for copy in copies:
        copy.wait()


def per_device(
    frozen_queries, key_value_pairs, adapter_input, adapter_up_matrix, upstream, document_index
):
    bf16, f32 = jnp.bfloat16, jnp.float32
    chunks = lax.axis_size("seq")
    packs = lax.axis_size("dp")
    place = lax.axis_index("seq")
    rows = frozen_queries.shape[2]
    columns = QUERY_HEADS * HEAD_SIZE
    block = rows // BLOCKS
    span = document_index.shape[2] // SPAN_PARTS
    window = span + block
    width = columns // chunks
    rank = adapter_input.shape[3]
    stack_rows = width // HEAD_SIZE * block
    per_head = chunks // HK
    last = chunks - 1
    z = SimpleNamespace(
        chunks=chunks, rows=rows, block=block, span=span, window=window, width=width, rank=rank
    )
    flops = 10 * stack_rows * window * HEAD_SIZE

    pieces = []
    left = span
    while left > 0:
        pieces.append((len(pieces) + 1, min(rows, left)))
        left -= rows

    own = key_value_pairs[0, 0]
    matrix = adapter_up_matrix[0]
    cotangents = upstream[0, 0]

    def sems(count):
        return dict(sems=pltpu.SemaphoreType.DMA((count,)))

    piece = ((rows, width), bf16)
    first = run(split_first, z, dict(upstream=cotangents), dict(piece=piece), sems(COPIES)).piece
    cots = [passed_along(first, "section", -1)]
    outputs = dict(
        piece=piece, matrix_copy=((rank, width), bf16), pairs_copy=(own.shape, bf16)
    )
    second = run(
        split_second,
        z,
        dict(upstream=cotangents, pairs=own, matrix=matrix, after=first),
        outputs,
        sems(COPIES * len(outputs)),
    )
    cots.append(passed_along(second.piece, "section", -1))
    own, matrix = second.pairs_copy, second.matrix_copy
    outputs = numbered("piece", [piece] * (last - 2) + [((block, width), bf16)] * BLOCKS)
    rest = run(
        split_rest,
        z,
        dict(upstream=cotangents, after=second.piece),
        outputs,
        sems(COPIES * len(outputs)),
    )
    held = listed(rest, "piece")
    cots.append(passed_along(held[0], "section", -1))
    halo = [passed_along(own[rows - count :], "seq", distance) for distance, count in pieces]
    halo = jnp.concatenate(halo[::-1], axis=0)
    ups = {0: matrix}
    for away in sorted(range(1, chunks), key=low_bit, reverse=True):
        bit = low_bit(away)
        ups[away] = swapped(ups[away - bit], "seq", bit)

    numbers = jnp.concatenate([jnp.full((span,), -1, jnp.int32), document_index[0, 0]])
    numbers = lax.dynamic_slice_in_dim(numbers, place * rows, span + rows, 0)
    reach = jnp.arange(window, dtype=jnp.int32)[:, None] <= (
        jnp.arange(block, dtype=jnp.int32)[None, :] + span
    )
    bias = []
    for start in range(0, rows, block):
        seen = numbers[start : start + window, None]
        same = seen == numbers[None, start + span : start + span + block]
        bias.append(jnp.where(same & reach, 0.0, -jnp.inf))
    bias = jnp.concatenate(bias, axis=0).astype(f32)
    bias = jnp.concatenate([bias, bias], axis=1)
    fq = frozen_queries[0, 0]
    at = adapter_input[0, 0].T

    outputs = numbered("stack", [((stack_rows, HEAD_SIZE), bf16)] * BLOCKS)
    outputs |= numbered("probs", [((window, stack_rows), f32)] * BLOCKS)
    outputs.update(held=(held[1].shape, bf16))
    inputs = dict(fq=fq, at=at, up=matrix, halo=halo, own=own, bias=bias, held_in=held[1])
    ahead = run(forward, z, inputs, outputs, {}, flops)
    cots.append(passed_along(ahead.held, "section", -1))

    halo_type = bf16 if per_head == 1 else f32
    halo_part, own_part = ((span, PAIR), halo_type), ((rows, PAIR), f32)
    dq_shape = ((rows, columns), bf16)
    input_shape = ((rank, rows), f32)
    terms = {away: [] for away in range(chunks)}
    grads, halo_parts, own_parts = [], [], []
    state = None
    for step in range(last):
        away = last - step
        inputs = dict(fq=fq, at=at, halo=halo, own=own, bias=bias, cot=cots[step], up=ups[away])
        inputs |= numbered("term", terms[away])
        outputs = dict(
            halo_part=halo_part,
            own_part=own_part,
            input_grad=input_shape,
            grad=piece,
            weight=((rank, width), bf16),
        )
        if step > 0:
            inputs.update(input_sum=state.input_grad)
        else:
            inputs.update(after=ahead.stack0)
        if 0 < step < last - 1:
            inputs.update(pending=grads[-1])
            outputs.update(dq=dq_shape)
            if step > 1:
                inputs.update(dq_in=dq)
        if step + 2 < len(held):
            inputs.update(held_in=held[step + 2])
            outputs.update(held=(held[step + 2].shape, bf16))
        body = functools.partial(whole, step)
        body.__name__ = whole.__name__
        state = run(body, z, inputs, outputs, sems(1), 2 * flops)
        grads.append(state.grad)
        halo_parts.append(state.halo_part)
        own_parts.append(state.own_part)
        dq = getattr(state, "dq", None) if step < last - 1 else dq
        if step + 2 < len(held):
            cots.append(passed_along(state.held, "section", -1))
        bit = low_bit(away)
        terms[away - bit].append(swapped(state.weight, "seq", bit))

    common = dict(at=at, up=matrix, halo=halo, own=own)
    outputs = dict(
        dq=dq_shape,
        halo_grads=((span, chunks * PAIR), halo_type),
        own_part=own_part,
        weight_part=((rank, width), f32),
        input_grad=input_shape,
        grad=((block, width), bf16),
    )
    early = run(
        front,
        z,
        common
        | dict(
            cot=cots[last],
            stack=ahead.stack0,
            probs=ahead.probs0,
            dq_in=dq,
            input_sum=state.input_grad,
        )
        | numbered("halo_part", halo_parts)
        | numbered("pending", grads[-BLOCKS:])
        | numbered("term", terms[0][:-1]),
        outputs,
        sems(BLOCKS),
        flops,
    )
    halo_grads = early.halo_grads
    if per_head > 1:
        halo_grads = jnp.sum(halo_grads.reshape(span, HK, per_head, PAIR), axis=2)
        halo_grads = halo_grads.astype(bf16).reshape(span, HK * PAIR)
    backs = []
    stop = span
    for distance, count in pieces:
        backs.append(passed_along(halo_grads[stop - count : stop], "seq", -distance))
        stop -= count

    outputs = dict(grad=((block, width), bf16), dscores=((window, stack_rows), bf16))
    outputs |= numbered("share", [((rank // packs, width), bf16)] * packs)
    late = run(
        back,
        z,
        common
        | dict(cot=cots[last + 1], probs=ahead.probs1, weight_part=early.weight_part)
        | numbered("term", terms[0][-1:]),
        outputs,
        dict(total=pltpu.VMEM((rank, width), bf16)),
        flops,
    )
    shares = listed(late, "share")
    shares[1:] = [passed_along(shares[away], "dp", away) for away in range(1, packs)]

    merged = per_head == 1 and len(pieces) == 1
    outputs = dict(dq=dq_shape, input_grad=((rank, rows), bf16))
    outputs.update(share_out=((rank // packs, width), bf16))
    inputs = dict(
        at=at,
        up=matrix,
        cot=cots[last + 1],
        stack=ahead.stack1,
        probs=ahead.probs1,
        dscores=late.dscores,
        input_sum=early.input_grad,
        dq_in=early.dq,
        share=shares[0],
    )
    inputs |= numbered("own_part", own_parts + [early.own_part])
    if merged:
        inputs.update(halo_back=backs[0])
        outputs.update(pair_grads=((rows, HK * PAIR), bf16))
    else:
        outputs.update(own_grads=((rows, chunks * PAIR), f32))
    final = run(
        finish,
        z,
        inputs | numbered("pending", [early.grad, late.grad]),
        outputs,
        sems(BLOCKS),
        flops,
    )
    weight_share = final.share_out.astype(f32)
    shares[1:] = shares[1:2] + shares[:1:-1]
    for share in shares[1:]:
        weight_share += share.astype(f32)
    if merged:
        pair_grads = final.pair_grads
    else:
        own_grads = jnp.sum(final.own_grads.reshape(rows, HK, per_head, PAIR), axis=2)
        own_grads = own_grads.reshape(rows, HK * PAIR)
        for rows_back in backs:
            low = rows - rows_back.shape[0]
            own_grads = own_grads.at[low:].add(rows_back.astype(f32))
        pair_grads = own_grads.astype(bf16)

    return (
        final.dq[None, None],
        pair_grads[None, None],
        final.input_grad.T[None, None],
        weight_share[None],
    )


def solution(mesh):
    placed = (
        P("section", "dp", "seq", None),
        P("section", "dp", "seq", None),
        P("section", "dp", "seq", None),
        P("section", None, "seq"),
        P("section", "dp", "seq", None),
        P("section", "dp", None),
    )
    return jax.shard_map(
        per_device,
        mesh=mesh,
        in_specs=placed,
        out_specs=(
            P("section", "dp", "seq", None),
            P("section", "dp", "seq", None),
            P("section", "dp", "seq", None),
            P("section", "dp", "seq"),
        ),
        check_vma=False,
    )
```

```python
import functools
import math
from types import SimpleNamespace

import jax
import jax.numpy as jnp
from jax import lax
from jax.experimental import pallas as pl
from jax.experimental.pallas import tpu as pltpu
from jax.sharding import PartitionSpec as P

QUERY_HEADS = 32
HK = 4
HEAD_SIZE = 128
PAIR = 2 * HEAD_SIZE
SCALE = 1.0 / math.sqrt(HEAD_SIZE)
SPAN_PARTS = 8
BLOCKS = 2
COPIES = 4
LIMIT = 16 * 1024 * 1024
IN = "_in"
IN_HBM = ("upstream", "pairs", "matrix", "dq", "dq" + IN, "weight_grad")
ANYWHERE = ("held", "held" + IN, "after")
VMEM = pl.BlockSpec(memory_space=pltpu.VMEM)
HBM = pl.BlockSpec(memory_space=pltpu.HBM)
ANY = pl.BlockSpec(memory_space=pl.ANY)


def passed_along(value, axis, steps):
    count = lax.axis_size(axis)
    pairs = [(source, (source + steps) % count) for source in range(count)]
    return lax.ppermute(value, axis, pairs)


def swapped(value, axis, bit):
    pairs = [(source, source ^ bit) for source in range(lax.axis_size(axis))]
    return lax.ppermute(value, axis, pairs)


def dot(left, right, left_dim, right_dim):
    return lax.dot_general(
        left, right, (((left_dim,), (right_dim,)), ((), ())), preferred_element_type=jnp.float32
    )


def low_bit(number):
    return number & -number


def numbered(name, arrays):
    return {name + str(index): array for index, array in enumerate(arrays)}


def listed(refs, name):
    found = []
    while hasattr(refs, name + str(len(found))):
        found.append(getattr(refs, name + str(len(found))))
    return found


def spec_of(name):
    return HBM if name in IN_HBM else ANY if name in ANYWHERE else VMEM


def run(body, sizes, inputs, outputs, scratch, flops=0):
    names = list(inputs) + list(outputs) + list(scratch)

    def kernel(*refs):
        body(sizes, SimpleNamespace(**dict(zip(names, refs))))

    operands = [
        pltpu.with_memory_space_constraint(array, pltpu.HBM) if name in IN_HBM[:3] else array
        for name, array in inputs.items()
    ]
    places = list(inputs)
    aliases = {
        places.index(name + IN): index
        for index, name in enumerate(outputs)
        if name + IN in inputs
    }
    results = pl.pallas_call(
        kernel,
        in_specs=[spec_of(name) for name in inputs],
        out_specs=[spec_of(name) for name in outputs],
        out_shape=[jax.ShapeDtypeStruct(shape, kind) for shape, kind in outputs.values()],
        scratch_shapes=list(scratch.values()),
        input_output_aliases=aliases,
        compiler_params=pltpu.CompilerParams(vmem_limit_bytes=LIMIT),
        cost_estimate=pl.CostEstimate(
            flops=flops // 1024, bytes_accessed=1024, transcendentals=flops // 1024
        ),
        name=body.__name__,
    )(*operands)
    return SimpleNamespace(**dict(zip(outputs, results)))


def copy_rows(source, target, sems, copies, parts=1):
    rows = source.shape[0] // parts
    for part in range(parts):
        piece = pl.ds(part * rows, rows)
        copies.append(
            pltpu.make_async_copy(source.at[piece], target.at[piece], sems.at[len(copies)])
        )
        copies[-1].start()


def chunk_at(step, chunks):
    return lax.axis_index("seq") ^ (chunks - 1 - step)


def chunk_columns(z, step):
    return pl.ds(pl.multiple_of(chunk_at(step, z.chunks) * z.width, HEAD_SIZE), z.width)


def pair_columns(z, step):
    return pl.ds(pl.multiple_of(chunk_at(step, z.chunks) * PAIR, HEAD_SIZE), PAIR)


def split_first(z, refs):
    copies = []
    source = refs.upstream.at[:, chunk_columns(z, 0)]
    copy_rows(source, refs.piece, refs.sems, copies, COPIES)
    for copy in copies:
        copy.wait()


def split_second(z, refs):
    copies = []
    source = refs.upstream.at[:, chunk_columns(z, 1)]
    copy_rows(source, refs.piece, refs.sems, copies, COPIES)
    copy_rows(refs.matrix, refs.matrix_copy, refs.sems, copies, COPIES)
    copy_rows(refs.pairs, refs.pairs_copy, refs.sems, copies, COPIES)
    for copy in copies:
        copy.wait()


def split_rest(z, refs):
    copies = []
    pieces = listed(refs, "piece")
    for step, piece in zip(range(2, z.chunks - 1), pieces):
        copy_rows(refs.upstream.at[:, chunk_columns(z, step)], piece, refs.sems, copies, COPIES)
    for index, piece in enumerate(pieces[-BLOCKS:]):
        rows = pl.ds(index * z.block, z.block)
        source = refs.upstream.at[rows, chunk_columns(z, z.chunks - 1)]
        copy_rows(source, piece, refs.sems, copies, COPIES)
    for copy in copies:
        copy.wait()


def stacked(array, rows):
    heads = array.shape[1] // HEAD_SIZE
    parts = [array[rows, head * HEAD_SIZE : (head + 1) * HEAD_SIZE] for head in range(heads)]
    return jnp.concatenate(parts, axis=0)


def seen_rows(z, refs, step, second):
    per_head = z.chunks // HK
    chunk = chunk_at(step, z.chunks)
    place = lax.div(chunk, per_head) if per_head > 1 else chunk
    start = pl.multiple_of(place * PAIR + second * HEAD_SIZE, HEAD_SIZE)
    columns = pl.ds(start, HEAD_SIZE)
    return jnp.concatenate([refs.halo[: z.span, columns], refs.own[:, columns]], axis=0)


def windowed(z, array, index):
    return array[index * z.block : index * z.block + z.window]


def softmax_blocks(z, refs, step, matrix, keys):
    queries = refs.fq[:, chunk_columns(z, step)].astype(jnp.float32)
    queries = (queries + dot(refs.at[...], matrix, 0, 0)).astype(jnp.bfloat16)
    stacks, probs = [], []
    for index in range(BLOCKS):
        stack = stacked(queries, slice(index * z.block, (index + 1) * z.block))
        hidden = refs.bias[index * z.window : (index + 1) * z.window]
        scores = dot(windowed(z, keys, index), stack, 1, 1) * SCALE
        scores += jnp.concatenate([hidden] * (stack.shape[0] // hidden.shape[1]), axis=1)
        shifted = jnp.exp(scores - jnp.max(scores, axis=0, keepdims=True))
        stacks.append(stack)
        probs.append(shifted * (1.0 / jnp.sum(shifted, axis=0, keepdims=True)))
    return stacks, probs


def score_grads(z, index, probs, keys, values, cot_stack):
    dprobs = dot(windowed(z, values, index), cot_stack, 1, 1)
    deltas = jnp.sum(probs * dprobs, axis=0, keepdims=True)
    dscores = (probs * (dprobs - deltas)).astype(jnp.bfloat16)
    return dscores, (dot(dscores, windowed(z, keys, index), 0, 0) * SCALE).astype(jnp.bfloat16)


def unstack(z, grad_stack, target, start):
    for head in range(grad_stack.shape[0] // z.block):
        columns = slice(head * HEAD_SIZE, (head + 1) * HEAD_SIZE)
        target[start : start + z.block, columns] = grad_stack[head * z.block : (head + 1) * z.block]


def pair_terms(z, index, dscores, probs, query_stack, cot_stack):
    key_term = dot(dscores, query_stack, 1, 0) * SCALE
    value_term = dot(probs.astype(jnp.bfloat16), cot_stack, 1, 0)
    term = jnp.concatenate([key_term, value_term], axis=1)
    start = index * z.block
    rest = z.span + z.rows - z.window - start
    if start > 0:
        term = jnp.concatenate([jnp.zeros((start, PAIR), jnp.float32), term], axis=0)
    if rest > 0:
        term = jnp.concatenate([term, jnp.zeros((rest, PAIR), jnp.float32)], axis=0)
    return term


def padded(z, grad, index):
    blank = jnp.zeros((z.block, grad.shape[1]), grad.dtype)
    return jnp.concatenate([grad if place == index else blank for place in range(BLOCKS)], axis=0)


def forward(z, refs):
    step = z.chunks - 1
    keys = seen_rows(z, refs, step, 0)
    stacks, probs = softmax_blocks(z, refs, step, refs.up[...], keys)
    for index in range(BLOCKS):
        listed(refs, "stack")[index][...] = stacks[index]
        listed(refs, "probs")[index][...] = probs[index]


def whole(step, z, refs):
    copies = []
    if hasattr(refs, "pending"):
        copy_rows(refs.pending, refs.dq.at[:, chunk_columns(z, step - 1)], refs.sems, copies)
    matrix = refs.up[...]
    keys, values = seen_rows(z, refs, step, 0), seen_rows(z, refs, step, 1)
    stacks, probs = softmax_blocks(z, refs, step, matrix, keys)
    pair_total = 0.0
    for index in range(BLOCKS):
        start = index * z.block
        cot_stack = stacked(refs.cot, slice(start, start + z.block))
        dscores, grad_stack = score_grads(z, index, probs[index], keys, values, cot_stack)
        unstack(z, grad_stack, refs.grad, start)
        pair_total += pair_terms(z, index, dscores, probs[index], stacks[index], cot_stack)
    grad = refs.grad[...]
    weight = dot(refs.at[...], grad, 1, 0)
    for term in listed(refs, "term"):
        weight += term[...].astype(jnp.float32)
    refs.weight[...] = weight.astype(jnp.bfloat16)
    refs.halo_part[...] = pair_total[: z.span].astype(refs.halo_part.dtype)
    refs.own_part[...] = pair_total[z.span :]
    input_grad = dot(matrix, grad, 1, 1)
    if step > 0:
        input_grad += refs.input_sum[...]
    refs.input_grad[...] = input_grad
    for copy in copies:
        copy.wait()


def front(z, refs):
    copies = []
    step = z.chunks - 1
    for place, grad in enumerate(listed(refs, "pending")):
        target = refs.dq.at[:, chunk_columns(z, step - BLOCKS + place)]
        copy_rows(grad, target, refs.sems, copies)
    keys, values = seen_rows(z, refs, step, 0), seen_rows(z, refs, step, 1)
    probs = refs.probs[...]
    cot_stack = stacked(refs.cot, slice(0, z.block))
    dscores, grad_stack = score_grads(z, 0, probs, keys, values, cot_stack)
    unstack(z, grad_stack, refs.grad, 0)
    pair_total = pair_terms(z, 0, dscores, probs, refs.stack[...], cot_stack)
    kind = refs.halo_grads.dtype
    for place, part in enumerate(listed(refs, "halo_part")):
        refs.halo_grads[:, pair_columns(z, place)] = part[...]
    refs.halo_grads[:, pair_columns(z, step)] = pair_total[: z.span].astype(kind)
    refs.own_part[...] = pair_total[z.span :]
    grad = padded(z, refs.grad[...], 0)
    weight = dot(refs.at[...], grad, 1, 0)
    for term in listed(refs, "term"):
        weight += term[...].astype(jnp.float32)
    refs.weight_part[...] = weight
    refs.input_grad[...] = refs.input_sum[...] + dot(refs.up[...], grad, 1, 1)
    for copy in copies:
        copy.wait()


def back(z, refs):
    step = z.chunks - 1
    keys, values = seen_rows(z, refs, step, 0), seen_rows(z, refs, step, 1)
    cot_stack = stacked(refs.cot, slice(0, z.block))
    dscores, grad_stack = score_grads(z, 1, refs.probs[...], keys, values, cot_stack)
    refs.dscores[...] = dscores
    parts = [grad_stack[start : start + z.block] for start in range(0, len(grad_stack), z.block)]
    grad = jnp.concatenate(parts, axis=1)
    refs.grad[...] = grad
    weight = refs.weight_part[...] + dot(refs.at[...], padded(z, grad, 1), 1, 0)
    for term in listed(refs, "term"):
        weight += term[...].astype(jnp.float32)
    refs.total[...] = weight.astype(jnp.bfloat16)
    shares = listed(refs, "share")
    rows = z.rank // len(shares)
    for away, share in enumerate(shares):
        target = lax.rem(lax.axis_index("dp") + away, len(shares))
        share[...] = refs.total[pl.ds(pl.multiple_of(target * rows, rows), rows)]


def add_shares(z, refs):
    total = refs.share0[...].astype(jnp.float32)
    for share in listed(refs, "share")[1:]:
        total += share[...].astype(jnp.float32)
    refs.total[...] = total
    copies = []
    copy_rows(refs.total, refs.weight_grad, refs.sems, copies)
    for copy in copies:
        copy.wait()


def finish(z, refs):
    copies = []
    step = z.chunks - 1
    for index, grad in enumerate(listed(refs, "pending")):
        target = refs.dq.at[pl.ds(index * z.block, z.block), chunk_columns(z, step)]
        copy_rows(grad, target, refs.sems, copies)
    cot_stack = stacked(refs.cot, slice(0, z.block))
    pair_total = pair_terms(z, 1, refs.dscores[...], refs.probs[...], refs.stack[...], cot_stack)
    parts = [part[...] for part in listed(refs, "own_part")]
    parts[step] += pair_total[z.span :]
    low = z.rows - z.span
    for place, part in enumerate(parts):
        columns = pair_columns(z, place)
        if hasattr(refs, "halo_back"):
            refs.pair_grads[:low, columns] = part[:low].astype(jnp.bfloat16)
            part = part[low:] + refs.halo_back[:, columns].astype(jnp.float32)
            refs.pair_grads[low:, columns] = part.astype(jnp.bfloat16)
        else:
            refs.own_grads[:, columns] = part
    refs.share_out[...] = refs.share[...]
    grad = padded(z, refs.pending1[...], 1)
    input_grad = refs.input_sum[...] + dot(refs.up[...], grad, 1, 1)
    refs.input_grad[...] = input_grad.astype(jnp.bfloat16)
    for copy in copies:
        copy.wait()


def per_device(
    frozen_queries, key_value_pairs, adapter_input, adapter_up_matrix, upstream, document_index
):
    bf16, f32 = jnp.bfloat16, jnp.float32
    chunks = lax.axis_size("seq")
    packs = lax.axis_size("dp")
    place = lax.axis_index("seq")
    rows = frozen_queries.shape[2]
    columns = QUERY_HEADS * HEAD_SIZE
    block = rows // BLOCKS
    span = document_index.shape[2] // SPAN_PARTS
    window = span + block
    width = columns // chunks
    rank = adapter_input.shape[3]
    stack_rows = width // HEAD_SIZE * block
    per_head = chunks // HK
    last = chunks - 1
    z = SimpleNamespace(
        chunks=chunks, rows=rows, block=block, span=span, window=window, width=width, rank=rank
    )
    flops = 10 * stack_rows * window * HEAD_SIZE

    pieces = []
    left = span
    while left > 0:
        pieces.append((len(pieces) + 1, min(rows, left)))
        left -= rows

    own = key_value_pairs[0, 0]
    matrix = adapter_up_matrix[0]
    cotangents = upstream[0, 0]

    def sems(count):
        return dict(sems=pltpu.SemaphoreType.DMA((count,)))

    piece = ((rows, width), bf16)
    first = run(split_first, z, dict(upstream=cotangents), dict(piece=piece), sems(COPIES)).piece
    cots = [passed_along(first, "section", -1)]
    outputs = dict(
        piece=piece, matrix_copy=((rank, width), bf16), pairs_copy=(own.shape, bf16)
    )
    second = run(
        split_second,
        z,
        dict(upstream=cotangents, pairs=own, matrix=matrix, after=first),
        outputs,
        sems(COPIES * len(outputs)),
    )
    cots.append(passed_along(second.piece, "section", -1))
    own, matrix = second.pairs_copy, second.matrix_copy
    outputs = numbered("piece", [piece] * (last - 2) + [((block, width), bf16)] * BLOCKS)
    rest = run(
        split_rest,
        z,
        dict(upstream=cotangents, after=second.piece),
        outputs,
        sems(COPIES * len(outputs)),
    )
    held = listed(rest, "piece")
    cots.append(passed_along(held[0], "section", -1))
    halo = [passed_along(own[rows - count :], "seq", distance) for distance, count in pieces]
    halo = jnp.concatenate(halo[::-1], axis=0)
    ups = {0: matrix}
    for away in sorted(range(1, chunks), key=low_bit, reverse=True):
        bit = low_bit(away)
        ups[away] = swapped(ups[away - bit], "seq", bit)

    numbers = jnp.concatenate([jnp.full((span,), -1, jnp.int32), document_index[0, 0]])
    numbers = lax.dynamic_slice_in_dim(numbers, place * rows, span + rows, 0)
    reach = jnp.arange(window, dtype=jnp.int32)[:, None] <= (
        jnp.arange(block, dtype=jnp.int32)[None, :] + span
    )
    bias = []
    for start in range(0, rows, block):
        seen = numbers[start : start + window, None]
        same = seen == numbers[None, start + span : start + span + block]
        bias.append(jnp.where(same & reach, 0.0, -jnp.inf))
    bias = jnp.concatenate(bias, axis=0).astype(f32)
    bias = jnp.concatenate([bias, bias], axis=1)
    fq = frozen_queries[0, 0]
    at = adapter_input[0, 0].T

    outputs = numbered("stack", [((stack_rows, HEAD_SIZE), bf16)] * BLOCKS)
    outputs |= numbered("probs", [((window, stack_rows), f32)] * BLOCKS)
    outputs.update(held=(held[1].shape, bf16))
    inputs = dict(fq=fq, at=at, up=matrix, halo=halo, own=own, bias=bias, held_in=held[1])
    ahead = run(forward, z, inputs, outputs, {}, flops)
    cots.append(passed_along(ahead.held, "section", -1))

    halo_type = bf16 if per_head == 1 else f32
    halo_part, own_part = ((span, PAIR), halo_type), ((rows, PAIR), f32)
    dq_shape = ((rows, columns), bf16)
    input_shape = ((rank, rows), f32)
    terms = {away: [] for away in range(chunks)}
    grads, halo_parts, own_parts = [], [], []
    state = None
    for step in range(last):
        away = last - step
        inputs = dict(fq=fq, at=at, halo=halo, own=own, bias=bias, cot=cots[step], up=ups[away])
        inputs |= numbered("term", terms[away])
        outputs = dict(
            halo_part=halo_part,
            own_part=own_part,
            input_grad=input_shape,
            grad=piece,
            weight=((rank, width), bf16),
        )
        if step > 0:
            inputs.update(input_sum=state.input_grad)
        else:
            inputs.update(after=ahead.stack0)
        if 0 < step < last - 1:
            inputs.update(pending=grads[-1])
            outputs.update(dq=dq_shape)
            if step > 1:
                inputs.update(dq_in=dq)
        if step + 2 < len(held):
            inputs.update(held_in=held[step + 2])
            outputs.update(held=(held[step + 2].shape, bf16))
        body = functools.partial(whole, step)
        body.__name__ = whole.__name__
        state = run(body, z, inputs, outputs, sems(1), 2 * flops)
        grads.append(state.grad)
        halo_parts.append(state.halo_part)
        own_parts.append(state.own_part)
        dq = getattr(state, "dq", None) if step < last - 1 else dq
        if step + 2 < len(held):
            cots.append(passed_along(state.held, "section", -1))
        bit = low_bit(away)
        terms[away - bit].append(swapped(state.weight, "seq", bit))

    common = dict(at=at, up=matrix, halo=halo, own=own)
    outputs = dict(
        dq=dq_shape,
        halo_grads=((span, chunks * PAIR), halo_type),
        own_part=own_part,
        weight_part=((rank, width), f32),
        input_grad=input_shape,
        grad=((block, width), bf16),
    )
    early = run(
        front,
        z,
        common
        | dict(
            cot=cots[last],
            stack=ahead.stack0,
            probs=ahead.probs0,
            dq_in=dq,
            input_sum=state.input_grad,
        )
        | numbered("halo_part", halo_parts)
        | numbered("pending", grads[-BLOCKS:])
        | numbered("term", terms[0][:-1]),
        outputs,
        sems(BLOCKS),
        flops,
    )
    halo_grads = early.halo_grads
    if per_head > 1:
        halo_grads = jnp.sum(halo_grads.reshape(span, HK, per_head, PAIR), axis=2)
        halo_grads = halo_grads.astype(bf16).reshape(span, HK * PAIR)
    backs = []
    stop = span
    for distance, count in pieces:
        backs.append(passed_along(halo_grads[stop - count : stop], "seq", -distance))
        stop -= count

    outputs = dict(grad=((block, width), bf16), dscores=((window, stack_rows), bf16))
    outputs |= numbered("share", [((rank // packs, width), bf16)] * packs)
    late = run(
        back,
        z,
        common
        | dict(cot=cots[last + 1], probs=ahead.probs1, weight_part=early.weight_part)
        | numbered("term", terms[0][-1:]),
        outputs,
        dict(total=pltpu.VMEM((rank, width), bf16)),
        flops,
    )
    shares = listed(late, "share")
    shares[1:] = [passed_along(shares[away], "dp", away) for away in range(1, packs)]

    merged = per_head == 1 and len(pieces) == 1
    outputs = dict(dq=dq_shape, input_grad=((rank, rows), bf16))
    outputs.update(share_out=((rank // packs, width), bf16))
    inputs = dict(
        at=at,
        up=matrix,
        cot=cots[last + 1],
        stack=ahead.stack1,
        probs=ahead.probs1,
        dscores=late.dscores,
        input_sum=early.input_grad,
        dq_in=early.dq,
        share=shares[0],
    )
    inputs |= numbered("own_part", own_parts + [early.own_part])
    if merged:
        inputs.update(halo_back=backs[0])
        outputs.update(pair_grads=((rows, HK * PAIR), bf16))
    else:
        outputs.update(own_grads=((rows, chunks * PAIR), f32))
    final = run(
        finish,
        z,
        inputs | numbered("pending", [early.grad, late.grad]),
        outputs,
        sems(BLOCKS),
        flops,
    )
    shares[0] = final.share_out
    share_shape = ((rank // packs, width), f32)
    weight_share = run(
        add_shares,
        z,
        numbered("share", shares),
        dict(weight_grad=share_shape),
        dict(total=pltpu.VMEM(*share_shape)) | sems(1),
    ).weight_grad
    if merged:
        pair_grads = final.pair_grads
    else:
        own_grads = jnp.sum(final.own_grads.reshape(rows, HK, per_head, PAIR), axis=2)
        own_grads = own_grads.reshape(rows, HK * PAIR)
        for rows_back in backs:
            low = rows - rows_back.shape[0]
            own_grads = own_grads.at[low:].add(rows_back.astype(f32))
        pair_grads = own_grads.astype(bf16)

    return (
        final.dq[None, None],
        pair_grads[None, None],
        final.input_grad.T[None, None],
        weight_share[None],
    )


def solution(mesh):
    placed = (
        P("section", "dp", "seq", None),
        P("section", "dp", "seq", None),
        P("section", "dp", "seq", None),
        P("section", None, "seq"),
        P("section", "dp", "seq", None),
        P("section", "dp", None),
    )
    return jax.shard_map(
        per_device,
        mesh=mesh,
        in_specs=placed,
        out_specs=(
            P("section", "dp", "seq", None),
            P("section", "dp", "seq", None),
            P("section", "dp", "seq", None),
            P("section", "dp", "seq"),
        ),
        check_vma=False,
    )
```

```python
import functools
import math
from types import SimpleNamespace

import jax
import jax.numpy as jnp
from jax import lax
from jax.experimental import pallas as pl
from jax.experimental.pallas import tpu as pltpu
from jax.sharding import PartitionSpec as P

QUERY_HEADS = 32
HK = 4
HEAD_SIZE = 128
PAIR = 2 * HEAD_SIZE
SCALE = 1.0 / math.sqrt(HEAD_SIZE)
SPAN_PARTS = 8
BLOCKS = 2
COPIES = 4
LIMIT = 16 * 1024 * 1024
IN = "_in"
IN_HBM = ("upstream", "pairs", "matrix", "dq", "dq" + IN)
ANYWHERE = ("held", "held" + IN, "after")
VMEM = pl.BlockSpec(memory_space=pltpu.VMEM)
HBM = pl.BlockSpec(memory_space=pltpu.HBM)
ANY = pl.BlockSpec(memory_space=pl.ANY)


def passed_along(value, axis, steps):
    count = lax.axis_size(axis)
    pairs = [(source, (source + steps) % count) for source in range(count)]
    return lax.ppermute(value, axis, pairs)


def swapped(value, axis, bit):
    pairs = [(source, source ^ bit) for source in range(lax.axis_size(axis))]
    return lax.ppermute(value, axis, pairs)


def dot(left, right, left_dim, right_dim):
    return lax.dot_general(
        left, right, (((left_dim,), (right_dim,)), ((), ())), preferred_element_type=jnp.float32
    )


def low_bit(number):
    return number & -number


def numbered(name, arrays):
    return {name + str(index): array for index, array in enumerate(arrays)}


def listed(refs, name):
    found = []
    while hasattr(refs, name + str(len(found))):
        found.append(getattr(refs, name + str(len(found))))
    return found


def spec_of(name):
    return HBM if name in IN_HBM else ANY if name in ANYWHERE else VMEM


def run(body, sizes, inputs, outputs, scratch, flops=0):
    names = list(inputs) + list(outputs) + list(scratch)

    def kernel(*refs):
        body(sizes, SimpleNamespace(**dict(zip(names, refs))))

    operands = [
        pltpu.with_memory_space_constraint(array, pltpu.HBM) if name in IN_HBM[:3] else array
        for name, array in inputs.items()
    ]
    places = list(inputs)
    aliases = {
        places.index(name + IN): index
        for index, name in enumerate(outputs)
        if name + IN in inputs
    }
    results = pl.pallas_call(
        kernel,
        in_specs=[spec_of(name) for name in inputs],
        out_specs=[spec_of(name) for name in outputs],
        out_shape=[jax.ShapeDtypeStruct(shape, kind) for shape, kind in outputs.values()],
        scratch_shapes=list(scratch.values()),
        input_output_aliases=aliases,
        compiler_params=pltpu.CompilerParams(vmem_limit_bytes=LIMIT),
        cost_estimate=pl.CostEstimate(
            flops=flops // 1024, bytes_accessed=1024, transcendentals=flops // 1024
        ),
        name=body.__name__,
    )(*operands)
    return SimpleNamespace(**dict(zip(outputs, results)))


def copy_rows(source, target, sems, copies, parts=1):
    rows = source.shape[0] // parts
    for part in range(parts):
        piece = pl.ds(part * rows, rows)
        copies.append(
            pltpu.make_async_copy(source.at[piece], target.at[piece], sems.at[len(copies)])
        )
        copies[-1].start()


def chunk_at(step, chunks):
    return lax.axis_index("seq") ^ (chunks - 1 - step)


def chunk_columns(z, step):
    return pl.ds(pl.multiple_of(chunk_at(step, z.chunks) * z.width, HEAD_SIZE), z.width)


def pair_columns(z, step):
    return pl.ds(pl.multiple_of(chunk_at(step, z.chunks) * PAIR, HEAD_SIZE), PAIR)


def split_first(z, refs):
    copies = []
    source = refs.upstream.at[:, chunk_columns(z, 0)]
    copy_rows(source, refs.piece, refs.sems, copies, COPIES)
    for copy in copies:
        copy.wait()


def split_second(z, refs):
    copies = []
    source = refs.upstream.at[:, chunk_columns(z, 1)]
    copy_rows(source, refs.piece, refs.sems, copies, COPIES)
    copy_rows(refs.matrix, refs.matrix_copy, refs.sems, copies, COPIES)
    copy_rows(refs.pairs, refs.pairs_copy, refs.sems, copies, COPIES)
    for copy in copies:
        copy.wait()


def split_rest(z, refs):
    copies = []
    pieces = listed(refs, "piece")
    for step, piece in zip(range(2, z.chunks - 1), pieces):
        copy_rows(refs.upstream.at[:, chunk_columns(z, step)], piece, refs.sems, copies, COPIES)
    for index, piece in enumerate(pieces[-BLOCKS:]):
        rows = pl.ds(index * z.block, z.block)
        source = refs.upstream.at[rows, chunk_columns(z, z.chunks - 1)]
        copy_rows(source, piece, refs.sems, copies, COPIES)
    for copy in copies:
        copy.wait()


def stacked(array, rows):
    heads = array.shape[1] // HEAD_SIZE
    parts = [array[rows, head * HEAD_SIZE : (head + 1) * HEAD_SIZE] for head in range(heads)]
    return jnp.concatenate(parts, axis=0)


def seen_rows(z, refs, step, second):
    per_head = z.chunks // HK
    chunk = chunk_at(step, z.chunks)
    place = lax.div(chunk, per_head) if per_head > 1 else chunk
    start = pl.multiple_of(place * PAIR + second * HEAD_SIZE, HEAD_SIZE)
    columns = pl.ds(start, HEAD_SIZE)
    return jnp.concatenate([refs.halo[: z.span, columns], refs.own[:, columns]], axis=0)


def windowed(z, array, index):
    return array[index * z.block : index * z.block + z.window]


def softmax_blocks(z, refs, step, matrix, keys):
    queries = refs.fq[:, chunk_columns(z, step)].astype(jnp.float32)
    queries = (queries + dot(refs.at[...], matrix, 0, 0)).astype(jnp.bfloat16)
    stacks, probs = [], []
    for index in range(BLOCKS):
        stack = stacked(queries, slice(index * z.block, (index + 1) * z.block))
        hidden = refs.bias[index * z.window : (index + 1) * z.window]
        scores = dot(windowed(z, keys, index), stack, 1, 1) * SCALE
        scores += jnp.concatenate([hidden] * (stack.shape[0] // hidden.shape[1]), axis=1)
        shifted = jnp.exp(scores - jnp.max(scores, axis=0, keepdims=True))
        stacks.append(stack)
        probs.append(shifted * (1.0 / jnp.sum(shifted, axis=0, keepdims=True)))
    return stacks, probs


def score_grads(z, index, probs, keys, values, cot_stack):
    dprobs = dot(windowed(z, values, index), cot_stack, 1, 1)
    deltas = jnp.sum(probs * dprobs, axis=0, keepdims=True)
    dscores = (probs * (dprobs - deltas)).astype(jnp.bfloat16)
    return dscores, (dot(dscores, windowed(z, keys, index), 0, 0) * SCALE).astype(jnp.bfloat16)


def unstack(z, grad_stack, target, start):
    for head in range(grad_stack.shape[0] // z.block):
        columns = slice(head * HEAD_SIZE, (head + 1) * HEAD_SIZE)
        target[start : start + z.block, columns] = grad_stack[head * z.block : (head + 1) * z.block]


def pair_terms(z, index, dscores, probs, query_stack, cot_stack):
    key_term = dot(dscores, query_stack, 1, 0) * SCALE
    value_term = dot(probs.astype(jnp.bfloat16), cot_stack, 1, 0)
    term = jnp.concatenate([key_term, value_term], axis=1)
    start = index * z.block
    rest = z.span + z.rows - z.window - start
    if start > 0:
        term = jnp.concatenate([jnp.zeros((start, PAIR), jnp.float32), term], axis=0)
    if rest > 0:
        term = jnp.concatenate([term, jnp.zeros((rest, PAIR), jnp.float32)], axis=0)
    return term


def padded(z, grad, index):
    blank = jnp.zeros((z.block, grad.shape[1]), grad.dtype)
    return jnp.concatenate([grad if place == index else blank for place in range(BLOCKS)], axis=0)


def forward(z, refs):
    step = z.chunks - 1
    keys = seen_rows(z, refs, step, 0)
    stacks, probs = softmax_blocks(z, refs, step, refs.up[...], keys)
    for index in range(BLOCKS):
        listed(refs, "stack")[index][...] = stacks[index]
        listed(refs, "probs")[index][...] = probs[index]


def whole(step, z, refs):
    copies = []
    if hasattr(refs, "pending"):
        copy_rows(refs.pending, refs.dq.at[:, chunk_columns(z, step - 1)], refs.sems, copies)
    matrix = refs.up[...]
    keys, values = seen_rows(z, refs, step, 0), seen_rows(z, refs, step, 1)
    stacks, probs = softmax_blocks(z, refs, step, matrix, keys)
    pair_total = 0.0
    for index in range(BLOCKS):
        start = index * z.block
        cot_stack = stacked(refs.cot, slice(start, start + z.block))
        dscores, grad_stack = score_grads(z, index, probs[index], keys, values, cot_stack)
        unstack(z, grad_stack, refs.grad, start)
        pair_total += pair_terms(z, index, dscores, probs[index], stacks[index], cot_stack)
    grad = refs.grad[...]
    weight = dot(refs.at[...], grad, 1, 0)
    for term in listed(refs, "term"):
        weight += term[...].astype(jnp.float32)
    refs.weight[...] = weight.astype(jnp.bfloat16)
    refs.halo_part[...] = pair_total[: z.span].astype(refs.halo_part.dtype)
    refs.own_part[...] = pair_total[z.span :]
    input_grad = dot(matrix, grad, 1, 1)
    if step > 0:
        input_grad += refs.input_sum[...]
    refs.input_grad[...] = input_grad
    for copy in copies:
        copy.wait()


def front(z, refs):
    copies = []
    step = z.chunks - 1
    for place, grad in enumerate(listed(refs, "pending")):
        target = refs.dq.at[:, chunk_columns(z, step - BLOCKS + place)]
        copy_rows(grad, target, refs.sems, copies)
    keys, values = seen_rows(z, refs, step, 0), seen_rows(z, refs, step, 1)
    probs = refs.probs[...]
    cot_stack = stacked(refs.cot, slice(0, z.block))
    dscores, grad_stack = score_grads(z, 0, probs, keys, values, cot_stack)
    unstack(z, grad_stack, refs.grad, 0)
    pair_total = pair_terms(z, 0, dscores, probs, refs.stack[...], cot_stack)
    kind = refs.halo_grads.dtype
    for place, part in enumerate(listed(refs, "halo_part")):
        refs.halo_grads[:, pair_columns(z, place)] = part[...]
    refs.halo_grads[:, pair_columns(z, step)] = pair_total[: z.span].astype(kind)
    refs.own_part[...] = pair_total[z.span :]
    grad = padded(z, refs.grad[...], 0)
    weight = dot(refs.at[...], grad, 1, 0)
    for term in listed(refs, "term"):
        weight += term[...].astype(jnp.float32)
    refs.weight_part[...] = weight
    refs.input_grad[...] = refs.input_sum[...] + dot(refs.up[...], grad, 1, 1)
    for copy in copies:
        copy.wait()


def back(z, refs):
    step = z.chunks - 1
    keys, values = seen_rows(z, refs, step, 0), seen_rows(z, refs, step, 1)
    cot_stack = stacked(refs.cot, slice(0, z.block))
    dscores, grad_stack = score_grads(z, 1, refs.probs[...], keys, values, cot_stack)
    refs.dscores[...] = dscores
    unstack(z, grad_stack, refs.grad, 0)
    weight = refs.weight_part[...] + dot(refs.at[...], padded(z, refs.grad[...], 1), 1, 0)
    for term in listed(refs, "term"):
        weight += term[...].astype(jnp.float32)
    refs.total[...] = weight.astype(jnp.bfloat16)
    shares = listed(refs, "share")
    rows = z.rank // len(shares)
    for away, share in enumerate(shares):
        target = lax.rem(lax.axis_index("dp") + away, len(shares))
        share[...] = refs.total[pl.ds(pl.multiple_of(target * rows, rows), rows)]


def finish(z, refs):
    copies = []
    step = z.chunks - 1
    for index, grad in enumerate(listed(refs, "pending")):
        target = refs.dq.at[pl.ds(index * z.block, z.block), chunk_columns(z, step)]
        copy_rows(grad, target, refs.sems, copies)
    cot_stack = stacked(refs.cot, slice(0, z.block))
    pair_total = pair_terms(z, 1, refs.dscores[...], refs.probs[...], refs.stack[...], cot_stack)
    parts = [part[...] for part in listed(refs, "own_part")]
    parts[step] += pair_total[z.span :]
    low = z.rows - z.span
    for place, part in enumerate(parts):
        columns = pair_columns(z, place)
        if hasattr(refs, "halo_back"):
            refs.pair_grads[:low, columns] = part[:low].astype(jnp.bfloat16)
            part = part[low:] + refs.halo_back[:, columns].astype(jnp.float32)
            refs.pair_grads[low:, columns] = part.astype(jnp.bfloat16)
        else:
            refs.own_grads[:, columns] = part
    refs.share_out[...] = refs.share[...]
    grad = padded(z, refs.pending1[...], 1)
    input_grad = refs.input_sum[...] + dot(refs.up[...], grad, 1, 1)
    refs.input_grad[...] = input_grad.astype(jnp.bfloat16)
    for copy in copies:
        copy.wait()


def per_device(
    frozen_queries, key_value_pairs, adapter_input, adapter_up_matrix, upstream, document_index
):
    bf16, f32 = jnp.bfloat16, jnp.float32
    chunks = lax.axis_size("seq")
    packs = lax.axis_size("dp")
    place = lax.axis_index("seq")
    rows = frozen_queries.shape[2]
    columns = QUERY_HEADS * HEAD_SIZE
    block = rows // BLOCKS
    span = document_index.shape[2] // SPAN_PARTS
    window = span + block
    width = columns // chunks
    rank = adapter_input.shape[3]
    stack_rows = width // HEAD_SIZE * block
    per_head = chunks // HK
    last = chunks - 1
    z = SimpleNamespace(
        chunks=chunks, rows=rows, block=block, span=span, window=window, width=width, rank=rank
    )
    flops = 10 * stack_rows * window * HEAD_SIZE

    pieces = []
    left = span
    while left > 0:
        pieces.append((len(pieces) + 1, min(rows, left)))
        left -= rows

    own = key_value_pairs[0, 0]
    matrix = adapter_up_matrix[0]
    cotangents = upstream[0, 0]

    def sems(count):
        return dict(sems=pltpu.SemaphoreType.DMA((count,)))

    piece = ((rows, width), bf16)
    first = run(split_first, z, dict(upstream=cotangents), dict(piece=piece), sems(COPIES)).piece
    cots = [passed_along(first, "section", -1)]
    outputs = dict(
        piece=piece, matrix_copy=((rank, width), bf16), pairs_copy=(own.shape, bf16)
    )
    second = run(
        split_second,
        z,
        dict(upstream=cotangents, pairs=own, matrix=matrix, after=first),
        outputs,
        sems(COPIES * len(outputs)),
    )
    cots.append(passed_along(second.piece, "section", -1))
    own, matrix = second.pairs_copy, second.matrix_copy
    outputs = numbered("piece", [piece] * (last - 2) + [((block, width), bf16)] * BLOCKS)
    rest = run(
        split_rest,
        z,
        dict(upstream=cotangents, after=second.piece),
        outputs,
        sems(COPIES * len(outputs)),
    )
    held = listed(rest, "piece")
    cots.append(passed_along(held[0], "section", -1))
    halo = [passed_along(own[rows - count :], "seq", distance) for distance, count in pieces]
    halo = jnp.concatenate(halo[::-1], axis=0)
    ups = {0: matrix}
    for away in sorted(range(1, chunks), key=low_bit, reverse=True):
        bit = low_bit(away)
        ups[away] = swapped(ups[away - bit], "seq", bit)

    numbers = jnp.concatenate([jnp.full((span,), -1, jnp.int32), document_index[0, 0]])
    numbers = lax.dynamic_slice_in_dim(numbers, place * rows, span + rows, 0)
    reach = jnp.arange(window, dtype=jnp.int32)[:, None] <= (
        jnp.arange(block, dtype=jnp.int32)[None, :] + span
    )
    bias = []
    for start in range(0, rows, block):
        seen = numbers[start : start + window, None]
        same = seen == numbers[None, start + span : start + span + block]
        bias.append(jnp.where(same & reach, 0.0, -jnp.inf))
    bias = jnp.concatenate(bias, axis=0).astype(f32)
    bias = jnp.concatenate([bias, bias], axis=1)
    fq = frozen_queries[0, 0]
    at = adapter_input[0, 0].T

    outputs = numbered("stack", [((stack_rows, HEAD_SIZE), bf16)] * BLOCKS)
    outputs |= numbered("probs", [((window, stack_rows), f32)] * BLOCKS)
    outputs.update(held=(held[1].shape, bf16))
    inputs = dict(fq=fq, at=at, up=matrix, halo=halo, own=own, bias=bias, held_in=held[1])
    ahead = run(forward, z, inputs, outputs, {}, flops)
    cots.append(passed_along(ahead.held, "section", -1))

    halo_type = bf16 if per_head == 1 else f32
    halo_part, own_part = ((span, PAIR), halo_type), ((rows, PAIR), f32)
    dq_shape = ((rows, columns), bf16)
    input_shape = ((rank, rows), f32)
    terms = {away: [] for away in range(chunks)}
    grads, halo_parts, own_parts = [], [], []
    state = None
    for step in range(last):
        away = last - step
        inputs = dict(fq=fq, at=at, halo=halo, own=own, bias=bias, cot=cots[step], up=ups[away])
        inputs |= numbered("term", terms[away])
        outputs = dict(
            halo_part=halo_part,
            own_part=own_part,
            input_grad=input_shape,
            grad=piece,
            weight=((rank, width), bf16),
        )
        if step > 0:
            inputs.update(input_sum=state.input_grad)
        else:
            inputs.update(after=ahead.stack0)
        if 0 < step < last - 1:
            inputs.update(pending=grads[-1])
            outputs.update(dq=dq_shape)
            if step > 1:
                inputs.update(dq_in=dq)
        if step + 2 < len(held):
            inputs.update(held_in=held[step + 2])
            outputs.update(held=(held[step + 2].shape, bf16))
        body = functools.partial(whole, step)
        body.__name__ = whole.__name__
        state = run(body, z, inputs, outputs, sems(1), 2 * flops)
        grads.append(state.grad)
        halo_parts.append(state.halo_part)
        own_parts.append(state.own_part)
        dq = getattr(state, "dq", None) if step < last - 1 else dq
        if step + 2 < len(held):
            cots.append(passed_along(state.held, "section", -1))
        bit = low_bit(away)
        terms[away - bit].append(swapped(state.weight, "seq", bit))

    common = dict(at=at, up=matrix, halo=halo, own=own)
    outputs = dict(
        dq=dq_shape,
        halo_grads=((span, chunks * PAIR), halo_type),
        own_part=own_part,
        weight_part=((rank, width), f32),
        input_grad=input_shape,
        grad=((block, width), bf16),
    )
    early = run(
        front,
        z,
        common
        | dict(
            cot=cots[last],
            stack=ahead.stack0,
            probs=ahead.probs0,
            dq_in=dq,
            input_sum=state.input_grad,
        )
        | numbered("halo_part", halo_parts)
        | numbered("pending", grads[-BLOCKS:])
        | numbered("term", terms[0][:-1]),
        outputs,
        sems(BLOCKS),
        flops,
    )
    halo_grads = early.halo_grads
    if per_head > 1:
        halo_grads = jnp.sum(halo_grads.reshape(span, HK, per_head, PAIR), axis=2)
        halo_grads = halo_grads.astype(bf16).reshape(span, HK * PAIR)
    backs = []
    stop = span
    for distance, count in pieces:
        backs.append(passed_along(halo_grads[stop - count : stop], "seq", -distance))
        stop -= count

    outputs = dict(grad=((block, width), bf16), dscores=((window, stack_rows), bf16))
    outputs |= numbered("share", [((rank // packs, width), bf16)] * packs)
    late = run(
        back,
        z,
        common
        | dict(cot=cots[last + 1], probs=ahead.probs1, weight_part=early.weight_part)
        | numbered("term", terms[0][-1:]),
        outputs,
        dict(total=pltpu.VMEM((rank, width), bf16)),
        flops,
    )
    shares = listed(late, "share")
    shares[1:] = [passed_along(shares[away], "dp", away) for away in range(1, packs)]

    merged = per_head == 1 and len(pieces) == 1
    outputs = dict(dq=dq_shape, input_grad=((rank, rows), bf16))
    outputs.update(share_out=((rank // packs, width), bf16))
    inputs = dict(
        at=at,
        up=matrix,
        cot=cots[last + 1],
        stack=ahead.stack1,
        probs=ahead.probs1,
        dscores=late.dscores,
        input_sum=early.input_grad,
        dq_in=early.dq,
        share=shares[0],
    )
    inputs |= numbered("own_part", own_parts + [early.own_part])
    if merged:
        inputs.update(halo_back=backs[0])
        outputs.update(pair_grads=((rows, HK * PAIR), bf16))
    else:
        outputs.update(own_grads=((rows, chunks * PAIR), f32))
    final = run(
        finish,
        z,
        inputs | numbered("pending", [early.grad, late.grad]),
        outputs,
        sems(BLOCKS),
        flops,
    )
    weight_share = final.share_out.astype(f32)
    for share in shares[2:0:-1] + shares[3:]:
        weight_share += share.astype(f32)
    if merged:
        pair_grads = final.pair_grads
    else:
        own_grads = jnp.sum(final.own_grads.reshape(rows, HK, per_head, PAIR), axis=2)
        own_grads = own_grads.reshape(rows, HK * PAIR)
        for rows_back in backs:
            low = rows - rows_back.shape[0]
            own_grads = own_grads.at[low:].add(rows_back.astype(f32))
        pair_grads = own_grads.astype(bf16)

    return (
        final.dq[None, None],
        pair_grads[None, None],
        final.input_grad.T[None, None],
        weight_share[None],
    )


def solution(mesh):
    placed = (
        P("section", "dp", "seq", None),
        P("section", "dp", "seq", None),
        P("section", "dp", "seq", None),
        P("section", None, "seq"),
        P("section", "dp", "seq", None),
        P("section", "dp", None),
    )
    return jax.shard_map(
        per_device,
        mesh=mesh,
        in_specs=placed,
        out_specs=(
            P("section", "dp", "seq", None),
            P("section", "dp", "seq", None),
            P("section", "dp", "seq", None),
            P("section", "dp", "seq"),
        ),
        check_vma=False,
    )
```

```python
import functools
import math
from types import SimpleNamespace

import jax
import jax.numpy as jnp
from jax import lax
from jax.experimental import pallas as pl
from jax.experimental.pallas import tpu as pltpu
from jax.sharding import PartitionSpec as P

QUERY_HEADS = 32
HK = 4
HEAD_SIZE = 128
PAIR = 2 * HEAD_SIZE
SCALE = 1.0 / math.sqrt(HEAD_SIZE)
SPAN_PARTS = 8
BLOCKS = 2
COPIES = 4
LIMIT = 16 * 1024 * 1024
IN = "_in"
IN_HBM = ("upstream", "pairs", "matrix", "dq", "dq" + IN)
ANYWHERE = ("held", "held" + IN, "after")
VMEM = pl.BlockSpec(memory_space=pltpu.VMEM)
HBM = pl.BlockSpec(memory_space=pltpu.HBM)
ANY = pl.BlockSpec(memory_space=pl.ANY)


def passed_along(value, axis, steps):
    count = lax.axis_size(axis)
    pairs = [(source, (source + steps) % count) for source in range(count)]
    return lax.ppermute(value, axis, pairs)


def swapped(value, axis, bit):
    pairs = [(source, source ^ bit) for source in range(lax.axis_size(axis))]
    return lax.ppermute(value, axis, pairs)


def dot(left, right, left_dim, right_dim):
    return lax.dot_general(
        left, right, (((left_dim,), (right_dim,)), ((), ())), preferred_element_type=jnp.float32
    )


def low_bit(number):
    return number & -number


def numbered(name, arrays):
    return {name + str(index): array for index, array in enumerate(arrays)}


def listed(refs, name):
    found = []
    while hasattr(refs, name + str(len(found))):
        found.append(getattr(refs, name + str(len(found))))
    return found


def spec_of(name):
    return HBM if name in IN_HBM else ANY if name in ANYWHERE else VMEM


def run(body, sizes, inputs, outputs, scratch, flops=0):
    names = list(inputs) + list(outputs) + list(scratch)

    def kernel(*refs):
        body(sizes, SimpleNamespace(**dict(zip(names, refs))))

    operands = [
        pltpu.with_memory_space_constraint(array, pltpu.HBM) if name in IN_HBM[:3] else array
        for name, array in inputs.items()
    ]
    places = list(inputs)
    aliases = {
        places.index(name + IN): index
        for index, name in enumerate(outputs)
        if name + IN in inputs
    }
    results = pl.pallas_call(
        kernel,
        in_specs=[spec_of(name) for name in inputs],
        out_specs=[spec_of(name) for name in outputs],
        out_shape=[jax.ShapeDtypeStruct(shape, kind) for shape, kind in outputs.values()],
        scratch_shapes=list(scratch.values()),
        input_output_aliases=aliases,
        compiler_params=pltpu.CompilerParams(vmem_limit_bytes=LIMIT),
        cost_estimate=pl.CostEstimate(
            flops=flops // 1024, bytes_accessed=1024, transcendentals=flops // 1024
        ),
        name=body.__name__,
    )(*operands)
    return SimpleNamespace(**dict(zip(outputs, results)))


def copy_rows(source, target, sems, copies, parts=1):
    rows = source.shape[0] // parts
    for part in range(parts):
        piece = pl.ds(part * rows, rows)
        copies.append(
            pltpu.make_async_copy(source.at[piece], target.at[piece], sems.at[len(copies)])
        )
        copies[-1].start()


def chunk_at(step, chunks):
    return lax.axis_index("seq") ^ (chunks - 1 - step)


def chunk_columns(z, step):
    return pl.ds(pl.multiple_of(chunk_at(step, z.chunks) * z.width, HEAD_SIZE), z.width)


def pair_columns(z, step):
    return pl.ds(pl.multiple_of(chunk_at(step, z.chunks) * PAIR, HEAD_SIZE), PAIR)


def split_first(z, refs):
    copies = []
    source = refs.upstream.at[pl.ds(0, z.block), chunk_columns(z, 0)]
    copy_rows(source, refs.piece, refs.sems, copies, COPIES)
    for copy in copies:
        copy.wait()


def split_second(z, refs):
    copies = []
    source = refs.upstream.at[pl.ds(z.block, z.block), chunk_columns(z, 0)]
    copy_rows(source, refs.second, refs.sems, copies, COPIES)
    source = refs.upstream.at[:, chunk_columns(z, 1)]
    copy_rows(source, refs.piece, refs.sems, copies, COPIES)
    copy_rows(refs.matrix, refs.matrix_copy, refs.sems, copies, COPIES)
    copy_rows(refs.pairs, refs.pairs_copy, refs.sems, copies, COPIES)
    for copy in copies:
        copy.wait()


def split_rest(z, refs):
    copies = []
    pieces = listed(refs, "piece")
    for step, piece in zip(range(2, z.chunks - 1), pieces):
        copy_rows(refs.upstream.at[:, chunk_columns(z, step)], piece, refs.sems, copies, COPIES)
    for index, piece in enumerate(pieces[-BLOCKS:]):
        rows = pl.ds(index * z.block, z.block)
        source = refs.upstream.at[rows, chunk_columns(z, z.chunks - 1)]
        copy_rows(source, piece, refs.sems, copies, COPIES)
    for copy in copies:
        copy.wait()


def stacked(array, rows):
    heads = array.shape[1] // HEAD_SIZE
    parts = [array[rows, head * HEAD_SIZE : (head + 1) * HEAD_SIZE] for head in range(heads)]
    return jnp.concatenate(parts, axis=0)


def seen_rows(z, refs, step, second):
    per_head = z.chunks // HK
    chunk = chunk_at(step, z.chunks)
    place = lax.div(chunk, per_head) if per_head > 1 else chunk
    start = pl.multiple_of(place * PAIR + second * HEAD_SIZE, HEAD_SIZE)
    columns = pl.ds(start, HEAD_SIZE)
    return jnp.concatenate([refs.halo[: z.span, columns], refs.own[:, columns]], axis=0)


def windowed(z, array, index):
    return array[index * z.block : index * z.block + z.window]


def softmax_blocks(z, refs, step, matrix, keys):
    queries = refs.fq[:, chunk_columns(z, step)].astype(jnp.float32)
    queries = (queries + dot(refs.at[...], matrix, 0, 0)).astype(jnp.bfloat16)
    stacks, probs = [], []
    for index in range(BLOCKS):
        stack = stacked(queries, slice(index * z.block, (index + 1) * z.block))
        hidden = refs.bias[index * z.window : (index + 1) * z.window]
        scores = dot(windowed(z, keys, index), stack, 1, 1) * SCALE
        scores += jnp.concatenate([hidden] * (stack.shape[0] // hidden.shape[1]), axis=1)
        shifted = jnp.exp(scores - jnp.max(scores, axis=0, keepdims=True))
        stacks.append(stack)
        probs.append(shifted * (1.0 / jnp.sum(shifted, axis=0, keepdims=True)))
    return stacks, probs


def score_grads(z, index, probs, keys, values, cot_stack):
    dprobs = dot(windowed(z, values, index), cot_stack, 1, 1)
    deltas = jnp.sum(probs * dprobs, axis=0, keepdims=True)
    dscores = (probs * (dprobs - deltas)).astype(jnp.bfloat16)
    return dscores, (dot(dscores, windowed(z, keys, index), 0, 0) * SCALE).astype(jnp.bfloat16)


def unstack(z, grad_stack, target, start):
    for head in range(grad_stack.shape[0] // z.block):
        columns = slice(head * HEAD_SIZE, (head + 1) * HEAD_SIZE)
        target[start : start + z.block, columns] = grad_stack[head * z.block : (head + 1) * z.block]


def pair_terms(z, index, dscores, probs, query_stack, cot_stack):
    key_term = dot(dscores, query_stack, 1, 0) * SCALE
    value_term = dot(probs.astype(jnp.bfloat16), cot_stack, 1, 0)
    term = jnp.concatenate([key_term, value_term], axis=1)
    start = index * z.block
    rest = z.span + z.rows - z.window - start
    if start > 0:
        term = jnp.concatenate([jnp.zeros((start, PAIR), jnp.float32), term], axis=0)
    if rest > 0:
        term = jnp.concatenate([term, jnp.zeros((rest, PAIR), jnp.float32)], axis=0)
    return term


def padded(z, grad, index):
    blank = jnp.zeros((z.block, grad.shape[1]), grad.dtype)
    return jnp.concatenate([grad if place == index else blank for place in range(BLOCKS)], axis=0)


def forward(z, refs):
    step = z.chunks - 1
    keys = seen_rows(z, refs, step, 0)
    stacks, probs = softmax_blocks(z, refs, step, refs.up[...], keys)
    for index in range(BLOCKS):
        listed(refs, "stack")[index][...] = stacks[index]
        listed(refs, "probs")[index][...] = probs[index]


def whole(step, z, refs):
    copies = []
    if hasattr(refs, "pending"):
        copy_rows(refs.pending, refs.dq.at[:, chunk_columns(z, step - 1)], refs.sems, copies)
    matrix = refs.up[...]
    keys, values = seen_rows(z, refs, step, 0), seen_rows(z, refs, step, 1)
    stacks, probs = softmax_blocks(z, refs, step, matrix, keys)
    pair_total = 0.0
    for index in range(BLOCKS):
        start = index * z.block
        if step > 0:
            cot_stack = stacked(refs.cot, slice(start, start + z.block))
        else:
            cot_stack = stacked((refs.cot, refs.second)[index], slice(0, z.block))
        dscores, grad_stack = score_grads(z, index, probs[index], keys, values, cot_stack)
        unstack(z, grad_stack, refs.grad, start)
        pair_total += pair_terms(z, index, dscores, probs[index], stacks[index], cot_stack)
    grad = refs.grad[...]
    weight = dot(refs.at[...], grad, 1, 0)
    for term in listed(refs, "term"):
        weight += term[...].astype(jnp.float32)
    refs.weight[...] = weight.astype(jnp.bfloat16)
    refs.halo_part[...] = pair_total[: z.span].astype(refs.halo_part.dtype)
    refs.own_part[...] = pair_total[z.span :]
    input_grad = dot(matrix, grad, 1, 1)
    if step > 0:
        input_grad += refs.input_sum[...]
    refs.input_grad[...] = input_grad
    for copy in copies:
        copy.wait()


def front(z, refs):
    copies = []
    step = z.chunks - 1
    for place, grad in enumerate(listed(refs, "pending")):
        target = refs.dq.at[:, chunk_columns(z, step - BLOCKS + place)]
        copy_rows(grad, target, refs.sems, copies)
    keys, values = seen_rows(z, refs, step, 0), seen_rows(z, refs, step, 1)
    probs = refs.probs[...]
    cot_stack = stacked(refs.cot, slice(0, z.block))
    dscores, grad_stack = score_grads(z, 0, probs, keys, values, cot_stack)
    unstack(z, grad_stack, refs.grad, 0)
    pair_total = pair_terms(z, 0, dscores, probs, refs.stack[...], cot_stack)
    kind = refs.halo_grads.dtype
    for place, part in enumerate(listed(refs, "halo_part")):
        refs.halo_grads[:, pair_columns(z, place)] = part[...]
    refs.halo_grads[:, pair_columns(z, step)] = pair_total[: z.span].astype(kind)
    refs.own_part[...] = pair_total[z.span :]
    grad = padded(z, refs.grad[...], 0)
    weight = dot(refs.at[...], grad, 1, 0)
    for term in listed(refs, "term"):
        weight += term[...].astype(jnp.float32)
    refs.weight_part[...] = weight
    refs.input_grad[...] = refs.input_sum[...] + dot(refs.up[...], grad, 1, 1)
    for copy in copies:
        copy.wait()


def back(z, refs):
    step = z.chunks - 1
    keys, values = seen_rows(z, refs, step, 0), seen_rows(z, refs, step, 1)
    cot_stack = stacked(refs.cot, slice(0, z.block))
    dscores, grad_stack = score_grads(z, 1, refs.probs[...], keys, values, cot_stack)
    refs.dscores[...] = dscores
    unstack(z, grad_stack, refs.grad, 0)
    weight = refs.weight_part[...] + dot(refs.at[...], padded(z, refs.grad[...], 1), 1, 0)
    for term in listed(refs, "term"):
        weight += term[...].astype(jnp.float32)
    refs.total[...] = weight.astype(jnp.bfloat16)
    shares = listed(refs, "share")
    rows = z.rank // len(shares)
    for away, share in enumerate(shares):
        target = lax.rem(lax.axis_index("dp") + away, len(shares))
        share[...] = refs.total[pl.ds(pl.multiple_of(target * rows, rows), rows)]


def finish(z, refs):
    copies = []
    step = z.chunks - 1
    for index, grad in enumerate(listed(refs, "pending")):
        target = refs.dq.at[pl.ds(index * z.block, z.block), chunk_columns(z, step)]
        copy_rows(grad, target, refs.sems, copies)
    cot_stack = stacked(refs.cot, slice(0, z.block))
    pair_total = pair_terms(z, 1, refs.dscores[...], refs.probs[...], refs.stack[...], cot_stack)
    parts = [part[...] for part in listed(refs, "own_part")]
    parts[step] += pair_total[z.span :]
    low = z.rows - z.span
    for place, part in enumerate(parts):
        columns = pair_columns(z, place)
        if hasattr(refs, "halo_back"):
            refs.pair_grads[:low, columns] = part[:low].astype(jnp.bfloat16)
            part = part[low:] + refs.halo_back[:, columns].astype(jnp.float32)
            refs.pair_grads[low:, columns] = part.astype(jnp.bfloat16)
        else:
            refs.own_grads[:, columns] = part
    refs.share_out[...] = refs.share[...]
    grad = padded(z, refs.pending1[...], 1)
    input_grad = refs.input_sum[...] + dot(refs.up[...], grad, 1, 1)
    refs.input_grad[...] = input_grad.astype(jnp.bfloat16)
    for copy in copies:
        copy.wait()


def per_device(
    frozen_queries, key_value_pairs, adapter_input, adapter_up_matrix, upstream, document_index
):
    bf16, f32 = jnp.bfloat16, jnp.float32
    chunks = lax.axis_size("seq")
    packs = lax.axis_size("dp")
    place = lax.axis_index("seq")
    rows = frozen_queries.shape[2]
    columns = QUERY_HEADS * HEAD_SIZE
    block = rows // BLOCKS
    span = document_index.shape[2] // SPAN_PARTS
    window = span + block
    width = columns // chunks
    rank = adapter_input.shape[3]
    stack_rows = width // HEAD_SIZE * block
    per_head = chunks // HK
    last = chunks - 1
    z = SimpleNamespace(
        chunks=chunks, rows=rows, block=block, span=span, window=window, width=width, rank=rank
    )
    flops = 10 * stack_rows * window * HEAD_SIZE

    pieces = []
    left = span
    while left > 0:
        pieces.append((len(pieces) + 1, min(rows, left)))
        left -= rows

    own = key_value_pairs[0, 0]
    matrix = adapter_up_matrix[0]
    cotangents = upstream[0, 0]

    def sems(count):
        return dict(sems=pltpu.SemaphoreType.DMA((count,)))

    piece = ((rows, width), bf16)
    half = ((block, width), bf16)
    first = run(split_first, z, dict(upstream=cotangents), dict(piece=half), sems(COPIES)).piece
    cots = [passed_along(first, "section", -1)]
    outputs = dict(
        second=half, piece=piece, matrix_copy=((rank, width), bf16), pairs_copy=(own.shape, bf16)
    )
    second = run(
        split_second,
        z,
        dict(upstream=cotangents, pairs=own, matrix=matrix, after=first),
        outputs,
        sems(COPIES * len(outputs)),
    )
    second_half = passed_along(second.second, "section", -1)
    cots.append(passed_along(second.piece, "section", -1))
    own, matrix = second.pairs_copy, second.matrix_copy
    outputs = numbered("piece", [piece] * (last - 2) + [((block, width), bf16)] * BLOCKS)
    rest = run(
        split_rest,
        z,
        dict(upstream=cotangents, after=second.piece),
        outputs,
        sems(COPIES * len(outputs)),
    )
    held = listed(rest, "piece")
    cots.append(passed_along(held[0], "section", -1))
    halo = [passed_along(own[rows - count :], "seq", distance) for distance, count in pieces]
    halo = jnp.concatenate(halo[::-1], axis=0)
    ups = {0: matrix}
    for away in sorted(range(1, chunks), key=low_bit, reverse=True):
        bit = low_bit(away)
        ups[away] = swapped(ups[away - bit], "seq", bit)

    numbers = jnp.concatenate([jnp.full((span,), -1, jnp.int32), document_index[0, 0]])
    numbers = lax.dynamic_slice_in_dim(numbers, place * rows, span + rows, 0)
    reach = jnp.arange(window, dtype=jnp.int32)[:, None] <= (
        jnp.arange(block, dtype=jnp.int32)[None, :] + span
    )
    bias = []
    for start in range(0, rows, block):
        seen = numbers[start : start + window, None]
        same = seen == numbers[None, start + span : start + span + block]
        bias.append(jnp.where(same & reach, 0.0, -jnp.inf))
    bias = jnp.concatenate(bias, axis=0).astype(f32)
    bias = jnp.concatenate([bias, bias], axis=1)
    fq = frozen_queries[0, 0]
    at = adapter_input[0, 0].T

    outputs = numbered("stack", [((stack_rows, HEAD_SIZE), bf16)] * BLOCKS)
    outputs |= numbered("probs", [((window, stack_rows), f32)] * BLOCKS)
    outputs.update(held=(held[1].shape, bf16))
    inputs = dict(fq=fq, at=at, up=matrix, halo=halo, own=own, bias=bias, held_in=held[1])
    ahead = run(forward, z, inputs, outputs, {}, flops)
    cots.append(passed_along(ahead.held, "section", -1))

    halo_type = bf16 if per_head == 1 else f32
    halo_part, own_part = ((span, PAIR), halo_type), ((rows, PAIR), f32)
    dq_shape = ((rows, columns), bf16)
    input_shape = ((rank, rows), f32)
    terms = {away: [] for away in range(chunks)}
    grads, halo_parts, own_parts = [], [], []
    state = None
    for step in range(last):
        away = last - step
        inputs = dict(fq=fq, at=at, halo=halo, own=own, bias=bias, cot=cots[step], up=ups[away])
        inputs |= numbered("term", terms[away])
        outputs = dict(
            halo_part=halo_part,
            own_part=own_part,
            input_grad=input_shape,
            grad=piece,
            weight=((rank, width), bf16),
        )
        if step > 0:
            inputs.update(input_sum=state.input_grad)
        else:
            inputs.update(after=ahead.stack0, second=second_half)
        if 0 < step < last - 1:
            inputs.update(pending=grads[-1])
            outputs.update(dq=dq_shape)
            if step > 1:
                inputs.update(dq_in=dq)
        if step + 2 < len(held):
            inputs.update(held_in=held[step + 2])
            outputs.update(held=(held[step + 2].shape, bf16))
        body = functools.partial(whole, step)
        body.__name__ = whole.__name__
        state = run(body, z, inputs, outputs, sems(1), 2 * flops)
        grads.append(state.grad)
        halo_parts.append(state.halo_part)
        own_parts.append(state.own_part)
        dq = getattr(state, "dq", None) if step < last - 1 else dq
        if step + 2 < len(held):
            cots.append(passed_along(state.held, "section", -1))
        bit = low_bit(away)
        terms[away - bit].append(swapped(state.weight, "seq", bit))

    common = dict(at=at, up=matrix, halo=halo, own=own)
    outputs = dict(
        dq=dq_shape,
        halo_grads=((span, chunks * PAIR), halo_type),
        own_part=own_part,
        weight_part=((rank, width), f32),
        input_grad=input_shape,
        grad=((block, width), bf16),
    )
    early = run(
        front,
        z,
        common
        | dict(
            cot=cots[last],
            stack=ahead.stack0,
            probs=ahead.probs0,
            dq_in=dq,
            input_sum=state.input_grad,
        )
        | numbered("halo_part", halo_parts)
        | numbered("pending", grads[-BLOCKS:])
        | numbered("term", terms[0][:-1]),
        outputs,
        sems(BLOCKS),
        flops,
    )
    halo_grads = early.halo_grads
    if per_head > 1:
        halo_grads = jnp.sum(halo_grads.reshape(span, HK, per_head, PAIR), axis=2)
        halo_grads = halo_grads.astype(bf16).reshape(span, HK * PAIR)
    backs = []
    stop = span
    for distance, count in pieces:
        backs.append(passed_along(halo_grads[stop - count : stop], "seq", -distance))
        stop -= count

    outputs = dict(grad=((block, width), bf16), dscores=((window, stack_rows), bf16))
    outputs |= numbered("share", [((rank // packs, width), bf16)] * packs)
    late = run(
        back,
        z,
        common
        | dict(cot=cots[last + 1], probs=ahead.probs1, weight_part=early.weight_part)
        | numbered("term", terms[0][-1:]),
        outputs,
        dict(total=pltpu.VMEM((rank, width), bf16)),
        flops,
    )
    shares = listed(late, "share")
    shares[1:] = [passed_along(shares[away], "dp", away) for away in range(1, packs)]

    merged = per_head == 1 and len(pieces) == 1
    outputs = dict(dq=dq_shape, input_grad=((rank, rows), bf16))
    outputs.update(share_out=((rank // packs, width), bf16))
    inputs = dict(
        at=at,
        up=matrix,
        cot=cots[last + 1],
        stack=ahead.stack1,
        probs=ahead.probs1,
        dscores=late.dscores,
        input_sum=early.input_grad,
        dq_in=early.dq,
        share=shares[0],
    )
    inputs |= numbered("own_part", own_parts + [early.own_part])
    if merged:
        inputs.update(halo_back=backs[0])
        outputs.update(pair_grads=((rows, HK * PAIR), bf16))
    else:
        outputs.update(own_grads=((rows, chunks * PAIR), f32))
    final = run(
        finish,
        z,
        inputs | numbered("pending", [early.grad, late.grad]),
        outputs,
        sems(BLOCKS),
        flops,
    )
    weight_share = final.share_out.astype(f32)
    for share in shares[1:]:
        weight_share += share.astype(f32)
    if merged:
        pair_grads = final.pair_grads
    else:
        own_grads = jnp.sum(final.own_grads.reshape(rows, HK, per_head, PAIR), axis=2)
        own_grads = own_grads.reshape(rows, HK * PAIR)
        for rows_back in backs:
            low = rows - rows_back.shape[0]
            own_grads = own_grads.at[low:].add(rows_back.astype(f32))
        pair_grads = own_grads.astype(bf16)

    return (
        final.dq[None, None],
        pair_grads[None, None],
        final.input_grad.T[None, None],
        weight_share[None],
    )


def solution(mesh):
    placed = (
        P("section", "dp", "seq", None),
        P("section", "dp", "seq", None),
        P("section", "dp", "seq", None),
        P("section", None, "seq"),
        P("section", "dp", "seq", None),
        P("section", "dp", None),
    )
    return jax.shard_map(
        per_device,
        mesh=mesh,
        in_specs=placed,
        out_specs=(
            P("section", "dp", "seq", None),
            P("section", "dp", "seq", None),
            P("section", "dp", "seq", None),
            P("section", "dp", "seq"),
        ),
        check_vma=False,
    )
```

```python
import functools
import math
from types import SimpleNamespace

import jax
import jax.numpy as jnp
from jax import lax
from jax.experimental import pallas as pl
from jax.experimental.pallas import tpu as pltpu
from jax.sharding import PartitionSpec as P

QUERY_HEADS = 32
HK = 4
HEAD_SIZE = 128
PAIR = 2 * HEAD_SIZE
SCALE = 1.0 / math.sqrt(HEAD_SIZE)
SPAN_PARTS = 8
BLOCKS = 2
COPIES = 4
LIMIT = 16 * 1024 * 1024
IN = "_in"
IN_HBM = ("upstream", "pairs", "matrix", "dq", "dq" + IN)
ANYWHERE = ("held", "held" + IN, "after")
VMEM = pl.BlockSpec(memory_space=pltpu.VMEM)
HBM = pl.BlockSpec(memory_space=pltpu.HBM)
ANY = pl.BlockSpec(memory_space=pl.ANY)


def passed_along(value, axis, steps):
    count = lax.axis_size(axis)
    pairs = [(source, (source + steps) % count) for source in range(count)]
    return lax.ppermute(value, axis, pairs)


def swapped(value, axis, bit):
    pairs = [(source, source ^ bit) for source in range(lax.axis_size(axis))]
    return lax.ppermute(value, axis, pairs)


def dot(left, right, left_dim, right_dim):
    return lax.dot_general(
        left, right, (((left_dim,), (right_dim,)), ((), ())), preferred_element_type=jnp.float32
    )


def low_bit(number):
    return number & -number


def numbered(name, arrays):
    return {name + str(index): array for index, array in enumerate(arrays)}


def listed(refs, name):
    found = []
    while hasattr(refs, name + str(len(found))):
        found.append(getattr(refs, name + str(len(found))))
    return found


def spec_of(name):
    return HBM if name in IN_HBM else ANY if name in ANYWHERE else VMEM


def run(body, sizes, inputs, outputs, scratch, flops=0):
    names = list(inputs) + list(outputs) + list(scratch)

    def kernel(*refs):
        body(sizes, SimpleNamespace(**dict(zip(names, refs))))

    operands = [
        pltpu.with_memory_space_constraint(array, pltpu.HBM) if name in IN_HBM[:3] else array
        for name, array in inputs.items()
    ]
    places = list(inputs)
    aliases = {
        places.index(name + IN): index
        for index, name in enumerate(outputs)
        if name + IN in inputs
    }
    results = pl.pallas_call(
        kernel,
        in_specs=[spec_of(name) for name in inputs],
        out_specs=[spec_of(name) for name in outputs],
        out_shape=[jax.ShapeDtypeStruct(shape, kind) for shape, kind in outputs.values()],
        scratch_shapes=list(scratch.values()),
        input_output_aliases=aliases,
        compiler_params=pltpu.CompilerParams(vmem_limit_bytes=LIMIT),
        cost_estimate=pl.CostEstimate(
            flops=flops // 1024, bytes_accessed=1024, transcendentals=flops // 1024
        ),
        name=body.__name__,
    )(*operands)
    return SimpleNamespace(**dict(zip(outputs, results)))


def copy_rows(source, target, sems, copies, parts=1):
    rows = source.shape[0] // parts
    for part in range(parts):
        piece = pl.ds(part * rows, rows)
        copies.append(
            pltpu.make_async_copy(source.at[piece], target.at[piece], sems.at[len(copies)])
        )
        copies[-1].start()


def chunk_at(step, chunks):
    return lax.axis_index("seq") ^ (chunks - 1 - step)


def chunk_columns(z, step):
    return pl.ds(pl.multiple_of(chunk_at(step, z.chunks) * z.width, HEAD_SIZE), z.width)


def pair_columns(z, step):
    return pl.ds(pl.multiple_of(chunk_at(step, z.chunks) * PAIR, HEAD_SIZE), PAIR)


def split_first(z, refs):
    copies = []
    source = refs.upstream.at[:, chunk_columns(z, 0)]
    copy_rows(source, refs.piece, refs.sems, copies, COPIES)
    for copy in copies:
        copy.wait()


def split_second(z, refs):
    copies = []
    source = refs.upstream.at[:, chunk_columns(z, 1)]
    copy_rows(source, refs.piece, refs.sems, copies, COPIES)
    copy_rows(refs.matrix, refs.matrix_copy, refs.sems, copies, COPIES)
    copy_rows(refs.pairs, refs.pairs_copy, refs.sems, copies, COPIES)
    height = refs.near.shape[0]
    near = refs.pairs.at[pl.ds(z.rows - height, height)]
    copy_rows(near, refs.near, refs.sems, copies, COPIES)
    for copy in copies:
        copy.wait()


def split_rest(z, refs):
    copies = []
    pieces = listed(refs, "piece")
    for step, piece in zip(range(2, z.chunks - 1), pieces):
        copy_rows(refs.upstream.at[:, chunk_columns(z, step)], piece, refs.sems, copies, COPIES)
    for index, piece in enumerate(pieces[-BLOCKS:]):
        rows = pl.ds(index * z.block, z.block)
        source = refs.upstream.at[rows, chunk_columns(z, z.chunks - 1)]
        copy_rows(source, piece, refs.sems, copies, COPIES)
    for copy in copies:
        copy.wait()


def stacked(array, rows):
    heads = array.shape[1] // HEAD_SIZE
    parts = [array[rows, head * HEAD_SIZE : (head + 1) * HEAD_SIZE] for head in range(heads)]
    return jnp.concatenate(parts, axis=0)


def seen_rows(z, refs, step, second):
    per_head = z.chunks // HK
    chunk = chunk_at(step, z.chunks)
    place = lax.div(chunk, per_head) if per_head > 1 else chunk
    start = pl.multiple_of(place * PAIR + second * HEAD_SIZE, HEAD_SIZE)
    columns = pl.ds(start, HEAD_SIZE)
    return jnp.concatenate([refs.halo[: z.span, columns], refs.own[:, columns]], axis=0)


def windowed(z, array, index):
    return array[index * z.block : index * z.block + z.window]


def softmax_blocks(z, refs, step, matrix, keys):
    queries = refs.fq[:, chunk_columns(z, step)].astype(jnp.float32)
    queries = (queries + dot(refs.at[...], matrix, 0, 0)).astype(jnp.bfloat16)
    stacks, probs = [], []
    for index in range(BLOCKS):
        stack = stacked(queries, slice(index * z.block, (index + 1) * z.block))
        hidden = refs.bias[index * z.window : (index + 1) * z.window]
        scores = dot(windowed(z, keys, index), stack, 1, 1) * SCALE
        scores += jnp.concatenate([hidden] * (stack.shape[0] // hidden.shape[1]), axis=1)
        shifted = jnp.exp(scores - jnp.max(scores, axis=0, keepdims=True))
        stacks.append(stack)
        probs.append(shifted * (1.0 / jnp.sum(shifted, axis=0, keepdims=True)))
    return stacks, probs


def score_grads(z, index, probs, keys, values, cot_stack):
    dprobs = dot(windowed(z, values, index), cot_stack, 1, 1)
    deltas = jnp.sum(probs * dprobs, axis=0, keepdims=True)
    dscores = (probs * (dprobs - deltas)).astype(jnp.bfloat16)
    return dscores, (dot(dscores, windowed(z, keys, index), 0, 0) * SCALE).astype(jnp.bfloat16)


def unstack(z, grad_stack, target, start):
    for head in range(grad_stack.shape[0] // z.block):
        columns = slice(head * HEAD_SIZE, (head + 1) * HEAD_SIZE)
        target[start : start + z.block, columns] = grad_stack[head * z.block : (head + 1) * z.block]


def pair_terms(z, index, dscores, probs, query_stack, cot_stack):
    key_term = dot(dscores, query_stack, 1, 0) * SCALE
    value_term = dot(probs.astype(jnp.bfloat16), cot_stack, 1, 0)
    term = jnp.concatenate([key_term, value_term], axis=1)
    start = index * z.block
    rest = z.span + z.rows - z.window - start
    if start > 0:
        term = jnp.concatenate([jnp.zeros((start, PAIR), jnp.float32), term], axis=0)
    if rest > 0:
        term = jnp.concatenate([term, jnp.zeros((rest, PAIR), jnp.float32)], axis=0)
    return term


def padded(z, grad, index):
    blank = jnp.zeros((z.block, grad.shape[1]), grad.dtype)
    return jnp.concatenate([grad if place == index else blank for place in range(BLOCKS)], axis=0)


def forward(z, refs):
    step = z.chunks - 1
    keys = seen_rows(z, refs, step, 0)
    stacks, probs = softmax_blocks(z, refs, step, refs.up[...], keys)
    for index in range(BLOCKS):
        listed(refs, "stack")[index][...] = stacks[index]
        listed(refs, "probs")[index][...] = probs[index]


def whole(step, z, refs):
    copies = []
    if hasattr(refs, "pending"):
        copy_rows(refs.pending, refs.dq.at[:, chunk_columns(z, step - 1)], refs.sems, copies)
    matrix = refs.up[...]
    keys, values = seen_rows(z, refs, step, 0), seen_rows(z, refs, step, 1)
    stacks, probs = softmax_blocks(z, refs, step, matrix, keys)
    pair_total = 0.0
    for index in range(BLOCKS):
        start = index * z.block
        cot_stack = stacked(refs.cot, slice(start, start + z.block))
        dscores, grad_stack = score_grads(z, index, probs[index], keys, values, cot_stack)
        unstack(z, grad_stack, refs.grad, start)
        pair_total += pair_terms(z, index, dscores, probs[index], stacks[index], cot_stack)
    grad = refs.grad[...]
    weight = dot(refs.at[...], grad, 1, 0)
    for term in listed(refs, "term"):
        weight += term[...].astype(jnp.float32)
    refs.weight[...] = weight.astype(jnp.bfloat16)
    refs.halo_part[...] = pair_total[: z.span].astype(refs.halo_part.dtype)
    refs.own_part[...] = pair_total[z.span :]
    input_grad = dot(matrix, grad, 1, 1)
    if step > 0:
        input_grad += refs.input_sum[...]
    refs.input_grad[...] = input_grad
    for copy in copies:
        copy.wait()


def front(z, refs):
    copies = []
    step = z.chunks - 1
    for place, grad in enumerate(listed(refs, "pending")):
        target = refs.dq.at[:, chunk_columns(z, step - BLOCKS + place)]
        copy_rows(grad, target, refs.sems, copies)
    keys, values = seen_rows(z, refs, step, 0), seen_rows(z, refs, step, 1)
    probs = refs.probs[...]
    cot_stack = stacked(refs.cot, slice(0, z.block))
    dscores, grad_stack = score_grads(z, 0, probs, keys, values, cot_stack)
    unstack(z, grad_stack, refs.grad, 0)
    pair_total = pair_terms(z, 0, dscores, probs, refs.stack[...], cot_stack)
    kind = refs.halo_grads.dtype
    for place, part in enumerate(listed(refs, "halo_part")):
        refs.halo_grads[:, pair_columns(z, place)] = part[...]
    refs.halo_grads[:, pair_columns(z, step)] = pair_total[: z.span].astype(kind)
    refs.own_part[...] = pair_total[z.span :]
    grad = padded(z, refs.grad[...], 0)
    weight = dot(refs.at[...], grad, 1, 0)
    for term in listed(refs, "term"):
        weight += term[...].astype(jnp.float32)
    refs.weight_part[...] = weight
    refs.input_grad[...] = refs.input_sum[...] + dot(refs.up[...], grad, 1, 1)
    for copy in copies:
        copy.wait()


def back(z, refs):
    step = z.chunks - 1
    keys, values = seen_rows(z, refs, step, 0), seen_rows(z, refs, step, 1)
    cot_stack = stacked(refs.cot, slice(0, z.block))
    dscores, grad_stack = score_grads(z, 1, refs.probs[...], keys, values, cot_stack)
    refs.dscores[...] = dscores
    unstack(z, grad_stack, refs.grad, 0)
    weight = refs.weight_part[...] + dot(refs.at[...], padded(z, refs.grad[...], 1), 1, 0)
    for term in listed(refs, "term"):
        weight += term[...].astype(jnp.float32)
    refs.total[...] = weight.astype(jnp.bfloat16)
    shares = listed(refs, "share")
    rows = z.rank // len(shares)
    for away, share in enumerate(shares):
        target = lax.rem(lax.axis_index("dp") + away, len(shares))
        share[...] = refs.total[pl.ds(pl.multiple_of(target * rows, rows), rows)]


def finish(z, refs):
    copies = []
    step = z.chunks - 1
    for index, grad in enumerate(listed(refs, "pending")):
        target = refs.dq.at[pl.ds(index * z.block, z.block), chunk_columns(z, step)]
        copy_rows(grad, target, refs.sems, copies)
    cot_stack = stacked(refs.cot, slice(0, z.block))
    pair_total = pair_terms(z, 1, refs.dscores[...], refs.probs[...], refs.stack[...], cot_stack)
    parts = [part[...] for part in listed(refs, "own_part")]
    parts[step] += pair_total[z.span :]
    low = z.rows - z.span
    for place, part in enumerate(parts):
        columns = pair_columns(z, place)
        if hasattr(refs, "halo_back"):
            refs.pair_grads[:low, columns] = part[:low].astype(jnp.bfloat16)
            part = part[low:] + refs.halo_back[:, columns].astype(jnp.float32)
            refs.pair_grads[low:, columns] = part.astype(jnp.bfloat16)
        else:
            refs.own_grads[:, columns] = part
    refs.share_out[...] = refs.share[...]
    grad = padded(z, refs.pending1[...], 1)
    input_grad = refs.input_sum[...] + dot(refs.up[...], grad, 1, 1)
    refs.input_grad[...] = input_grad.astype(jnp.bfloat16)
    for copy in copies:
        copy.wait()


def per_device(
    frozen_queries, key_value_pairs, adapter_input, adapter_up_matrix, upstream, document_index
):
    bf16, f32 = jnp.bfloat16, jnp.float32
    chunks = lax.axis_size("seq")
    packs = lax.axis_size("dp")
    place = lax.axis_index("seq")
    rows = frozen_queries.shape[2]
    columns = QUERY_HEADS * HEAD_SIZE
    block = rows // BLOCKS
    span = document_index.shape[2] // SPAN_PARTS
    window = span + block
    width = columns // chunks
    rank = adapter_input.shape[3]
    stack_rows = width // HEAD_SIZE * block
    per_head = chunks // HK
    last = chunks - 1
    z = SimpleNamespace(
        chunks=chunks, rows=rows, block=block, span=span, window=window, width=width, rank=rank
    )
    flops = 10 * stack_rows * window * HEAD_SIZE

    pieces = []
    left = span
    while left > 0:
        pieces.append((len(pieces) + 1, min(rows, left)))
        left -= rows

    own = key_value_pairs[0, 0]
    matrix = adapter_up_matrix[0]
    cotangents = upstream[0, 0]

    def sems(count):
        return dict(sems=pltpu.SemaphoreType.DMA((count,)))

    piece = ((rows, width), bf16)
    first = run(split_first, z, dict(upstream=cotangents), dict(piece=piece), sems(COPIES)).piece
    cots = [passed_along(first, "section", -1)]
    outputs = dict(
        piece=piece,
        matrix_copy=((rank, width), bf16),
        pairs_copy=(own.shape, bf16),
        near=((pieces[-1][1], own.shape[1]), bf16),
    )
    second = run(
        split_second,
        z,
        dict(upstream=cotangents, pairs=own, matrix=matrix, after=first),
        outputs,
        sems(COPIES * len(outputs)),
    )
    cots.append(passed_along(second.piece, "section", -1))
    own, matrix = second.pairs_copy, second.matrix_copy
    outputs = numbered("piece", [piece] * (last - 2) + [((block, width), bf16)] * BLOCKS)
    rest = run(
        split_rest,
        z,
        dict(upstream=cotangents, after=second.piece),
        outputs,
        sems(COPIES * len(outputs)),
    )
    held = listed(rest, "piece")
    cots.append(passed_along(held[0], "section", -1))
    halo = [passed_along(own, "seq", distance) for distance, _ in pieces[:-1]]
    halo.append(passed_along(second.near, "seq", pieces[-1][0]))
    halo = jnp.concatenate(halo[::-1], axis=0)
    ups = {0: matrix}
    for away in sorted(range(1, chunks), key=low_bit, reverse=True):
        bit = low_bit(away)
        ups[away] = swapped(ups[away - bit], "seq", bit)

    numbers = jnp.concatenate([jnp.full((span,), -1, jnp.int32), document_index[0, 0]])
    numbers = lax.dynamic_slice_in_dim(numbers, place * rows, span + rows, 0)
    reach = jnp.arange(window, dtype=jnp.int32)[:, None] <= (
        jnp.arange(block, dtype=jnp.int32)[None, :] + span
    )
    bias = []
    for start in range(0, rows, block):
        seen = numbers[start : start + window, None]
        same = seen == numbers[None, start + span : start + span + block]
        bias.append(jnp.where(same & reach, 0.0, -jnp.inf))
    bias = jnp.concatenate(bias, axis=0).astype(f32)
    bias = jnp.concatenate([bias, bias], axis=1)
    fq = frozen_queries[0, 0]
    at = adapter_input[0, 0].T

    outputs = numbered("stack", [((stack_rows, HEAD_SIZE), bf16)] * BLOCKS)
    outputs |= numbered("probs", [((window, stack_rows), f32)] * BLOCKS)
    outputs.update(held=(held[1].shape, bf16))
    inputs = dict(fq=fq, at=at, up=matrix, halo=halo, own=own, bias=bias, held_in=held[1])
    ahead = run(forward, z, inputs, outputs, {}, flops)
    cots.append(passed_along(ahead.held, "section", -1))

    halo_type = bf16 if per_head == 1 else f32
    halo_part, own_part = ((span, PAIR), halo_type), ((rows, PAIR), f32)
    dq_shape = ((rows, columns), bf16)
    input_shape = ((rank, rows), f32)
    terms = {away: [] for away in range(chunks)}
    grads, halo_parts, own_parts = [], [], []
    state = None
    for step in range(last):
        away = last - step
        inputs = dict(fq=fq, at=at, halo=halo, own=own, bias=bias, cot=cots[step], up=ups[away])
        inputs |= numbered("term", terms[away])
        outputs = dict(
            halo_part=halo_part,
            own_part=own_part,
            input_grad=input_shape,
            grad=piece,
            weight=((rank, width), bf16),
        )
        if step > 0:
            inputs.update(input_sum=state.input_grad)
        else:
            inputs.update(after=ahead.stack0)
        if 0 < step < last - 1:
            inputs.update(pending=grads[-1])
            outputs.update(dq=dq_shape)
            if step > 1:
                inputs.update(dq_in=dq)
        if step + 2 < len(held):
            inputs.update(held_in=held[step + 2])
            outputs.update(held=(held[step + 2].shape, bf16))
        body = functools.partial(whole, step)
        body.__name__ = whole.__name__
        state = run(body, z, inputs, outputs, sems(1), 2 * flops)
        grads.append(state.grad)
        halo_parts.append(state.halo_part)
        own_parts.append(state.own_part)
        dq = getattr(state, "dq", None) if step < last - 1 else dq
        if step + 2 < len(held):
            cots.append(passed_along(state.held, "section", -1))
        bit = low_bit(away)
        terms[away - bit].append(swapped(state.weight, "seq", bit))

    common = dict(at=at, up=matrix, halo=halo, own=own)
    outputs = dict(
        dq=dq_shape,
        halo_grads=((span, chunks * PAIR), halo_type),
        own_part=own_part,
        weight_part=((rank, width), f32),
        input_grad=input_shape,
        grad=((block, width), bf16),
    )
    early = run(
        front,
        z,
        common
        | dict(
            cot=cots[last],
            stack=ahead.stack0,
            probs=ahead.probs0,
            dq_in=dq,
            input_sum=state.input_grad,
        )
        | numbered("halo_part", halo_parts)
        | numbered("pending", grads[-BLOCKS:])
        | numbered("term", terms[0][:-1]),
        outputs,
        sems(BLOCKS),
        flops,
    )
    halo_grads = early.halo_grads
    if per_head > 1:
        halo_grads = jnp.sum(halo_grads.reshape(span, HK, per_head, PAIR), axis=2)
        halo_grads = halo_grads.astype(bf16).reshape(span, HK * PAIR)
    backs = []
    stop = span
    for distance, count in pieces:
        backs.append(passed_along(halo_grads[stop - count : stop], "seq", -distance))
        stop -= count

    outputs = dict(grad=((block, width), bf16), dscores=((window, stack_rows), bf16))
    outputs |= numbered("share", [((rank // packs, width), bf16)] * packs)
    late = run(
        back,
        z,
        common
        | dict(cot=cots[last + 1], probs=ahead.probs1, weight_part=early.weight_part)
        | numbered("term", terms[0][-1:]),
        outputs,
        dict(total=pltpu.VMEM((rank, width), bf16)),
        flops,
    )
    shares = listed(late, "share")
    shares[1:] = [passed_along(shares[away], "dp", away) for away in range(1, packs)]

    merged = per_head == 1 and len(pieces) == 1
    outputs = dict(dq=dq_shape, input_grad=((rank, rows), bf16))
    outputs.update(share_out=((rank // packs, width), bf16))
    inputs = dict(
        at=at,
        up=matrix,
        cot=cots[last + 1],
        stack=ahead.stack1,
        probs=ahead.probs1,
        dscores=late.dscores,
        input_sum=early.input_grad,
        dq_in=early.dq,
        share=shares[0],
    )
    inputs |= numbered("own_part", own_parts + [early.own_part])
    if merged:
        inputs.update(halo_back=backs[0])
        outputs.update(pair_grads=((rows, HK * PAIR), bf16))
    else:
        outputs.update(own_grads=((rows, chunks * PAIR), f32))
    final = run(
        finish,
        z,
        inputs | numbered("pending", [early.grad, late.grad]),
        outputs,
        sems(BLOCKS),
        flops,
    )
    weight_share = final.share_out.astype(f32)
    for share in shares[1:]:
        weight_share += share.astype(f32)
    if merged:
        pair_grads = final.pair_grads
    else:
        own_grads = jnp.sum(final.own_grads.reshape(rows, HK, per_head, PAIR), axis=2)
        own_grads = own_grads.reshape(rows, HK * PAIR)
        for rows_back in backs:
            low = rows - rows_back.shape[0]
            own_grads = own_grads.at[low:].add(rows_back.astype(f32))
        pair_grads = own_grads.astype(bf16)

    return (
        final.dq[None, None],
        pair_grads[None, None],
        final.input_grad.T[None, None],
        weight_share[None],
    )


def solution(mesh):
    placed = (
        P("section", "dp", "seq", None),
        P("section", "dp", "seq", None),
        P("section", "dp", "seq", None),
        P("section", None, "seq"),
        P("section", "dp", "seq", None),
        P("section", "dp", None),
    )
    return jax.shard_map(
        per_device,
        mesh=mesh,
        in_specs=placed,
        out_specs=(
            P("section", "dp", "seq", None),
            P("section", "dp", "seq", None),
            P("section", "dp", "seq", None),
            P("section", "dp", "seq"),
        ),
        check_vma=False,
    )
```

```python
import functools
import math
from types import SimpleNamespace

import jax
import jax.numpy as jnp
from jax import lax
from jax.experimental import pallas as pl
from jax.experimental.pallas import tpu as pltpu
from jax.sharding import PartitionSpec as P

QUERY_HEADS = 32
HK = 4
HEAD_SIZE = 128
PAIR = 2 * HEAD_SIZE
SCALE = 1.0 / math.sqrt(HEAD_SIZE)
SPAN_PARTS = 8
BLOCKS = 2
COPIES = 4
LIMIT = 16 * 1024 * 1024
IN = "_in"
IN_HBM = ("upstream", "pairs", "matrix", "dq", "dq" + IN)
ANYWHERE = ("held", "held" + IN, "after")
VMEM = pl.BlockSpec(memory_space=pltpu.VMEM)
HBM = pl.BlockSpec(memory_space=pltpu.HBM)
ANY = pl.BlockSpec(memory_space=pl.ANY)


def passed_along(value, axis, steps):
    count = lax.axis_size(axis)
    pairs = [(source, (source + steps) % count) for source in range(count)]
    return lax.ppermute(value, axis, pairs)


def swapped(value, axis, bit):
    pairs = [(source, source ^ bit) for source in range(lax.axis_size(axis))]
    return lax.ppermute(value, axis, pairs)


def dot(left, right, left_dim, right_dim):
    return lax.dot_general(
        left, right, (((left_dim,), (right_dim,)), ((), ())), preferred_element_type=jnp.float32
    )


def low_bit(number):
    return number & -number


def numbered(name, arrays):
    return {name + str(index): array for index, array in enumerate(arrays)}


def listed(refs, name):
    found = []
    while hasattr(refs, name + str(len(found))):
        found.append(getattr(refs, name + str(len(found))))
    return found


def spec_of(name):
    return HBM if name in IN_HBM else ANY if name in ANYWHERE else VMEM


def run(body, sizes, inputs, outputs, scratch, flops=0):
    names = list(inputs) + list(outputs) + list(scratch)

    def kernel(*refs):
        body(sizes, SimpleNamespace(**dict(zip(names, refs))))

    operands = [
        pltpu.with_memory_space_constraint(array, pltpu.HBM) if name in IN_HBM[:3] else array
        for name, array in inputs.items()
    ]
    places = list(inputs)
    aliases = {
        places.index(name + IN): index
        for index, name in enumerate(outputs)
        if name + IN in inputs
    }
    results = pl.pallas_call(
        kernel,
        in_specs=[spec_of(name) for name in inputs],
        out_specs=[spec_of(name) for name in outputs],
        out_shape=[jax.ShapeDtypeStruct(shape, kind) for shape, kind in outputs.values()],
        scratch_shapes=list(scratch.values()),
        input_output_aliases=aliases,
        compiler_params=pltpu.CompilerParams(vmem_limit_bytes=LIMIT),
        cost_estimate=pl.CostEstimate(
            flops=flops // 1024, bytes_accessed=1024, transcendentals=flops // 1024
        ),
        name=body.__name__,
    )(*operands)
    return SimpleNamespace(**dict(zip(outputs, results)))


def copy_rows(source, target, sems, copies, parts=1):
    rows = source.shape[0] // parts
    for part in range(parts):
        piece = pl.ds(part * rows, rows)
        copies.append(
            pltpu.make_async_copy(source.at[piece], target.at[piece], sems.at[len(copies)])
        )
        copies[-1].start()


def chunk_at(step, chunks):
    return lax.axis_index("seq") ^ (chunks - 1 - step)


def chunk_columns(z, step):
    return pl.ds(pl.multiple_of(chunk_at(step, z.chunks) * z.width, HEAD_SIZE), z.width)


def pair_columns(z, step):
    return pl.ds(pl.multiple_of(chunk_at(step, z.chunks) * PAIR, HEAD_SIZE), PAIR)


def split_first(z, refs):
    copies = []
    source = refs.upstream.at[:, chunk_columns(z, 0)]
    copy_rows(source, refs.piece, refs.sems, copies, COPIES)
    for copy in copies:
        copy.wait()


def split_second(z, refs):
    copies = []
    source = refs.upstream.at[:, chunk_columns(z, 1)]
    copy_rows(source, refs.piece, refs.sems, copies, COPIES)
    copy_rows(refs.matrix, refs.matrix_copy, refs.sems, copies, COPIES)
    height = refs.near.shape[0]
    near = refs.pairs.at[pl.ds(z.rows - height, height)]
    copy_rows(near, refs.near, refs.sems, copies, COPIES)
    for copy in copies:
        copy.wait()


def split_rest(z, refs):
    copies = []
    pieces = listed(refs, "piece")
    for step, piece in zip(range(2, z.chunks - 1), pieces):
        copy_rows(refs.upstream.at[:, chunk_columns(z, step)], piece, refs.sems, copies, COPIES)
    for index, piece in enumerate(pieces[-BLOCKS:]):
        rows = pl.ds(index * z.block, z.block)
        source = refs.upstream.at[rows, chunk_columns(z, z.chunks - 1)]
        copy_rows(source, piece, refs.sems, copies, COPIES)
    for copy in copies:
        copy.wait()


def stacked(array, rows):
    heads = array.shape[1] // HEAD_SIZE
    parts = [array[rows, head * HEAD_SIZE : (head + 1) * HEAD_SIZE] for head in range(heads)]
    return jnp.concatenate(parts, axis=0)


def seen_rows(z, refs, step, second):
    per_head = z.chunks // HK
    chunk = chunk_at(step, z.chunks)
    place = lax.div(chunk, per_head) if per_head > 1 else chunk
    start = pl.multiple_of(place * PAIR + second * HEAD_SIZE, HEAD_SIZE)
    columns = pl.ds(start, HEAD_SIZE)
    return jnp.concatenate([refs.halo[: z.span, columns], refs.own[:, columns]], axis=0)


def windowed(z, array, index):
    return array[index * z.block : index * z.block + z.window]


def softmax_blocks(z, refs, step, matrix, keys):
    queries = refs.fq[:, chunk_columns(z, step)].astype(jnp.float32)
    queries = (queries + dot(refs.at[...], matrix, 0, 0)).astype(jnp.bfloat16)
    stacks, probs = [], []
    for index in range(BLOCKS):
        stack = stacked(queries, slice(index * z.block, (index + 1) * z.block))
        hidden = refs.bias[index * z.window : (index + 1) * z.window]
        scores = dot(windowed(z, keys, index), stack, 1, 1) * SCALE
        scores += jnp.concatenate([hidden] * (stack.shape[0] // hidden.shape[1]), axis=1)
        shifted = jnp.exp(scores - jnp.max(scores, axis=0, keepdims=True))
        stacks.append(stack)
        probs.append(shifted * (1.0 / jnp.sum(shifted, axis=0, keepdims=True)))
    return stacks, probs


def score_grads(z, index, probs, keys, values, cot_stack):
    dprobs = dot(windowed(z, values, index), cot_stack, 1, 1)
    deltas = jnp.sum(probs * dprobs, axis=0, keepdims=True)
    dscores = (probs * (dprobs - deltas)).astype(jnp.bfloat16)
    return dscores, (dot(dscores, windowed(z, keys, index), 0, 0) * SCALE).astype(jnp.bfloat16)


def unstack(z, grad_stack, target, start):
    for head in range(grad_stack.shape[0] // z.block):
        columns = slice(head * HEAD_SIZE, (head + 1) * HEAD_SIZE)
        target[start : start + z.block, columns] = grad_stack[head * z.block : (head + 1) * z.block]


def pair_terms(z, index, dscores, probs, query_stack, cot_stack):
    key_term = dot(dscores, query_stack, 1, 0) * SCALE
    value_term = dot(probs.astype(jnp.bfloat16), cot_stack, 1, 0)
    term = jnp.concatenate([key_term, value_term], axis=1)
    start = index * z.block
    rest = z.span + z.rows - z.window - start
    if start > 0:
        term = jnp.concatenate([jnp.zeros((start, PAIR), jnp.float32), term], axis=0)
    if rest > 0:
        term = jnp.concatenate([term, jnp.zeros((rest, PAIR), jnp.float32)], axis=0)
    return term


def padded(z, grad, index):
    blank = jnp.zeros((z.block, grad.shape[1]), grad.dtype)
    return jnp.concatenate([grad if place == index else blank for place in range(BLOCKS)], axis=0)


def forward(z, refs):
    step = z.chunks - 1
    keys = seen_rows(z, refs, step, 0)
    stacks, probs = softmax_blocks(z, refs, step, refs.up[...], keys)
    for index in range(BLOCKS):
        listed(refs, "stack")[index][...] = stacks[index]
        listed(refs, "probs")[index][...] = probs[index]


def whole(step, z, refs):
    copies = []
    if hasattr(refs, "pending"):
        copy_rows(refs.pending, refs.dq.at[:, chunk_columns(z, step - 1)], refs.sems, copies)
    matrix = refs.up[...]
    keys, values = seen_rows(z, refs, step, 0), seen_rows(z, refs, step, 1)
    stacks, probs = softmax_blocks(z, refs, step, matrix, keys)
    pair_total = 0.0
    for index in range(BLOCKS):
        start = index * z.block
        cot_stack = stacked(refs.cot, slice(start, start + z.block))
        dscores, grad_stack = score_grads(z, index, probs[index], keys, values, cot_stack)
        unstack(z, grad_stack, refs.grad, start)
        pair_total += pair_terms(z, index, dscores, probs[index], stacks[index], cot_stack)
    grad = refs.grad[...]
    weight = dot(refs.at[...], grad, 1, 0)
    for term in listed(refs, "term"):
        weight += term[...].astype(jnp.float32)
    refs.weight[...] = weight.astype(jnp.bfloat16)
    refs.halo_part[...] = pair_total[: z.span].astype(refs.halo_part.dtype)
    refs.own_part[...] = pair_total[z.span :]
    input_grad = dot(matrix, grad, 1, 1)
    if step > 0:
        input_grad += refs.input_sum[...]
    refs.input_grad[...] = input_grad
    for copy in copies:
        copy.wait()


def front(z, refs):
    copies = []
    step = z.chunks - 1
    for place, grad in enumerate(listed(refs, "pending")):
        target = refs.dq.at[:, chunk_columns(z, step - BLOCKS + place)]
        copy_rows(grad, target, refs.sems, copies)
    keys, values = seen_rows(z, refs, step, 0), seen_rows(z, refs, step, 1)
    probs = refs.probs[...]
    cot_stack = stacked(refs.cot, slice(0, z.block))
    dscores, grad_stack = score_grads(z, 0, probs, keys, values, cot_stack)
    unstack(z, grad_stack, refs.grad, 0)
    pair_total = pair_terms(z, 0, dscores, probs, refs.stack[...], cot_stack)
    kind = refs.halo_grads.dtype
    for place, part in enumerate(listed(refs, "halo_part")):
        refs.halo_grads[:, pair_columns(z, place)] = part[...]
    refs.halo_grads[:, pair_columns(z, step)] = pair_total[: z.span].astype(kind)
    refs.own_part[...] = pair_total[z.span :]
    grad = padded(z, refs.grad[...], 0)
    weight = dot(refs.at[...], grad, 1, 0)
    for term in listed(refs, "term"):
        weight += term[...].astype(jnp.float32)
    refs.weight_part[...] = weight
    refs.input_grad[...] = refs.input_sum[...] + dot(refs.up[...], grad, 1, 1)
    for copy in copies:
        copy.wait()


def back(z, refs):
    step = z.chunks - 1
    keys, values = seen_rows(z, refs, step, 0), seen_rows(z, refs, step, 1)
    cot_stack = stacked(refs.cot, slice(0, z.block))
    dscores, grad_stack = score_grads(z, 1, refs.probs[...], keys, values, cot_stack)
    refs.dscores[...] = dscores
    unstack(z, grad_stack, refs.grad, 0)
    weight = refs.weight_part[...] + dot(refs.at[...], padded(z, refs.grad[...], 1), 1, 0)
    for term in listed(refs, "term"):
        weight += term[...].astype(jnp.float32)
    refs.total[...] = weight.astype(jnp.bfloat16)
    shares = listed(refs, "share")
    rows = z.rank // len(shares)
    for away, share in enumerate(shares):
        target = lax.rem(lax.axis_index("dp") + away, len(shares))
        share[...] = refs.total[pl.ds(pl.multiple_of(target * rows, rows), rows)]


def finish(z, refs):
    copies = []
    step = z.chunks - 1
    for index, grad in enumerate(listed(refs, "pending")):
        target = refs.dq.at[pl.ds(index * z.block, z.block), chunk_columns(z, step)]
        copy_rows(grad, target, refs.sems, copies)
    cot_stack = stacked(refs.cot, slice(0, z.block))
    pair_total = pair_terms(z, 1, refs.dscores[...], refs.probs[...], refs.stack[...], cot_stack)
    parts = [part[...] for part in listed(refs, "own_part")]
    parts[step] += pair_total[z.span :]
    low = z.rows - z.span
    for place, part in enumerate(parts):
        columns = pair_columns(z, place)
        if hasattr(refs, "halo_back"):
            refs.pair_grads[:low, columns] = part[:low].astype(jnp.bfloat16)
            part = part[low:] + refs.halo_back[:, columns].astype(jnp.float32)
            refs.pair_grads[low:, columns] = part.astype(jnp.bfloat16)
        else:
            refs.own_grads[:, columns] = part
    refs.share_out[...] = refs.share[...]
    grad = padded(z, refs.pending1[...], 1)
    input_grad = refs.input_sum[...] + dot(refs.up[...], grad, 1, 1)
    refs.input_grad[...] = input_grad.astype(jnp.bfloat16)
    for copy in copies:
        copy.wait()


def per_device(
    frozen_queries, key_value_pairs, adapter_input, adapter_up_matrix, upstream, document_index
):
    bf16, f32 = jnp.bfloat16, jnp.float32
    chunks = lax.axis_size("seq")
    packs = lax.axis_size("dp")
    place = lax.axis_index("seq")
    rows = frozen_queries.shape[2]
    columns = QUERY_HEADS * HEAD_SIZE
    block = rows // BLOCKS
    span = document_index.shape[2] // SPAN_PARTS
    window = span + block
    width = columns // chunks
    rank = adapter_input.shape[3]
    stack_rows = width // HEAD_SIZE * block
    per_head = chunks // HK
    last = chunks - 1
    z = SimpleNamespace(
        chunks=chunks, rows=rows, block=block, span=span, window=window, width=width, rank=rank
    )
    flops = 10 * stack_rows * window * HEAD_SIZE

    pieces = []
    left = span
    while left > 0:
        pieces.append((len(pieces) + 1, min(rows, left)))
        left -= rows

    own = key_value_pairs[0, 0]
    matrix = adapter_up_matrix[0]
    cotangents = upstream[0, 0]

    def sems(count):
        return dict(sems=pltpu.SemaphoreType.DMA((count,)))

    piece = ((rows, width), bf16)
    first = run(split_first, z, dict(upstream=cotangents), dict(piece=piece), sems(COPIES)).piece
    cots = [passed_along(first, "section", -1)]
    outputs = dict(
        piece=piece,
        matrix_copy=((rank, width), bf16),
        near=((pieces[-1][1], own.shape[1]), bf16),
    )
    second = run(
        split_second,
        z,
        dict(upstream=cotangents, pairs=own, matrix=matrix, after=first),
        outputs,
        sems(COPIES * len(outputs)),
    )
    cots.append(passed_along(second.piece, "section", -1))
    matrix = second.matrix_copy
    outputs = numbered("piece", [piece] * (last - 2) + [((block, width), bf16)] * BLOCKS)
    rest = run(
        split_rest,
        z,
        dict(upstream=cotangents, after=second.piece),
        outputs,
        sems(COPIES * len(outputs)),
    )
    held = listed(rest, "piece")
    cots.append(passed_along(held[0], "section", -1))
    halo = [passed_along(own, "seq", distance) for distance, _ in pieces[:-1]]
    halo.append(passed_along(second.near, "seq", pieces[-1][0]))
    halo = jnp.concatenate(halo[::-1], axis=0)
    ups = {0: matrix}
    for away in sorted(range(1, chunks), key=low_bit, reverse=True):
        bit = low_bit(away)
        ups[away] = swapped(ups[away - bit], "seq", bit)

    numbers = jnp.concatenate([jnp.full((span,), -1, jnp.int32), document_index[0, 0]])
    numbers = lax.dynamic_slice_in_dim(numbers, place * rows, span + rows, 0)
    reach = jnp.arange(window, dtype=jnp.int32)[:, None] <= (
        jnp.arange(block, dtype=jnp.int32)[None, :] + span
    )
    bias = []
    for start in range(0, rows, block):
        seen = numbers[start : start + window, None]
        same = seen == numbers[None, start + span : start + span + block]
        bias.append(jnp.where(same & reach, 0.0, -jnp.inf))
    bias = jnp.concatenate(bias, axis=0).astype(f32)
    bias = jnp.concatenate([bias, bias], axis=1)
    fq = frozen_queries[0, 0]
    at = adapter_input[0, 0].T

    outputs = numbered("stack", [((stack_rows, HEAD_SIZE), bf16)] * BLOCKS)
    outputs |= numbered("probs", [((window, stack_rows), f32)] * BLOCKS)
    outputs.update(held=(held[1].shape, bf16))
    inputs = dict(fq=fq, at=at, up=matrix, halo=halo, own=own, bias=bias, held_in=held[1])
    ahead = run(forward, z, inputs, outputs, {}, flops)
    cots.append(passed_along(ahead.held, "section", -1))

    halo_type = bf16 if per_head == 1 else f32
    halo_part, own_part = ((span, PAIR), halo_type), ((rows, PAIR), f32)
    dq_shape = ((rows, columns), bf16)
    input_shape = ((rank, rows), f32)
    terms = {away: [] for away in range(chunks)}
    grads, halo_parts, own_parts = [], [], []
    state = None
    for step in range(last):
        away = last - step
        inputs = dict(fq=fq, at=at, halo=halo, own=own, bias=bias, cot=cots[step], up=ups[away])
        inputs |= numbered("term", terms[away])
        outputs = dict(
            halo_part=halo_part,
            own_part=own_part,
            input_grad=input_shape,
            grad=piece,
            weight=((rank, width), bf16),
        )
        if step > 0:
            inputs.update(input_sum=state.input_grad)
        else:
            inputs.update(after=ahead.stack0)
        if 0 < step < last - 1:
            inputs.update(pending=grads[-1])
            outputs.update(dq=dq_shape)
            if step > 1:
                inputs.update(dq_in=dq)
        if step + 2 < len(held):
            inputs.update(held_in=held[step + 2])
            outputs.update(held=(held[step + 2].shape, bf16))
        body = functools.partial(whole, step)
        body.__name__ = whole.__name__
        state = run(body, z, inputs, outputs, sems(1), 2 * flops)
        grads.append(state.grad)
        halo_parts.append(state.halo_part)
        own_parts.append(state.own_part)
        dq = getattr(state, "dq", None) if step < last - 1 else dq
        if step + 2 < len(held):
            cots.append(passed_along(state.held, "section", -1))
        bit = low_bit(away)
        terms[away - bit].append(swapped(state.weight, "seq", bit))

    common = dict(at=at, up=matrix, halo=halo, own=own)
    outputs = dict(
        dq=dq_shape,
        halo_grads=((span, chunks * PAIR), halo_type),
        own_part=own_part,
        weight_part=((rank, width), f32),
        input_grad=input_shape,
        grad=((block, width), bf16),
    )
    early = run(
        front,
        z,
        common
        | dict(
            cot=cots[last],
            stack=ahead.stack0,
            probs=ahead.probs0,
            dq_in=dq,
            input_sum=state.input_grad,
        )
        | numbered("halo_part", halo_parts)
        | numbered("pending", grads[-BLOCKS:])
        | numbered("term", terms[0][:-1]),
        outputs,
        sems(BLOCKS),
        flops,
    )
    halo_grads = early.halo_grads
    if per_head > 1:
        halo_grads = jnp.sum(halo_grads.reshape(span, HK, per_head, PAIR), axis=2)
        halo_grads = halo_grads.astype(bf16).reshape(span, HK * PAIR)
    backs = []
    stop = span
    for distance, count in pieces:
        backs.append(passed_along(halo_grads[stop - count : stop], "seq", -distance))
        stop -= count

    outputs = dict(grad=((block, width), bf16), dscores=((window, stack_rows), bf16))
    outputs |= numbered("share", [((rank // packs, width), bf16)] * packs)
    late = run(
        back,
        z,
        common
        | dict(cot=cots[last + 1], probs=ahead.probs1, weight_part=early.weight_part)
        | numbered("term", terms[0][-1:]),
        outputs,
        dict(total=pltpu.VMEM((rank, width), bf16)),
        flops,
    )
    shares = listed(late, "share")
    shares[1:] = [passed_along(shares[away], "dp", away) for away in range(1, packs)]

    merged = per_head == 1 and len(pieces) == 1
    outputs = dict(dq=dq_shape, input_grad=((rank, rows), bf16))
    outputs.update(share_out=((rank // packs, width), bf16))
    inputs = dict(
        at=at,
        up=matrix,
        cot=cots[last + 1],
        stack=ahead.stack1,
        probs=ahead.probs1,
        dscores=late.dscores,
        input_sum=early.input_grad,
        dq_in=early.dq,
        share=shares[0],
    )
    inputs |= numbered("own_part", own_parts + [early.own_part])
    if merged:
        inputs.update(halo_back=backs[0])
        outputs.update(pair_grads=((rows, HK * PAIR), bf16))
    else:
        outputs.update(own_grads=((rows, chunks * PAIR), f32))
    final = run(
        finish,
        z,
        inputs | numbered("pending", [early.grad, late.grad]),
        outputs,
        sems(BLOCKS),
        flops,
    )
    weight_share = final.share_out.astype(f32)
    for share in shares[1:]:
        weight_share += share.astype(f32)
    if merged:
        pair_grads = final.pair_grads
    else:
        own_grads = jnp.sum(final.own_grads.reshape(rows, HK, per_head, PAIR), axis=2)
        own_grads = own_grads.reshape(rows, HK * PAIR)
        for rows_back in backs:
            low = rows - rows_back.shape[0]
            own_grads = own_grads.at[low:].add(rows_back.astype(f32))
        pair_grads = own_grads.astype(bf16)

    return (
        final.dq[None, None],
        pair_grads[None, None],
        final.input_grad.T[None, None],
        weight_share[None],
    )


def solution(mesh):
    placed = (
        P("section", "dp", "seq", None),
        P("section", "dp", "seq", None),
        P("section", "dp", "seq", None),
        P("section", None, "seq"),
        P("section", "dp", "seq", None),
        P("section", "dp", None),
    )
    return jax.shard_map(
        per_device,
        mesh=mesh,
        in_specs=placed,
        out_specs=(
            P("section", "dp", "seq", None),
            P("section", "dp", "seq", None),
            P("section", "dp", "seq", None),
            P("section", "dp", "seq"),
        ),
        check_vma=False,
    )
```
